32 devices in a mesh: dp: 8 (over z, y), row: 2 (over core), col: 2 (over x).
Axes of the slice: x: 2, y: 2, z: 4, core: 2. Of those that a mesh axis runs over, the one named last changes fastest.
Arguments:
- block_input: bfloat16 [384, 32768], P(('row', 'col'), 'dp'), may hold values from -6 to 6
- condition: float32 [128, 384], P('dp', 'col'), may hold values from -6 to 6
- w_ada: bfloat16 [384, 2304], P('col', 'row'), may hold values from -0.3125 to 0.3125
- b_ada: bfloat16 [6, 384], P(None, ('row', 'col')), may hold values from -3 to 3
- w_qkv: bfloat16 [384, 1152], P('row', 'col'), may hold values from -0.3125 to 0.3125
- b_qkv: bfloat16 [2, 384], P(None, 'col'), may hold values from -3 to 3
- w_proj: bfloat16 [384, 384], P('col', 'row'), may hold values from -2.5 to 2.5
- b_proj: bfloat16 [384], P(('row', 'col')), may hold values from -3 to 3
- w_fc1: bfloat16 [384, 1536], P('row', 'col'), may hold values from -0.3125 to 0.3125
- b_fc1: bfloat16 [1536], P('col'), may hold values from -3 to 3
- w_fc2: bfloat16 [384, 1536], P('row', 'col'), may hold values from -0.15625 to 0.15625
- b_fc2: bfloat16 [384], P(('row', 'col')), may hold values from -3 to 3
- out_grad: bfloat16 [384, 32768], P(('row', 'col'), 'dp'), may hold values from -6 to 6
Outputs:
- block_output: float32 [384, 32768], P(('row', 'col'), 'dp')
- input_grad: float32 [384, 32768], P(('row', 'col'), 'dp')
- cond_grad: float32 [128, 384], P('dp', 'col')
- grad_w_ada: float32 [384, 2304], P('col', 'row')
- grad_b_ada: float32 [6, 384], P(None, ('row', 'col'))
- grad_w_qkv: float32 [384, 1152], P('row', 'col')
- grad_b_qkv: float32 [2, 384], P(None, 'col')
- grad_w_proj: float32 [384, 384], P('col', 'row')
- grad_b_proj: float32 [384], P(('row', 'col'))
- grad_w_fc1: float32 [384, 1536], P('row', 'col')
- grad_b_fc1: float32 [1536], P('col')
- grad_w_fc2: float32 [384, 1536], P('row', 'col')
- grad_b_fc2: float32 [384], P(('row', 'col'))
The draws below stay inside these ranges and needn't reach their ends.
All inputs are finite; a program needn't handle non-finite values.
Results may differ from the reference program's by a relative error of at most 0.012.
The reference program's roundings to bfloat16 on the way count: a program that leaves them out, or rounds other values in their place, can miss the bound.
Values may be sent and summed in bfloat16 or wider, within the bound.
No kernel may reach another device: no remote copies, remote signals or barrier semaphores. Data moves between devices by JAX's collectives and lax.ppermute only.
A program may use at most 128 MiB of HBM per device.

```python
import jax
import jax.numpy as jnp
from jax import lax

D = 384
HEADS = 6
HD = 64
FF = 1536
SEQ = 256
LAT_DEV = 16
LATENTS = 128
TOKENS = 32768
N_COL = 2


def shard_levels(stream_key, extent, cuts, smallest, largest):
    loudness, own = 1.0, jax.random.fold_in(stream_key, 6)
    for axis_at, parts in cuts:
        heights = jnp.exp(jax.random.uniform(jax.random.fold_in(own, axis_at), (parts,), jnp.float32, smallest / len(cuts), largest / len(cuts)))
        loudness = loudness * jnp.repeat(heights, extent[axis_at] // parts).reshape([-1 if axis == axis_at else 1 for axis in range(len(extent))])
    return loudness


def noise(own_key, shape, width, limit, split=(), kind=jnp.bfloat16):
    factor_of = shard_levels(own_key, shape, split, -0.22, 0.18) if split else 1.0
    drawn = jax.random.normal(own_key, shape, jnp.float32) * width * factor_of
    return jnp.minimum(jnp.maximum(drawn, -limit), limit).astype(kind)


def setup_inputs(seed: int = 0) -> dict:
    splits = jax.random.split(jax.random.key(seed), 14)
    return {
        "block_input": noise(splits[0], (D, TOKENS), 1.0, 6.0, ((0, 4), (1, 8))),
        "condition": noise(splits[1], (LATENTS, D), 1.0, 6.0, ((0, 8), (1, 2)), jnp.float32),
        "w_ada": noise(splits[2], (D, 6 * D), D ** -0.5, 0.3125, ((0, 2), (1, 2))),
        "b_ada": noise(splits[3], (6, D), 0.5, 3.0, ((1, 4),)),
        "w_qkv": noise(splits[4], (D, 3 * D), D ** -0.5, 0.3125, ((0, 2), (1, 2))),
        "b_qkv": noise(splits[5], (2, D), 0.5, 3.0, ((1, 2),)),
        "w_proj": noise(splits[6], (D, D), (D * 4 // SEQ) ** -0.5, 2.5, ((0, 2), (1, 2))),
        "b_proj": noise(splits[7], (D,), 0.5, 3.0, ((0, 4),)),
        "w_fc1": noise(splits[8], (D, FF), D ** -0.5, 0.3125, ((0, 2), (1, 2))),
        "b_fc1": noise(splits[9], (FF,), 0.5, 3.0, ((0, 2),)),
        "w_fc2": noise(splits[10], (D, FF), FF ** -0.5, 0.15625, ((0, 2), (1, 2))),
        "b_fc2": noise(splits[11], (D,), 0.5, 3.0, ((0, 4),)),
        "out_grad": noise(splits[12], (D, TOKENS), 1.0, 6.0, ((0, 4), (1, 8))),
    }


@jax.custom_vjp
def low(v):
    return lax.optimization_barrier(v.astype(jnp.bfloat16)).astype(jnp.float32)

@jax.custom_vjp
def low_back(v):
    return v

def low_keep(v):
    return (low(v), None)

def low_pass(kept, grad):
    return (grad,)

def back_keep(v):
    return (v, None)

def back_low(kept, grad):
    return (low(grad),)
low.defvjp(low_keep, low_pass)
low_back.defvjp(back_keep, back_low)
EPSILON = 1e-06
HIGHEST = lax.Precision.HIGHEST

def layer_norm(value):
    center = lax.optimization_barrier(jnp.mean(value, axis=-1, keepdims=True))
    spread = lax.optimization_barrier(jnp.mean(value * value, axis=-1, keepdims=True)) - center * center
    return (value - center) * lax.rsqrt(spread + EPSILON)

def attend_block(operands):
    query, keys, values = operands
    scores = low_back(jnp.einsum('lqhe,lkhe->lhqk', query, keys, precision=HIGHEST) * HD ** (-0.5))
    probs = jax.nn.softmax(scores, axis=-1)
    return jnp.einsum('lhqk,lkhe->lqhe', low(probs), values, precision=HIGHEST)

def forward(block_input, condition, w_ada, b_ada, w_qkv, b_qkv, w_proj, b_proj, w_fc1, b_fc1, w_fc2, b_fc2):
    latents = condition.shape[0]
    groups = N_COL
    per_group = HEADS // N_COL
    cond_low = low(jax.nn.silu(condition))
    ada_table = w_ada.reshape(D, D, 6)
    modulation = low_back(jnp.einsum('li,idm->lmd', cond_low, ada_table, precision=HIGHEST) + b_ada[None])
    pieces = [modulation[:, index][:, None, :] for index in range(6)]
    shift_one, scale_one, gate_one, shift_two, scale_two, gate_two = pieces
    inputs = block_input.T.reshape(latents, SEQ, D)
    mod_one = low(layer_norm(inputs) * (1.0 + scale_one) + shift_one)
    qkv = jnp.einsum('lsi,ij->lsj', mod_one, w_qkv, precision=HIGHEST).reshape(latents, SEQ, groups, 3, per_group, HD)
    bias = b_qkv.reshape(2, groups, per_group, HD)
    query = low(low_back((qkv[:, :, :, 0] + bias[0]).reshape(latents, SEQ, HEADS, HD)))
    keys = low(low_back(qkv[:, :, :, 1].reshape(latents, SEQ, HEADS, HD)))
    values = low(low_back((qkv[:, :, :, 2] + bias[1]).reshape(latents, SEQ, HEADS, HD)))
    block_count = latents // LAT_DEV
    shaped = [item.reshape(block_count, LAT_DEV, SEQ, HEADS, HD) for item in (query, keys, values)]
    attended = lax.map(jax.checkpoint(attend_block), tuple(shaped))
    attended = low(low_back(attended.reshape(latents, SEQ, D)))
    attn_branch = low_back(jnp.einsum('lsi,ij->lsj', attended, w_proj, precision=HIGHEST) + b_proj)
    hidden_state = inputs + gate_one * attn_branch
    mod_two = low(layer_norm(hidden_state) * (1.0 + scale_two) + shift_two)
    pre_act = low_back(jnp.einsum('lsi,ij->lsj', mod_two, w_fc1, precision=HIGHEST) + b_fc1)
    act_low = low(jax.nn.gelu(pre_act, approximate=True))
    mlp_branch = low_back(jnp.einsum('lsj,ij->lsi', act_low, w_fc2, precision=HIGHEST) + b_fc2)
    block_output = hidden_state + gate_two * mlp_branch
    return block_output.reshape(latents * SEQ, D).T

def reference(block_input, condition, w_ada, b_ada, w_qkv, b_qkv, w_proj, b_proj, w_fc1, b_fc1, w_fc2, b_fc2, out_grad):
    primals = [item.astype(jnp.float32) for item in (block_input, condition, w_ada, b_ada, w_qkv, b_qkv, w_proj, b_proj, w_fc1, b_fc1, w_fc2, b_fc2)]
    block_output, pullback = jax.vjp(forward, *primals)
    grads = pullback(out_grad.astype(jnp.float32))
    return (block_output, grads[0], grads[1], grads[2], grads[3], grads[4], grads[5], grads[6], grads[7], grads[8], grads[9], grads[10], grads[11])
```

```python
import jax
import jax.numpy as jnp
from jax import lax
from jax.experimental import pallas as pl
from jax.experimental.pallas import tpu as pltpu
from jax.sharding import PartitionSpec as P

D = 384
HEADS = 6
HD = 64
FF = 1536
GROUPS = 2
EPSILON = 1e-06
BF16 = jnp.bfloat16
F32 = jnp.float32
GROUP = ("row", "col")
VMEM_BYTES = 56 * 1024 * 1024


def dot_nn(left, right):
    return lax.dot_general(left, right, (((1,), (0,)), ((), ())), preferred_element_type=F32)


def dot_nt(left, right):
    return lax.dot_general(left, right, (((1,), (1,)), ((), ())), preferred_element_type=F32)


def dot_tn(left, right):
    return lax.dot_general(left, right, (((0,), (0,)), ((), ())), preferred_element_type=F32)


def lane_sum(value):
    return jnp.sum(value, axis=1, keepdims=True)


def lane_fold(value):
    parts = [value[:, at : at + 128] for at in range(0, value.shape[1], 128)]
    return sum(parts[1:], parts[0])


def norm_stats(value):
    center = jnp.sum(value, axis=0, keepdims=True) * (1.0 / D)
    square = jnp.sum(value * value, axis=0, keepdims=True) * (1.0 / D)
    inverse = lax.rsqrt(square - center * center + EPSILON)
    return (value - center) * inverse, inverse


def norm_back(grad, normed, inverse):
    first = jnp.sum(grad, axis=0, keepdims=True) * (1.0 / D)
    second = jnp.sum(grad * normed, axis=0, keepdims=True) * (1.0 / D)
    return inverse * (grad - first - normed * second)


PIECES = ((0, 0), (0, 1), (1, 0), (1, 1))


def place_split(pieces, target, pos):
    row, col = pos[0], pos[1]
    for piece, (step_row, step_col) in zip(pieces, PIECES):
        height = piece.shape[0]
        at = pl.multiple_of((row ^ step_row) * height, height)
        target[col ^ step_col, pl.ds(at, height), :] = piece[...]


def place_proj(pieces, target, pos):
    row, col = pos[0], pos[1]
    for piece, (step_row, step_col) in zip(pieces, PIECES):
        height = piece.shape[0]
        at = pl.multiple_of((col ^ step_col) * height, height)
        target[row ^ step_row, pl.ds(at, height), :] = piece[...]


def place_features(pieces, target, pos):
    own = pos[0] * 2 + pos[1]
    for step, piece in enumerate(pieces):
        height = piece.shape[0]
        at = pl.multiple_of((own ^ step) * height, height)
        target[pl.ds(at, height), :] = piece[...].astype(target.dtype)


def split_features(source, pieces, pos):
    own = pos[0] * 2 + pos[1]
    for step, piece in enumerate(pieces):
        height = piece.shape[0]
        at = pl.multiple_of((own ^ step) * height, height)
        piece[...] = source[pl.ds(at, height), :].astype(piece.dtype)


def attention_forward(
    pos, x0, x1, x2, x3, mod, wq0, wq1, wq2, wq3, wp0, wp1, wp2, wp3, bias_q, bias_v, bias_p,
    x_out, mod_one_out, qkv_out, probs_out, attended_out, branch_out,
    x_s, wq_s, wq_t, wp_s, wp_t,
):
    @pl.when(pl.program_id(0) == 0)
    def _():
        place_split((wq0, wq1, wq2, wq3), wq_s, pos)
        place_proj((wp0, wp1, wp2, wp3), wp_s, pos)
        for part in range(GROUPS):
            wq_t[part] = wq_s[part].T
            wp_t[part] = wp_s[part].T

    place_features((x0, x1, x2, x3), x_s, pos)
    x = x_s[...]
    x_out[...] = x.astype(BF16)
    normed, _ = norm_stats(x)
    mod_one = (normed * (1.0 + mod[0, :, 1:2]) + mod[0, :, 0:1]).astype(BF16)
    mod_one_out[...] = mod_one
    third = D // GROUPS
    for part in range(GROUPS):
        qkv = dot_nn(wq_t[part], mod_one)
        base = part * third
        query = (qkv[:third] + bias_q[base : base + third]).astype(BF16)
        keys = qkv[third : 2 * third].astype(BF16)
        values = (qkv[2 * third :] + bias_v[base : base + third]).astype(BF16)
        qkv_out[part, :third] = query
        qkv_out[part, third : 2 * third] = keys
        qkv_out[part, 2 * third :] = values
        scaled = query * jnp.asarray(HD ** (-0.5), BF16)
        for head in range(HEADS // GROUPS):
            rows = slice(head * HD, (head + 1) * HD)
            scores = dot_tn(keys[rows], scaled[rows])
            top = jnp.max(scores, axis=0, keepdims=True)
            raised = jnp.exp(scores - top)
            total = jnp.sum(raised, axis=0, keepdims=True)
            probs = (raised * (1.0 / total)).astype(BF16)
            probs_out[0, part * (HEADS // GROUPS) + head] = probs
            attended_out[base + head * HD : base + (head + 1) * HD] = dot_nn(
                values[rows], probs
            ).astype(BF16)
    attended = attended_out[...]
    for part in range(2):
        rows = slice(part * third, (part + 1) * third)
        branch_out[rows] = dot_nn(wp_t[part], attended) + bias_p[rows]


def mlp_forward(
    pos, x, branch, mod, w10, w11, w12, w13, w20, w21, w22, w23, bias_1, bias_2,
    out0, out1, out2, out3, mod_two_out, act_out, slope_out, mlp_out,
    w1_s, w1_t, w2_s, block_s,
):
    @pl.when(pl.program_id(0) == 0)
    def _():
        place_split((w10, w11, w12, w13), w1_s, pos)
        place_split((w20, w21, w22, w23), w2_s, pos)
        for part in range(GROUPS):
            w1_t[part] = w1_s[part].T

    hidden = x[...].astype(F32) + mod[0, :, 2:3] * branch[...]
    normed, _ = norm_stats(hidden)
    mod_two = (normed * (1.0 + mod[0, :, 4:5]) + mod[0, :, 3:4]).astype(BF16)
    mod_two_out[...] = mod_two
    half = FF // GROUPS
    slope = (2.0 / jnp.pi) ** 0.5
    total = None
    for part in range(GROUPS):
        rows = slice(part * half, (part + 1) * half)
        pre = dot_nn(w1_t[part], mod_two) + bias_1[rows]
        square = pre * pre
        tanh = jnp.tanh(slope * pre * (1.0 + 0.044715 * square))
        upper = 0.5 + 0.5 * tanh
        act = (pre * upper).astype(BF16)
        act_out[rows] = act
        slope_out[rows] = (
            upper
            + (0.5 * slope) * pre * (1.0 - tanh * tanh) * (1.0 + (3 * 0.044715) * square)
        ).astype(BF16)
        partial = dot_nn(w2_s[part], act)
        total = partial if total is None else total + partial
    mlp = total + bias_2[...]
    mlp_out[...] = mlp
    block_s[...] = hidden + mod[0, :, 5:6] * mlp
    split_features(block_s, (out0, out1, out2, out3), pos)


def mlp_backward(
    pos, g0, g1, g2, g3, x, branch, mod, mod_two, act, slope, mlp, attended,
    w10, w11, w12, w13, w20, w21, w22, w23, wp0, wp1, wp2, wp3,
    hidden_grad_out, context_out, mod_grad_out, send_out, keep_out, sum1_out, sum2_out, sump_out,
    g_s, w1_s, w2_s, w2_t, wp_s, acc1, acc2, accp, sum1, sum2, sump,
):
    step = pl.program_id(0)

    @pl.when(step == 0)
    def _():
        place_split((w10, w11, w12, w13), w1_s, pos)
        place_split((w20, w21, w22, w23), w2_s, pos)
        place_proj((wp0, wp1, wp2, wp3), wp_s, pos)
        for part in range(GROUPS):
            w2_t[part] = w2_s[part].T
        for acc in (acc1, acc2, accp, sum1, sum2, sump):
            acc[...] = jnp.zeros_like(acc)

    place_features((g0, g1, g2, g3), g_s, pos)
    grad = g_s[...]
    gate_one = mod[0, :, 2:3]
    gate_two = mod[0, :, 5:6]
    hidden = x[...].astype(F32) + gate_one * branch[...]
    normed, inverse = norm_stats(hidden)
    mod_grad_out[0, :, 3:4] = lane_sum(grad * mlp[...])
    mlp_grad = (gate_two * grad).astype(BF16)
    sum2[...] += lane_fold(mlp_grad.astype(F32))
    half = FF // GROUPS
    third = D // GROUPS
    mod_two_low = mod_two[...]
    back = None
    for part in range(GROUPS):
        rows = slice(part * half, (part + 1) * half)
        acc2[part] += dot_nt(mlp_grad, act[rows])
        pre_grad = (dot_nn(w2_t[part], mlp_grad) * slope[rows].astype(F32)).astype(BF16)
        sum1[rows] += lane_fold(pre_grad.astype(F32))
        acc1[part] += dot_nt(mod_two_low, pre_grad)
        partial = dot_nn(w1_s[part], pre_grad)
        back = partial if back is None else back + partial
    mod_grad_out[0, :, 1:2] = lane_sum(back)
    mod_grad_out[0, :, 2:3] = lane_sum(back * normed)
    hidden_grad = grad + norm_back(back * (1.0 + mod[0, :, 4:5]), normed, inverse)
    hidden_grad_out[...] = hidden_grad
    mod_grad_out[0, :, 0:1] = lane_sum(hidden_grad * branch[...])
    branch_grad = (gate_one * hidden_grad).astype(BF16)
    sump[...] += lane_fold(branch_grad.astype(F32))
    context = None
    for part in range(2):
        rows = slice(part * third, (part + 1) * third)
        accp[part] += dot_nt(attended[...], branch_grad[rows])
        partial = dot_nn(wp_s[part], branch_grad[rows])
        context = partial if context is None else context + partial
    context_out[...] = context.astype(BF16)

    @pl.when(step == pl.num_programs(0) - 1)
    def _():
        mine = pl.multiple_of(pos[0] * third, third)
        other = pl.multiple_of((1 - pos[0]) * third, third)
        for part in range(GROUPS):
            rows = slice(part * third, (part + 1) * third)
            for out, at, who in ((send_out, other, 1 - pos[0]), (keep_out, mine, pos[0])):
                out[part, :, :half] = acc1[part, pl.ds(at, third), :].astype(out.dtype)
                out[part, :, half : 2 * half] = acc2[part, pl.ds(at, third), :].astype(out.dtype)
                out[part, :, 2 * half :] = accp[who, rows, :].astype(out.dtype)
        sum1_out[...] = lane_sum(sum1[...])
        sum2_out[...] = lane_sum(sum2[...])
        sump_out[...] = lane_sum(sump[...])


def attention_backward(
    pos, x, mod_one, mod, qkv, probs, context, hidden_grad, wq0, wq1, wq2, wq3,
    out0, out1, out2, out3, mod_grad_out, send_out, keep_out, sumq_out, sumv_out,
    wq_s, acc, sumq, sumv, grad_s, block_s,
):
    step = pl.program_id(0)

    @pl.when(step == 0)
    def _():
        place_split((wq0, wq1, wq2, wq3), wq_s, pos)
        for item in (acc, sumq, sumv):
            item[...] = jnp.zeros_like(item)

    third = D // GROUPS
    scale = HD ** (-0.5)
    mod_one_low = mod_one[...]
    back = None
    for part in range(GROUPS):
        base = part * third
        for head in range(HEADS // GROUPS):
            at = head * HD
            query = qkv[part, at : at + HD]
            keys = qkv[part, third + at : third + at + HD]
            values = qkv[part, 2 * third + at : 2 * third + at + HD]
            out_grad = context[base + at : base + at + HD]
            weight = probs[0, part * (HEADS // GROUPS) + head]
            prob_grad = dot_tn(values, out_grad)
            values_grad = dot_nt(out_grad, weight)
            wide = weight.astype(F32)
            product = wide * prob_grad
            row_dot = jnp.sum(product, axis=0, keepdims=True)
            score_grad = (product - wide * row_dot).astype(BF16)
            query_grad = dot_nn(keys, score_grad) * scale
            keys_grad = dot_nt(query, score_grad) * scale
            grad_s[at : at + HD] = query_grad.astype(BF16)
            grad_s[third + at : third + at + HD] = keys_grad.astype(BF16)
            grad_s[2 * third + at : 2 * third + at + HD] = values_grad.astype(BF16)
        qkv_grad = grad_s[...]
        sumq[base : base + third] += lane_fold(qkv_grad[:third].astype(F32))
        sumv[base : base + third] += lane_fold(qkv_grad[2 * third :].astype(F32))
        acc[part] += dot_nt(mod_one_low, qkv_grad)
        partial = dot_nn(wq_s[part], qkv_grad)
        back = partial if back is None else back + partial
    normed, inverse = norm_stats(x[...].astype(F32))
    mod_grad_out[0, :, 0:1] = lane_sum(back)
    mod_grad_out[0, :, 1:2] = lane_sum(back * normed)
    block_s[...] = hidden_grad[...] + norm_back(back * (1.0 + mod[0, :, 1:2]), normed, inverse)
    split_features(block_s, (out0, out1, out2, out3), pos)

    @pl.when(step == pl.num_programs(0) - 1)
    def _():
        mine = pl.multiple_of(pos[0] * third, third)
        other = pl.multiple_of((1 - pos[0]) * third, third)
        for part in range(GROUPS):
            send_out[part] = acc[part, pl.ds(other, third), :].astype(send_out.dtype)
            keep_out[part] = acc[part, pl.ds(mine, third), :].astype(keep_out.dtype)
        sumq_out[...] = lane_sum(sumq[...])
        sumv_out[...] = lane_sum(sumv[...])


def call(kernel, pos, steps, seq, inputs, outputs, scratch, flops, name):
    def spec(kind, shape):
        rank = len(shape)
        if kind == "t":
            lead = (0,) * (rank - 1)
            return pl.BlockSpec(shape[:-1] + (seq,), lambda i, p: lead + (i,))
        if kind == "l":
            tail = (0,) * (rank - 1)
            return pl.BlockSpec((1,) + shape[1:], lambda i, p: (i,) + tail)
        zeros = (0,) * rank
        return pl.BlockSpec(shape, lambda i, p: zeros)

    size = sum(a.size * a.dtype.itemsize for _, a in inputs)
    size += sum(a.size * jnp.dtype(a.dtype).itemsize for _, a in outputs)
    return pl.pallas_call(
        kernel,
        grid_spec=pltpu.PrefetchScalarGridSpec(
            num_scalar_prefetch=1,
            grid=(steps,),
            in_specs=[spec(kind, a.shape) for kind, a in inputs],
            out_specs=[spec(kind, a.shape) for kind, a in outputs],
            scratch_shapes=scratch,
        ),
        out_shape=[a for _, a in outputs],
        compiler_params=pltpu.CompilerParams(
            dimension_semantics=("arbitrary",), vmem_limit_bytes=VMEM_BYTES
        ),
        cost_estimate=pl.CostEstimate(flops=flops, bytes_accessed=size, transcendentals=0),
        name=name,
    )(pos, *[a for _, a in inputs])


def swap(value, axis):
    return lax.ppermute(value, axis, [(0, 1), (1, 0)])


def group_step(value, step):
    return lax.ppermute(value, GROUP, [(at, at ^ step) for at in range(4)])


def gather_pieces(block):
    beside = swap(block, "col")
    return (block, beside, swap(block, "row"), swap(beside, "row"))


def spread_tokens(value, own):
    width = value.shape[1] // 4
    pieces = []
    for step in range(4):
        piece = lax.dynamic_slice_in_dim(value, (own ^ step) * width, width, 1)
        pieces.append(group_step(piece, step) if step else piece)
    return pieces


def collect_tokens(pieces, own):
    width = pieces[0].shape[1]
    moved = [group_step(piece, step) if step else piece for step, piece in enumerate(pieces)]
    out = jnp.zeros((pieces[0].shape[0], 4 * width), F32)
    for step, piece in enumerate(moved):
        out = lax.dynamic_update_slice_in_dim(out, piece.astype(F32), (own ^ step) * width, 1)
    return out


def in_order(own_first, other, index, axis):
    first = jnp.where(index == 0, own_first, other)
    second = jnp.where(index == 0, other, own_first)
    return jnp.stack([first, second], axis=axis)


def gather_dp(value):
    count = lax.axis_size("dp")
    return lax.all_to_all(jnp.broadcast_to(value[None], (count,) + value.shape), "dp", 0, 0)


def reduce_dp(value):
    count = lax.axis_size("dp")
    rows, columns = value.shape
    parts = lax.all_to_all(value.astype(BF16).reshape(count, rows // count, columns), "dp", 0, 0)
    total = jnp.sum(parts.astype(F32), axis=0)
    return gather_dp(total.astype(BF16)).reshape(rows, columns).astype(F32)


def reduce_grads(send, keep, col):
    half = keep + swap(send, "row").astype(F32)
    mine = lax.dynamic_index_in_dim(half, col, 0, keepdims=False)
    theirs = lax.dynamic_index_in_dim(half, 1 - col, 0, keepdims=False)
    return reduce_dp(mine + swap(theirs.astype(BF16), "col").astype(F32))


def local(
    block_input, condition, w_ada, b_ada, w_qkv, b_qkv, w_proj, b_proj, w_fc1, b_fc1, w_fc2,
    b_fc2, out_grad,
):
    row = lax.axis_index("row")
    col = lax.axis_index("col")
    own = row * 2 + col
    pos = jnp.stack([row, col]).astype(jnp.int32)
    latents = condition.shape[0]
    tokens = block_input.shape[1]
    seq = tokens // latents
    steps = latents // 4
    width = tokens // 4
    third = D // GROUPS
    half = FF // GROUPS

    def shape(dims, kind):
        return jax.ShapeDtypeStruct(dims, kind)

    x_pieces = spread_tokens(block_input, own)

    silu, silu_back = jax.vjp(jax.nn.silu, condition)
    cond_low = silu.astype(BF16)
    ada = jnp.dot(cond_low, w_ada, preferred_element_type=F32).reshape(latents, third, 6)
    bias_ada = lax.dynamic_update_slice_in_dim(
        jnp.zeros((third, 6), F32), b_ada.astype(F32).T, col * (third // 2), 0
    )
    ada = (ada + bias_ada[None]).reshape(2, 2, steps, third * 6)
    mine = lax.dynamic_index_in_dim(ada, col, 1, keepdims=False)
    theirs = lax.dynamic_index_in_dim(ada, 1 - col, 1, keepdims=False)
    ada = mine + swap(theirs, "col")
    mine = lax.dynamic_index_in_dim(ada, row, 0, keepdims=False)
    theirs = lax.dynamic_index_in_dim(ada, 1 - row, 0, keepdims=False)
    mod = in_order(mine, swap(theirs, "row"), row, 1).reshape(steps, D, 6)

    packed = jnp.concatenate([b_qkv[0], b_qkv[1], b_proj, b_fc1, b_fc2])
    packed = in_order(packed, swap(packed, "col"), col, 0)
    packed = in_order(packed, swap(packed, "row"), row, 0).astype(F32)
    bias_q = packed[0, :, :third].reshape(D, 1)
    bias_v = packed[0, :, third : 2 * third].reshape(D, 1)
    quarter = D // 4
    at = 2 * third
    bias_p = packed[:, :, at : at + quarter].reshape(D, 1)
    bias_1 = packed[0, :, at + quarter : at + quarter + half].reshape(FF, 1)
    bias_2 = packed[:, :, at + quarter + half :].reshape(D, 1)

    wq = gather_pieces(w_qkv)
    wp = gather_pieces(w_proj)

    t_low = shape((D, width), BF16)
    t_wide = shape((D, width), F32)
    t_ff = shape((FF, width), BF16)
    t_piece = shape((quarter, width), BF16)
    per_matmul = 2 * width * D

    x, mod_one, qkv, probs, attended, branch = call(
        attention_forward, pos, steps, seq,
        [("t", a) for a in x_pieces] + [("l", mod)] + [("w", a) for a in wq + wp]
        + [("w", bias_q), ("w", bias_v), ("w", bias_p)],
        [("t", t_low), ("t", t_low), ("t", shape((2, 3 * third, width), BF16)),
         ("l", shape((steps, HEADS, seq, seq), BF16)), ("t", t_low), ("t", t_wide)],
        [pltpu.VMEM((D, seq), F32), pltpu.VMEM((2, D, 3 * third), BF16),
         pltpu.VMEM((2, 3 * third, D), BF16), pltpu.VMEM((2, D, third), BF16),
         pltpu.VMEM((2, third, D), BF16)],
        per_matmul * (4 * D + 8 * seq), "attention_forward",
    )

    w_fc1, w_fc2, _ = lax.optimization_barrier((w_fc1, w_fc2, x_pieces))
    w1 = gather_pieces(w_fc1)
    w2 = gather_pieces(w_fc2)

    out0, out1, out2, out3, mod_two, act, slope, mlp = call(
        mlp_forward, pos, steps, seq,
        [("t", x), ("t", branch), ("l", mod)] + [("w", a) for a in w1 + w2]
        + [("w", bias_1), ("w", bias_2)],
        [("t", t_piece)] * 4 + [("t", t_low), ("t", t_ff), ("t", t_ff), ("t", t_wide)],
        [pltpu.VMEM((2, D, half), BF16), pltpu.VMEM((2, half, D), BF16),
         pltpu.VMEM((2, D, half), BF16), pltpu.VMEM((D, seq), F32)],
        per_matmul * 2 * FF, "mlp_forward",
    )
    block_output = collect_tokens((out0, out1, out2, out3), own)

    out_grad, _ = lax.optimization_barrier((out_grad, w1[1]))
    g_pieces = spread_tokens(out_grad, own)
    fc_block = (2, third, 2 * half + third)
    hidden_grad, context, mod_grad_two, send_fc, keep_fc, sum1, sum2, sump = call(
        mlp_backward, pos, steps, seq,
        [("t", a) for a in g_pieces]
        + [("t", x), ("t", branch), ("l", mod), ("t", mod_two), ("t", act), ("t", slope),
           ("t", mlp), ("t", attended)]
        + [("w", a) for a in w1 + w2 + wp],
        [("t", t_wide), ("t", t_low), ("l", shape((steps, D, 4), F32)),
         ("w", shape(fc_block, BF16)), ("w", shape(fc_block, F32)),
         ("w", shape((FF, 1), F32)), ("w", shape((D, 1), F32)), ("w", shape((D, 1), F32))],
        [pltpu.VMEM((D, seq), F32), pltpu.VMEM((2, D, half), BF16), pltpu.VMEM((2, D, half), BF16),
         pltpu.VMEM((2, half, D), BF16), pltpu.VMEM((2, D, third), BF16),
         pltpu.VMEM((2, D, half), F32), pltpu.VMEM((2, D, half), F32),
         pltpu.VMEM((2, D, third), F32), pltpu.VMEM((FF, 128), F32),
         pltpu.VMEM((D, 128), F32), pltpu.VMEM((D, 128), F32)],
        per_matmul * (4 * FF + 2 * D), "mlp_backward",
    )
    grads_fc = reduce_grads(send_fc, keep_fc, col)

    in0, in1, in2, in3, mod_grad_one, send_qkv, keep_qkv, sumq, sumv = call(
        attention_backward, pos, steps, seq,
        [("t", x), ("t", mod_one), ("l", mod), ("t", qkv), ("l", probs), ("t", context),
         ("t", hidden_grad)] + [("w", a) for a in wq],
        [("t", t_piece)] * 4
        + [("l", shape((steps, D, 2), F32)), ("w", shape((2, third, 3 * third), BF16)),
           ("w", shape((2, third, 3 * third), F32)),
           ("w", shape((D, 1), F32)), ("w", shape((D, 1), F32))],
        [pltpu.VMEM((2, D, 3 * third), BF16), pltpu.VMEM((2, D, 3 * third), F32),
         pltpu.VMEM((D, 128), F32), pltpu.VMEM((D, 128), F32),
         pltpu.VMEM((3 * third, seq), BF16), pltpu.VMEM((D, seq), F32)],
        per_matmul * (6 * D + 16 * seq), "attention_backward",
    )
    input_grad = collect_tokens((in0, in1, in2, in3), own)
    grads_qkv = reduce_grads(send_qkv, keep_qkv, col)

    span = third * 6
    mod_grad = jnp.concatenate([mod_grad_one, mod_grad_two], axis=2).astype(BF16).astype(F32)
    halves = mod_grad.reshape(steps, 2, span)
    mine = lax.dynamic_index_in_dim(halves, row, 1, keepdims=False)
    theirs = lax.dynamic_index_in_dim(halves, 1 - row, 1, keepdims=False)
    sums = jnp.concatenate([sumq, sumv, sump, sum1, sum2])[:, 0]
    sums = jnp.pad(sums, (0, 3 * span - sums.shape[0])).reshape(3, span)
    moved = swap(jnp.concatenate([theirs, sums]), "row")
    sums = sums + moved[steps:]
    pair = in_order(mine, moved[:steps], row, 0)
    moved = swap(jnp.concatenate([pair.reshape(2 * steps, span), sums]), "col")
    sums = (sums + moved[2 * steps :]).reshape(-1)
    pairs = in_order(pair, moved[: 2 * steps].reshape(pair.shape), col, 1)
    mod_here = pairs.reshape(latents, span).astype(BF16)

    def part_of(start, size, index):
        return lax.dynamic_slice_in_dim(sums, start + index * size, size)

    mine = jnp.concatenate(
        [part_of(0, third, col), part_of(D, third, col), part_of(2 * D, quarter, own),
         part_of(3 * D, half, col), part_of(3 * D + FF, quarter, own)]
    )
    mine = jnp.pad(mine, (0, 2 * span - mine.shape[0])).reshape(2, span)
    everyone = gather_dp(jnp.concatenate([mod_here, mine.astype(BF16)]))
    cond_all = gather_dp(cond_low).reshape(-1, cond_low.shape[1])
    mod_all = everyone[:, :latents].reshape(-1, span)
    grad_w_ada = dot_tn(cond_all, mod_all)
    grad_b_ada = jnp.sum(mod_all.astype(F32), axis=0).reshape(third, 6)
    grad_b_ada = lax.dynamic_slice_in_dim(grad_b_ada, col * quarter, quarter, 0).T
    totals = jnp.sum(everyone[:, latents:].astype(F32), axis=0).reshape(-1)
    cond_part = dot_nt(mod_here, w_ada)
    cond_grad = silu_back(cond_part + swap(cond_part, "row"))[0]

    at = 2 * third
    return (
        block_output,
        input_grad,
        cond_grad,
        grad_w_ada,
        grad_b_ada,
        grads_qkv,
        totals[:at].reshape(2, third),
        grads_fc[:, 2 * half :],
        totals[at : at + quarter],
        grads_fc[:, :half],
        totals[at + quarter : at + quarter + half],
        grads_fc[:, half : 2 * half],
        totals[at + quarter + half : at + 2 * quarter + half],
    )


def solution(mesh):
    return jax.shard_map(
        local,
        mesh=mesh,
        in_specs=(
            P(("row", "col"), "dp"),
            P("dp", "col"),
            P("col", "row"),
            P(None, ("row", "col")),
            P("row", "col"),
            P(None, "col"),
            P("col", "row"),
            P(("row", "col")),
            P("row", "col"),
            P("col"),
            P("row", "col"),
            P(("row", "col")),
            P(("row", "col"), "dp"),
        ),
        out_specs=(
            P(("row", "col"), "dp"),
            P(("row", "col"), "dp"),
            P("dp", "col"),
            P("col", "row"),
            P(None, ("row", "col")),
            P("row", "col"),
            P(None, "col"),
            P("col", "row"),
            P(("row", "col")),
            P("row", "col"),
            P("col"),
            P("row", "col"),
            P(("row", "col")),
        ),
        check_vma=False,
    )
```

```python
import jax
import jax.numpy as jnp
from jax import lax
from jax.experimental import pallas as pl
from jax.experimental.pallas import tpu as pltpu
from jax.sharding import PartitionSpec as P

D = 384
HEADS = 6
HD = 64
FF = 1536
GROUPS = 2
EPSILON = 1e-06
BF16 = jnp.bfloat16
F32 = jnp.float32
GROUP = ("row", "col")
VMEM_BYTES = 56 * 1024 * 1024


def dot_nn(left, right):
    return lax.dot_general(left, right, (((1,), (0,)), ((), ())), preferred_element_type=F32)


def dot_nt(left, right):
    return lax.dot_general(left, right, (((1,), (1,)), ((), ())), preferred_element_type=F32)


def dot_tn(left, right):
    return lax.dot_general(left, right, (((0,), (0,)), ((), ())), preferred_element_type=F32)


def lane_sum(value):
    return jnp.sum(value, axis=1, keepdims=True)


def lane_fold(value):
    parts = [value[:, at : at + 128] for at in range(0, value.shape[1], 128)]
    return sum(parts[1:], parts[0])


def norm_stats(value):
    center = jnp.sum(value, axis=0, keepdims=True) * (1.0 / D)
    square = jnp.sum(value * value, axis=0, keepdims=True) * (1.0 / D)
    inverse = lax.rsqrt(square - center * center + EPSILON)
    return (value - center) * inverse, inverse


def norm_back(grad, normed, inverse):
    first = jnp.sum(grad, axis=0, keepdims=True) * (1.0 / D)
    second = jnp.sum(grad * normed, axis=0, keepdims=True) * (1.0 / D)
    return inverse * (grad - first - normed * second)


PIECES = ((0, 0), (0, 1), (1, 0), (1, 1))


def place_split(pieces, target, pos):
    row, col = pos[0], pos[1]
    for piece, (step_row, step_col) in zip(pieces, PIECES):
        height = piece.shape[0]
        at = pl.multiple_of((row ^ step_row) * height, height)
        target[col ^ step_col, pl.ds(at, height), :] = piece[...]


def place_proj(pieces, target, pos):
    row, col = pos[0], pos[1]
    for piece, (step_row, step_col) in zip(pieces, PIECES):
        height = piece.shape[0]
        at = pl.multiple_of((col ^ step_col) * height, height)
        target[row ^ step_row, pl.ds(at, height), :] = piece[...]


BIAS_ROWS = 8


def bias_columns(packs, pos, query_s, value_s, proj_s, last_s):
    own, col = pos[0] * 2 + pos[1], pos[1]
    third = D // GROUPS
    quarter = D // 4
    for step, pack in enumerate(packs):
        columns = pack[pack.shape[0] - BIAS_ROWS :, :].T
        if step < 2 and query_s is not None:
            at = pl.multiple_of((col ^ step) * third, third)
            query_s[pl.ds(at, third), :] = columns[:, 0:1]
            value_s[pl.ds(at, third), :] = columns[:, 1:2]
        at = pl.multiple_of((own ^ step) * quarter, quarter)
        if proj_s is not None:
            proj_s[pl.ds(at, quarter), :] = columns[:quarter, 2:3]
        if last_s is not None:
            last_s[pl.ds(at, quarter), :] = columns[:quarter, 3:4]


def cut_tokens(pos, x, out1, out2, out3):
    own = pos[0] * 2 + pos[1]
    width = out1.shape[1]
    for step, out in ((1, out1), (2, out2), (3, out3)):
        at = pl.multiple_of((own ^ step) * width, width)
        out[...] = x[:, pl.ds(at, width)]


def piece_order(latents, steps, own):
    here = lax.broadcasted_iota(jnp.int32, (latents, latents), 0)
    there = lax.broadcasted_iota(jnp.int32, (latents, latents), 1)
    return (there == (own ^ (here // steps)) * steps + here % steps).astype(BF16)


def modulation_parts(
    pos, condition, w_ada, b_ada, b_qkv, b_proj, b_fc2,
    pack0, pack1, pack2, pack3, cond_out, w_ada_out,
):
    own, col = pos[0] * 2 + pos[1], pos[1]
    latents = condition.shape[0]
    steps = latents // 4
    third = D // GROUPS
    quarter = D // 4
    value = condition[...]
    cond_low = (value * jax.nn.sigmoid(value)).astype(BF16)
    cond_out[...] = cond_low
    ordered = dot_nn(piece_order(latents, steps, own), cond_low).astype(BF16)
    zeros = jnp.zeros((6, quarter), F32)
    bias = b_ada[...].astype(F32)
    bias = jnp.where(
        col == 0, jnp.concatenate([bias, zeros], 1), jnp.concatenate([zeros, bias], 1)
    )
    rows = lax.broadcasted_iota(jnp.int32, (third * 6, third), 0)
    columns = lax.broadcasted_iota(jnp.int32, (third * 6, third), 1)
    packs = (pack0, pack1, pack2, pack3)
    for vector in range(6):
        select = (rows == columns * 6 + vector).astype(BF16)
        weight = dot_nn(w_ada[...], select).astype(BF16)
        w_ada_out[vector] = weight
        part = dot_nn(ordered, weight) + bias[vector : vector + 1]
        for step in range(4):
            for at in range(steps):
                packs[step][at * 8 + vector : at * 8 + vector + 1, :] = part[
                    step * steps + at : step * steps + at + 1
                ]
    for pack in packs:
        at = steps * 8
        pack[at : at + 2, :] = b_qkv[...].astype(F32)
        pack[at + 2 : at + 8, :] = jnp.zeros((6, third), F32)
        pack[at + 2 : at + 3, :quarter] = b_proj[...].astype(F32)
        pack[at + 3 : at + 4, :quarter] = b_fc2[...].astype(F32)
        for latent in range(steps):
            pack[latent * 8 + 6 : latent * 8 + 8, :] = jnp.zeros((2, third), F32)


def join_tokens(pos, x0, x1, x2, x3, out):
    for step, piece in enumerate((x0, x1, x2, x3)):

        @pl.when(pl.program_id(0) == step)
        def _():
            out[...] = piece[...].astype(out.dtype)


def group_vectors(pos, pack0, pack1, pack2, pack3, cond, w_ada, everyone, cond_part):
    own = pos[0] * 2 + pos[1]
    packs = (pack0, pack1, pack2, pack3)
    latents = cond.shape[0]
    steps = latents // 4
    low = jnp.concatenate([pack[: steps * 8, :].astype(BF16) for pack in packs], 0)
    wanted = lax.broadcasted_iota(jnp.int32, (6 * latents, 4 * steps * 8), 0)
    source = lax.broadcasted_iota(jnp.int32, (6 * latents, 4 * steps * 8), 1)
    latent = wanted % latents
    found = ((own ^ (latent // steps)) * steps + latent % steps) * 8 + wanted // latents
    rows = dot_nn((source == found).astype(BF16), low).astype(BF16)
    everyone[: 6 * latents] = rows
    total = None
    for vector in range(6):
        partial = dot_nt(rows[vector * latents : (vector + 1) * latents], w_ada[vector])
        total = partial if total is None else total + partial
    cond_part[...] = total
    sums = sum(pack[steps * 8 :, :] for pack in packs)
    sums = jnp.concatenate([sums, jnp.zeros_like(sums)], 0)
    everyone[6 * latents : 6 * latents + 2 * BIAS_ROWS] = sums.astype(BF16)
    everyone[6 * latents + 2 * BIAS_ROWS :] = cond[...]


def modulation_grads(pos, *refs):
    everyone, (w_out, b_out, fc1_out, qkv_out, proj_out, fc2_out) = refs[:-6], refs[-6:]
    third = D // GROUPS
    quarter = D // 4
    latents = (refs[0].shape[1] - 2 * BIAS_ROWS) // 7

    def rows_of(start, size):
        found = [ref[:, start : start + size, :].reshape(-1, third) for ref in everyone]
        return jnp.concatenate(found, 0)

    rows = lax.broadcasted_iota(jnp.int32, (third, third * 6), 0)
    columns = lax.broadcasted_iota(jnp.int32, (third, third * 6), 1)
    total = None
    for vector in range(6):
        grads = rows_of(vector * latents, latents)
        select = (columns == rows * 6 + vector).astype(BF16)
        partial = dot_nn(grads, select)
        total = partial if total is None else total + partial
        summed = jnp.sum(grads.astype(F32), axis=0, keepdims=True)
        b_out[vector : vector + 1, :] = jnp.where(
            pos[1] == 0, summed[:, :quarter], summed[:, quarter:]
        )
    cond = rows_of(6 * latents + 2 * BIAS_ROWS, latents)
    w_out[...] = dot_tn(cond, total.astype(BF16))
    sums = rows_of(6 * latents, 2 * BIAS_ROWS).astype(F32)
    sums = jnp.sum(sums.reshape(-1, 2 * BIAS_ROWS, third), axis=0)
    qkv_out[...] = sums[0:2]
    proj_out[...] = sums[2:3, :quarter]
    fc2_out[...] = sums[3:4, :quarter]
    fc1_out[...] = sums[4:8]


def place_features(pieces, target, pos):
    own = pos[0] * 2 + pos[1]
    for step, piece in enumerate(pieces):
        height = piece.shape[0]
        at = pl.multiple_of((own ^ step) * height, height)
        target[pl.ds(at, height), :] = piece[...].astype(target.dtype)


def split_features(source, pieces, pos):
    own = pos[0] * 2 + pos[1]
    for step, piece in enumerate(pieces):
        height = piece.shape[0]
        at = pl.multiple_of((own ^ step) * height, height)
        piece[...] = source[pl.ds(at, height), :].astype(piece.dtype)


def attention_forward(
    pos, x0, x1, x2, x3, wq0, wq1, wq2, wq3, wp0, wp1, wp2, wp3, pack0, pack1, pack2, pack3,
    x_out, mod_one_out, qkv_out, probs_out, attended_out, branch_out, mod,
    x_s, wq_s, wq_t, wp_s, wp_t, bias_q, bias_v, bias_p,
):
    @pl.when(pl.program_id(0) == 0)
    def _():
        place_split((wq0, wq1, wq2, wq3), wq_s, pos)
        place_proj((wp0, wp1, wp2, wp3), wp_s, pos)
        bias_columns((pack0, pack1, pack2, pack3), pos, bias_q, bias_v, bias_p, None)
        for part in range(GROUPS):
            wq_t[part] = wq_s[part].T
            wp_t[part] = wp_s[part].T

    third = D // GROUPS
    for first, second, who in ((pack0, pack1, pos[0]), (pack2, pack3, 1 - pos[0])):
        rows = pl.ds(pl.multiple_of(pl.program_id(0) * 8, 8), 8)
        at = pl.multiple_of(who * third, third)
        mod[0, pl.ds(at, third), :] = (first[rows, :] + second[rows, :]).T
    place_features((x0, x1, x2, x3), x_s, pos)
    x = x_s[...]
    x_out[...] = x.astype(BF16)
    normed, _ = norm_stats(x)
    mod_one = (normed * (1.0 + mod[0, :, 1:2]) + mod[0, :, 0:1]).astype(BF16)
    mod_one_out[...] = mod_one
    per_group = HEADS // GROUPS
    heads = []
    for part in range(GROUPS):
        qkv = dot_nn(wq_t[part], mod_one)
        base = part * third
        query = (qkv[:third] + bias_q[base : base + third]).astype(BF16)
        keys = qkv[third : 2 * third].astype(BF16)
        values = (qkv[2 * third :] + bias_v[base : base + third]).astype(BF16)
        qkv_out[part, :third] = query
        qkv_out[part, third : 2 * third] = keys
        qkv_out[part, 2 * third :] = values
        scaled = query * jnp.asarray(HD ** (-0.5), BF16)
        for head in range(per_group):
            rows = slice(head * HD, (head + 1) * HD)
            heads.append((keys[rows], scaled[rows], values[rows]))
    scores = [dot_nn(keys.T, query) for keys, query, _ in heads]
    probs = []
    for score in scores:
        raised = jnp.exp(score - jnp.max(score, axis=0, keepdims=True))
        total = jnp.sum(raised, axis=0, keepdims=True)
        probs.append((raised * (1.0 / total)).astype(BF16))
    for head, prob in enumerate(probs):
        probs_out[0, head] = prob
        attended_out[head * HD : (head + 1) * HD] = dot_nn(heads[head][2], prob).astype(BF16)
    attended = attended_out[...]
    for part in range(2):
        rows = slice(part * third, (part + 1) * third)
        branch_out[rows] = dot_nn(wp_t[part], attended) + bias_p[rows]


def mlp_forward(
    pos, x, branch, mod, w10, w11, w12, w13, w20, w21, w22, w23, pack0, pack1, pack2, pack3,
    b10, b11,
    out0, out1, out2, out3, mod_two_out, act_out, slope_out, mlp_out,
    w1_s, w1_t, w2_s, block_s, bias_1, bias_2,
):
    @pl.when(pl.program_id(0) == 0)
    def _():
        bias_columns((pack0, pack1, pack2, pack3), pos, None, None, None, bias_2)
        for step, piece in enumerate((b10, b11)):
            height = piece.shape[1]
            column = jnp.broadcast_to(piece[...].astype(F32), (8, height)).T
            at = pl.multiple_of((pos[1] ^ step) * height, height)
            bias_1[pl.ds(at, height), :] = column[:, 0:1]
        place_split((w10, w11, w12, w13), w1_s, pos)
        place_split((w20, w21, w22, w23), w2_s, pos)
        for part in range(GROUPS):
            w1_t[part] = w1_s[part].T

    hidden = x[...].astype(F32) + mod[0, :, 2:3] * branch[...]
    normed, _ = norm_stats(hidden)
    mod_two = (normed * (1.0 + mod[0, :, 4:5]) + mod[0, :, 3:4]).astype(BF16)
    mod_two_out[...] = mod_two
    half = FF // GROUPS
    slope = (2.0 / jnp.pi) ** 0.5
    parts = [slice(part * half, (part + 1) * half) for part in range(GROUPS)]
    pres = [dot_nn(w1_t[part], mod_two) + bias_1[rows] for part, rows in enumerate(parts)]
    acts = []
    for pre, rows in zip(pres, parts):
        square = pre * pre
        tanh = jnp.tanh(pre * (slope + (slope * 0.044715) * square))
        upper = 0.5 + 0.5 * tanh
        acts.append((pre * upper).astype(BF16))
        act_out[rows] = acts[-1]
        slope_out[rows] = (
            upper + pre * (1.0 - tanh * tanh) * (0.5 * slope + (1.5 * slope * 0.044715) * square)
        ).astype(BF16)
    total = dot_nn(w2_s[0], acts[0]) + dot_nn(w2_s[1], acts[1])
    mlp = total + bias_2[...]
    mlp_out[...] = mlp
    block_s[...] = hidden + mod[0, :, 5:6] * mlp
    split_features(block_s, (out0, out1, out2, out3), pos)


def mlp_backward(
    pos, g0, g1, g2, g3, x, branch, mod, mod_two, act, slope, mlp, attended,
    w10, w11, w12, w13, w20, w21, w22, w23, wp0, wp1, wp2, wp3,
    hidden_grad_out, context_out, mod_grad_out, send_out, keep_out, sum1_out, sum2_out, sump_out,
    g_s, w1_s, w2_s, w2_t, wp_s, acc1, acc2, accp, sum1, sum2, sump,
):
    step = pl.program_id(0)

    @pl.when(step == 0)
    def _():
        place_split((w10, w11, w12, w13), w1_s, pos)
        place_split((w20, w21, w22, w23), w2_s, pos)
        place_proj((wp0, wp1, wp2, wp3), wp_s, pos)
        for part in range(GROUPS):
            w2_t[part] = w2_s[part].T
        for acc in (acc1, acc2, accp, sum1, sum2, sump):
            acc[...] = jnp.zeros_like(acc)

    place_features((g0, g1, g2, g3), g_s, pos)
    grad = g_s[...]
    gate_one = mod[0, :, 2:3]
    gate_two = mod[0, :, 5:6]
    hidden = x[...].astype(F32) + gate_one * branch[...]
    normed, inverse = norm_stats(hidden)
    mod_grad_out[0, :, 3:4] = lane_sum(grad * mlp[...])
    mlp_grad = (gate_two * grad).astype(BF16)
    sum2[...] += lane_fold(mlp_grad.astype(F32))
    half = FF // GROUPS
    third = D // GROUPS
    mod_two_low = mod_two[...]
    parts = [slice(part * half, (part + 1) * half) for part in range(GROUPS)]
    act_grads = [dot_nn(w2_t[part], mlp_grad) for part in range(GROUPS)]
    pre_grads = []
    for act_grad, rows in zip(act_grads, parts):
        pre_grads.append((act_grad * slope[rows].astype(F32)).astype(BF16))
        sum1[rows] += lane_fold(pre_grads[-1].astype(F32))
    back = dot_nn(w1_s[0], pre_grads[0]) + dot_nn(w1_s[1], pre_grads[1])
    for part, rows in enumerate(parts):
        acc2[part] += dot_nt(mlp_grad, act[rows])
        acc1[part] += dot_nt(mod_two_low, pre_grads[part])
    mod_grad_out[0, :, 1:2] = lane_sum(back)
    mod_grad_out[0, :, 2:3] = lane_sum(back * normed)
    hidden_grad = grad + norm_back(back * (1.0 + mod[0, :, 4:5]), normed, inverse)
    hidden_grad_out[...] = hidden_grad
    mod_grad_out[0, :, 0:1] = lane_sum(hidden_grad * branch[...])
    branch_grad = (gate_one * hidden_grad).astype(BF16)
    sump[...] += lane_fold(branch_grad.astype(F32))
    context = None
    for part in range(2):
        rows = slice(part * third, (part + 1) * third)
        accp[part] += dot_nt(attended[...], branch_grad[rows])
        partial = dot_nn(wp_s[part], branch_grad[rows])
        context = partial if context is None else context + partial
    context_out[...] = context.astype(BF16)

    @pl.when(step == pl.num_programs(0) - 1)
    def _():
        mine = pl.multiple_of(pos[0] * third, third)
        other = pl.multiple_of((1 - pos[0]) * third, third)
        for part in range(GROUPS):
            rows = slice(part * third, (part + 1) * third)
            for out, at, who in ((send_out, other, 1 - pos[0]), (keep_out, mine, pos[0])):
                out[part, :, :half] = acc1[part, pl.ds(at, third), :].astype(out.dtype)
                out[part, :, half : 2 * half] = acc2[part, pl.ds(at, third), :].astype(out.dtype)
                out[part, :, 2 * half :] = accp[who, rows, :].astype(out.dtype)
        sum1_out[...] = lane_sum(sum1[...])
        sum2_out[...] = lane_sum(sum2[...])
        sump_out[...] = lane_sum(sump[...])


def attention_backward(
    pos, x, mod_one, mod, qkv, probs, context, hidden_grad, mod_grad, sum1, sum2, sump,
    wq0, wq1, wq2, wq3,
    left0, left1, left2, left3,
    out0, out1, out2, out3, send_out, keep_out, pack0, pack1, pack2, pack3, joined,
    wq_s, acc, sumq, sumv, grad_s, block_s, mod_s, bias_s,
):
    step = pl.program_id(0)

    @pl.when(step == 0)
    def _():
        place_split((wq0, wq1, wq2, wq3), wq_s, pos)
        for item in (acc, sumq, sumv):
            item[...] = jnp.zeros_like(item)

    third = D // GROUPS
    scale = HD ** (-0.5)
    mod_one_low = mod_one[...]
    per_group = HEADS // GROUPS
    heads = []
    for head in range(HEADS):
        part, at = head // per_group, head % per_group * HD
        heads.append(
            (
                qkv[part, at : at + HD],
                qkv[part, third + at : third + at + HD],
                qkv[part, 2 * third + at : 2 * third + at + HD],
                context[head * HD : (head + 1) * HD],
                probs[0, head],
            )
        )
    prob_grads = [dot_nn(values.T, grad) for _, _, values, grad, _ in heads]
    score_grads = []
    for prob_grad, (_, _, _, _, weight) in zip(prob_grads, heads):
        wide = weight.astype(F32)
        product = wide * prob_grad
        row_dot = jnp.sum(product, axis=0, keepdims=True)
        score_grads.append((product - wide * row_dot).astype(BF16))
    for head, (query, keys, _, grad, weight) in enumerate(heads):
        part, at = head // per_group, head % per_group * HD
        parts = (
            dot_nn(keys, score_grads[head]) * scale,
            dot_nt(query, score_grads[head]) * scale,
            dot_nt(grad, weight),
        )
        for which, value in enumerate(parts):
            start = which * third + at
            grad_s[part, start : start + HD] = value.astype(BF16)
    back = dot_nn(wq_s[0], grad_s[0]) + dot_nn(wq_s[1], grad_s[1])
    for part in range(GROUPS):
        base = part * third
        qkv_grad = grad_s[part]
        sumq[base : base + third] += lane_fold(qkv_grad[:third].astype(F32))
        sumv[base : base + third] += lane_fold(qkv_grad[2 * third :].astype(F32))
        acc[part] += dot_nt(mod_one_low, qkv_grad)
    normed, inverse = norm_stats(x[...].astype(F32))
    mod_s[...] = jnp.zeros_like(mod_s)
    mod_s[:, 0:1] = lane_sum(back)
    mod_s[:, 1:2] = lane_sum(back * normed)
    mod_s[:, 2:6] = mod_grad[0]
    packs = (pack0, pack1, pack2, pack3)
    rows = pl.ds(pl.multiple_of(step * 8, 8), 8)
    mine = pl.multiple_of(pos[0] * third, third)
    other = pl.multiple_of((1 - pos[0]) * third, third)
    vectors = mod_s[pl.ds(mine, third), :].T
    pack0[rows, :] = vectors
    pack1[rows, :] = vectors
    vectors = mod_s[pl.ds(other, third), :].T
    pack2[rows, :] = vectors
    pack3[rows, :] = vectors
    block_s[...] = hidden_grad[...] + norm_back(back * (1.0 + mod[0, :, 1:2]), normed, inverse)
    split_features(block_s, (out0, out1, out2, out3), pos)
    join_tokens(pos, left0, left1, left2, left3, joined)

    @pl.when(step == pl.num_programs(0) - 1)
    def _():
        for part in range(GROUPS):
            send_out[part] = acc[part, pl.ds(other, third), :].astype(send_out.dtype)
            keep_out[part] = acc[part, pl.ds(mine, third), :].astype(keep_out.dtype)

        own = pos[0] * 2 + pos[1]
        quarter = D // 4
        half = FF // GROUPS
        sumq[:, 0:1] = lane_sum(sumq[...])
        sumv[:, 0:1] = lane_sum(sumv[...])
        for index, pack in enumerate(packs):
            col = pos[1] ^ (index & 1)
            bias_s[...] = jnp.zeros_like(bias_s)
            for part in range(4):
                at = pl.multiple_of(col * half + part * third, third)
                bias_s[:, 4 + part : 5 + part] = sum1[pl.ds(at, third), :]
            at = pl.multiple_of(col * third, third)
            bias_s[:, 0:1] = sumq[pl.ds(at, third), 0:1]
            bias_s[:, 1:2] = sumv[pl.ds(at, third), 0:1]
            at = pl.multiple_of((own ^ index) * quarter, quarter)
            bias_s[:quarter, 2:3] = sump[pl.ds(at, quarter), :]
            bias_s[:quarter, 3:4] = sum2[pl.ds(at, quarter), :]
            pack[pack.shape[0] - BIAS_ROWS :, :] = bias_s[...].T


def call(kernel, pos, steps, seq, inputs, outputs, scratch, micros, name):
    def spec(kind, shape):
        rank = len(shape)
        if kind == "t":
            lead = (0,) * (rank - 1)
            return pl.BlockSpec(shape[:-1] + (seq,), lambda i, p: lead + (i,))
        if kind == "o":
            return pl.BlockSpec(
                shape[:-1] + (seq,), lambda i, p: (0, (p[0] * 2 + p[1]) * steps + i)
            )
        if kind == "j":
            return pl.BlockSpec(
                shape[:-1] + (shape[-1] // 4,), lambda i, p: (0, (p[0] * 2 + p[1]) ^ i)
            )
        if kind == "l":
            tail = (0,) * (rank - 1)
            return pl.BlockSpec((1,) + shape[1:], lambda i, p: (i,) + tail)
        zeros = (0,) * rank
        return pl.BlockSpec(shape, lambda i, p: zeros)

    size = sum(a.size * a.dtype.itemsize for _, a in inputs)
    size += sum(a.size * jnp.dtype(a.dtype).itemsize for _, a in outputs)
    return pl.pallas_call(
        kernel,
        grid_spec=pltpu.PrefetchScalarGridSpec(
            num_scalar_prefetch=1,
            grid=(steps,),
            in_specs=[spec(kind, a.shape) for kind, a in inputs],
            out_specs=[spec(kind, a.shape) for kind, a in outputs],
            scratch_shapes=scratch,
        ),
        out_shape=[a for _, a in outputs],
        compiler_params=pltpu.CompilerParams(
            dimension_semantics=("arbitrary",), vmem_limit_bytes=VMEM_BYTES
        ),
        cost_estimate=pl.CostEstimate(
            flops=int(micros * 1e9), bytes_accessed=size, transcendentals=0
        ),
        name=name,
    )(pos, *[a for _, a in inputs])


def swap(value, axis):
    return lax.ppermute(value, axis, [(0, 1), (1, 0)])


def group_step(value, step):
    return lax.ppermute(value, GROUP, [(at, at ^ step) for at in range(4)])


def gather_pieces(block, beside):
    return (block, beside, swap(block, "row"), swap(beside, "row"))


def in_order(own_first, other, index, axis):
    first = jnp.where(index == 0, own_first, other)
    second = jnp.where(index == 0, other, own_first)
    return jnp.stack([first, second], axis=axis)


def dp_bits():
    count = lax.axis_size("dp")
    return [1 << at for at in range(count.bit_length() - 1)]


def dp_step(value, bit):
    count = lax.axis_size("dp")
    return lax.ppermute(value, "dp", [(at, at ^ bit) for at in range(count)])


def scatter_terms(value):
    count = lax.axis_size("dp")
    cols, rows, columns = value.shape
    blocks = value.reshape(cols * count, rows // count, columns)
    return lax.all_to_all(blocks, ("col", "dp"), 0, 0)


def after(value, token):
    return lax.optimization_barrier((value, token))[0]


def double(value, bit):
    here = (lax.axis_index("dp") // bit) % 2
    return in_order(value, dp_step(value, bit), here, value.ndim - 2)


def local(
    block_input, condition, w_ada, b_ada, w_qkv, b_qkv, w_proj, b_proj, w_fc1, b_fc1, w_fc2,
    b_fc2, out_grad,
):
    row = lax.axis_index("row")
    col = lax.axis_index("col")
    pos = jnp.stack([row, col]).astype(jnp.int32)
    latents = condition.shape[0]
    tokens = block_input.shape[1]
    seq = tokens // latents
    steps = latents // 4
    width = tokens // 4
    third = D // GROUPS
    half = FF // GROUPS
    quarter = D // 4
    pack_rows = steps * 8 + BIAS_ROWS

    def shape(dims, kind):
        return jax.ShapeDtypeStruct(dims, kind)

    t_low = shape((D, width), BF16)
    t_wide = shape((D, width), F32)
    t_ff = shape((FF, width), BF16)
    t_piece = shape((quarter, width), BF16)
    pack = ("w", shape((pack_rows, third), F32))

    wq_beside, wp_beside = swap(w_qkv, "col"), swap(w_proj, "col")
    *packs, cond_low, w_ada_by_vector = call(
        modulation_parts, pos, 1, seq,
        [("w", condition), ("w", w_ada), ("w", b_ada), ("w", b_qkv),
         ("w", b_proj.reshape(1, -1)), ("w", b_fc2.reshape(1, -1))],
        [pack] * 4 + [("w", shape(condition.shape, BF16)), ("w", shape((6, third, third), BF16))],
        [], 6, "modulation_parts",
    )

    def cut(value, name):
        return call(
            cut_tokens, pos, 1, seq, [("w", value)], [("w", t_piece)] * 3, [], 3, name
        )

    packs, wq_beside, wp_beside, block_input = lax.optimization_barrier(
        (packs, wq_beside, wp_beside, block_input)
    )
    x_cuts = cut(block_input, "cut_input")
    x_moved = [group_step(piece, step) for step, piece in zip((1, 2, 3), x_cuts)]
    packs = [packs[0]] + [group_step(packs[step], step) for step in (1, 2, 3)]
    wq = gather_pieces(w_qkv, wq_beside)
    wp = gather_pieces(w_proj, wp_beside)
    out_late, b_fc1 = after((out_grad, b_fc1), x_cuts[0])
    g_cuts = cut(out_late, "cut_grad")
    b_fc1 = b_fc1.reshape(1, -1)
    x_moved, wq, wp, packs, g_cuts, w_fc1, w_fc2, b_fc1 = lax.optimization_barrier(
        (x_moved, wq, wp, packs, g_cuts, w_fc1, w_fc2, b_fc1)
    )
    w1_beside, w2_beside = swap(w_fc1, "col"), swap(w_fc2, "col")
    w1_row, w2_row = swap(w_fc1, "row"), swap(w_fc2, "row")
    b_fc1 = (b_fc1, swap(b_fc1, "col"))
    x, mod_one, qkv, probs, attended, branch, mod = call(
        attention_forward, pos, steps, seq,
        [("o", block_input)] + [("t", a) for a in x_moved]
        + [("w", a) for a in (*wq, *wp, *packs)],
        [("t", t_low), ("t", t_low), ("t", shape((2, 3 * third, width), BF16)),
         ("l", shape((steps, HEADS, seq, seq), BF16)), ("t", t_low), ("t", t_wide),
         ("l", shape((steps, D, 8), F32))],
        [pltpu.VMEM((D, seq), F32), pltpu.VMEM((2, D, 3 * third), BF16),
         pltpu.VMEM((2, 3 * third, D), BF16), pltpu.VMEM((2, D, third), BF16),
         pltpu.VMEM((2, third, D), BF16), pltpu.VMEM((D, 1), F32), pltpu.VMEM((D, 1), F32),
         pltpu.VMEM((D, 1), F32)],
        16, "attention_forward",
    )

    g_cuts, branch, w1_beside, w2_beside, w1_row, w2_row, b_fc1 = lax.optimization_barrier(
        (g_cuts, branch, w1_beside, w2_beside, w1_row, w2_row, b_fc1)
    )
    w1 = (w_fc1, w1_beside, w1_row, swap(w1_beside, "row"))
    w2 = (w_fc2, w2_beside, w2_row, swap(w2_beside, "row"))
    g_moved = [group_step(piece, step) for step, piece in zip((1, 2, 3), g_cuts)]
    *outs, mod_two, act, slope, mlp = call(
        mlp_forward, pos, steps, seq,
        [("t", x), ("t", branch), ("l", mod)] + [("w", a) for a in w1 + w2]
        + [("w", a) for a in (*packs, *b_fc1)],
        [("t", t_piece)] * 4 + [("t", t_low), ("t", t_ff), ("t", t_ff), ("t", t_wide)],
        [pltpu.VMEM((2, D, half), BF16), pltpu.VMEM((2, half, D), BF16),
         pltpu.VMEM((2, D, half), BF16), pltpu.VMEM((D, seq), F32), pltpu.VMEM((FF, 1), F32),
         pltpu.VMEM((D, 1), F32)],
        12, "mlp_forward",
    )
    outs, g_moved, mlp = lax.optimization_barrier((outs, g_moved, mlp))
    outs = [outs[0]] + [group_step(outs[step], step) for step in (1, 2, 3)]
    fc_block = (2, third, 2 * half + third)
    qkv_block = (2, third, 3 * third)
    blocks = lambda dims: [("w", shape(dims, BF16))] * 2
    hidden_grad, context, mod_grad, send_fc, keep_fc, sum1, sum2, sump = call(
        mlp_backward, pos, steps, seq,
        [("o", out_grad)] + [("t", a) for a in g_moved]
        + [("t", x), ("t", branch), ("l", mod), ("t", mod_two), ("t", act), ("t", slope),
           ("t", mlp), ("t", attended)]
        + [("w", a) for a in w1 + w2 + wp],
        [("t", t_wide), ("t", t_low), ("l", shape((steps, D, 4), F32))] + blocks(fc_block)
        + [("w", shape((FF, 1), F32)), ("w", shape((D, 1), F32)), ("w", shape((D, 1), F32))],
        [pltpu.VMEM((D, seq), F32), pltpu.VMEM((2, D, half), BF16), pltpu.VMEM((2, D, half), BF16),
         pltpu.VMEM((2, half, D), BF16), pltpu.VMEM((2, D, third), BF16),
         pltpu.VMEM((2, D, half), F32), pltpu.VMEM((2, D, half), F32),
         pltpu.VMEM((2, D, third), F32), pltpu.VMEM((FF, 128), F32),
         pltpu.VMEM((D, 128), F32), pltpu.VMEM((D, 128), F32)],
        20, "mlp_backward",
    )
    outs, send_fc = lax.optimization_barrier((outs, send_fc))
    fc = (keep_fc.astype(F32) + swap(send_fc, "row").astype(F32)).astype(BF16)
    fc, context = lax.optimization_barrier((fc, context))
    fc_parts = scatter_terms(fc)

    *ins, send_qkv, keep_qkv, back0, back1, back2, back3, block_output = call(
        attention_backward, pos, steps, seq,
        [("t", x), ("t", mod_one), ("l", mod), ("t", qkv), ("l", probs), ("t", context),
         ("t", hidden_grad), ("l", mod_grad), ("w", sum1), ("w", sum2), ("w", sump)]
        + [("w", a) for a in (*wq, *outs)],
        [("t", t_piece)] * 4 + blocks(qkv_block) + [pack] * 4
        + [("j", shape((quarter, tokens), F32))],
        [pltpu.VMEM((2, D, 3 * third), BF16), pltpu.VMEM((2, D, 3 * third), F32),
         pltpu.VMEM((D, 128), F32), pltpu.VMEM((D, 128), F32),
         pltpu.VMEM((2, 3 * third, seq), BF16), pltpu.VMEM((D, seq), F32), pltpu.VMEM((D, 8), F32),
         pltpu.VMEM((third, 8), F32)],
        16, "attention_backward",
    )
    bits = list(reversed(dp_bits()))
    count = lax.axis_size("dp")
    qkv = (keep_qkv.astype(F32) + swap(send_qkv, "row").astype(F32)).astype(BF16)
    backs = [back0] + [group_step(a, step) for step, a in ((1, back1), (2, back2), (3, back3))]
    ins = [ins[0]] + [group_step(ins[step], step) for step in (1, 2, 3)]
    rows = 7 * latents + 2 * BIAS_ROWS
    everyone, cond_part = call(
        group_vectors, pos, 1, seq,
        [("w", a) for a in backs] + [("w", cond_low), ("w", w_ada_by_vector)],
        [("w", shape((rows, third), BF16)), ("w", shape(condition.shape, F32))], [], 2,
        "group_vectors",
    )
    everyone = everyone[None]
    for bit in bits[:-2]:
        everyone = jnp.concatenate([everyone, dp_step(everyone, bit)])
    cond_part = cond_part + swap(cond_part, "row")
    fc_parts, qkv, ins, everyone, cond_part = lax.optimization_barrier(
        (fc_parts, qkv, ins, everyone, cond_part)
    )
    qkv_parts = scatter_terms(qkv)
    fc = jnp.sum(fc_parts.astype(F32), axis=0).astype(BF16)
    for bit in bits[:-2]:
        fc = double(fc, bit)
    for bit in bits[-2:-1]:
        everyone = jnp.concatenate([everyone, dp_step(everyone, bit)])
    input_grad = call(
        join_tokens, pos, 4, seq, [("w", a) for a in ins],
        [("j", shape((quarter, tokens), F32))], [], 2, "join_tokens",
    )[0]
    qkv_parts, fc, everyone, input_grad = lax.optimization_barrier(
        (qkv_parts, fc, everyone, input_grad)
    )
    qkv = jnp.sum(qkv_parts.astype(F32), axis=0).astype(BF16)
    qkv = lax.all_to_all(jnp.broadcast_to(qkv[None], (count,) + qkv.shape), "dp", 0, 0)
    for bit in bits[-2:]:
        fc = double(fc, bit)
    for bit in bits[-1:]:
        everyone = jnp.concatenate([everyone, dp_step(everyone, bit)])
    grads_fc = fc.reshape(fc_block[1:]).astype(F32)
    grad_w_ada, grad_b_ada, grad_b_fc1, grad_b_qkv, grad_b_proj, grad_b_fc2 = call(
        modulation_grads, pos, 1, seq, [("w", everyone)],
        [("w", shape((third, 6 * third), F32)), ("w", shape((6, quarter), F32)),
         ("w", shape((4, third), F32)), ("w", shape((2, third), F32)),
         ("w", shape((1, quarter), F32)), ("w", shape((1, quarter), F32))], [], 2,
        "modulation_grads",
    )
    grads_qkv = qkv.reshape(qkv_block[1:]).astype(F32)
    silu_back = jax.vjp(jax.nn.silu, condition)[1]
    cond_grad = silu_back(cond_part)[0]
    return (
        block_output,
        input_grad,
        cond_grad,
        grad_w_ada,
        grad_b_ada,
        grads_qkv,
        grad_b_qkv,
        grads_fc[:, 2 * half :],
        grad_b_proj.reshape(-1),
        grads_fc[:, :half],
        grad_b_fc1.reshape(-1),
        grads_fc[:, half : 2 * half],
        grad_b_fc2.reshape(-1),
    )


def solution(mesh):
    return jax.shard_map(
        local,
        mesh=mesh,
        in_specs=(
            P(("row", "col"), "dp"),
            P("dp", "col"),
            P("col", "row"),
            P(None, ("row", "col")),
            P("row", "col"),
            P(None, "col"),
            P("col", "row"),
            P(("row", "col")),
            P("row", "col"),
            P("col"),
            P("row", "col"),
            P(("row", "col")),
            P(("row", "col"), "dp"),
        ),
        out_specs=(
            P(("row", "col"), "dp"),
            P(("row", "col"), "dp"),
            P("dp", "col"),
            P("col", "row"),
            P(None, ("row", "col")),
            P("row", "col"),
            P(None, "col"),
            P("col", "row"),
            P(("row", "col")),
            P("row", "col"),
            P("col"),
            P("row", "col"),
            P(("row", "col")),
        ),
        check_vma=False,
    )
```

```python
import jax
import jax.numpy as jnp
from jax import lax
from jax.experimental import pallas as pl
from jax.experimental.pallas import tpu as pltpu
from jax.sharding import PartitionSpec as P

D = 384
HEADS = 6
HD = 64
FF = 1536
GROUPS = 2
EPSILON = 1e-06
BF16 = jnp.bfloat16
F32 = jnp.float32
GROUP = ("row", "col")
LIMITS = {"modulation_parts": 60, "attention_forward": 15, "mlp_forward": 16, "mlp_backward": 27, "attention_backward": 20}


def dot_nn(left, right):
    return lax.dot_general(left, right, (((1,), (0,)), ((), ())), preferred_element_type=F32)


def dot_nt(left, right):
    return lax.dot_general(left, right, (((1,), (1,)), ((), ())), preferred_element_type=F32)


def dot_tn(left, right):
    return lax.dot_general(left, right, (((0,), (0,)), ((), ())), preferred_element_type=F32)


def lane_sum(value):
    return jnp.sum(value, axis=1, keepdims=True)


def lane_fold(value):
    parts = [value[:, at : at + 128] for at in range(0, value.shape[1], 128)]
    return sum(parts[1:], parts[0])


def norm_stats(value):
    center = jnp.sum(value, axis=0, keepdims=True) * (1.0 / D)
    square = jnp.sum(value * value, axis=0, keepdims=True) * (1.0 / D)
    inverse = lax.rsqrt(square - center * center + EPSILON)
    return (value - center) * inverse, inverse


def norm_back(grad, normed, inverse):
    first = jnp.sum(grad, axis=0, keepdims=True) * (1.0 / D)
    second = jnp.sum(grad * normed, axis=0, keepdims=True) * (1.0 / D)
    return inverse * (grad - first - normed * second)


PIECES = ((0, 0), (0, 1), (1, 0), (1, 1))


def place_split(pieces, target, pos):
    row, col = pos[0], pos[1]
    for piece, (step_row, step_col) in zip(pieces, PIECES):
        height = piece.shape[0]
        at = pl.multiple_of((row ^ step_row) * height, height)
        target[col ^ step_col, pl.ds(at, height), :] = piece[...]


def place_proj(pieces, target, pos):
    row, col = pos[0], pos[1]
    for piece, (step_row, step_col) in zip(pieces, PIECES):
        height = piece.shape[0]
        at = pl.multiple_of((col ^ step_col) * height, height)
        target[row ^ step_row, pl.ds(at, height), :] = piece[...]


BIAS_ROWS = 8


def bias_columns(packs, pos, query_s, value_s, proj_s, last_s):
    own, col = pos[0] * 2 + pos[1], pos[1]
    third = D // GROUPS
    quarter = D // 4
    for step, pack in enumerate(packs):
        columns = pack[pack.shape[0] - BIAS_ROWS :, :].T
        if step < 2 and query_s is not None:
            at = pl.multiple_of((col ^ step) * third, third)
            query_s[pl.ds(at, third), :] = columns[:, 0:1]
            value_s[pl.ds(at, third), :] = columns[:, 1:2]
        at = pl.multiple_of((own ^ step) * quarter, quarter)
        if proj_s is not None:
            proj_s[pl.ds(at, quarter), :] = columns[:quarter, 2:3]
        if last_s is not None:
            last_s[pl.ds(at, quarter), :] = columns[:quarter, 3:4]


def cut_tokens(pos, x, out1, out2, out3):
    own = pos[0] * 2 + pos[1]
    width = out1.shape[1]
    for step, out in ((1, out1), (2, out2), (3, out3)):
        at = pl.multiple_of((own ^ step) * width, width)
        out[...] = x[:, pl.ds(at, width)]


def piece_order(latents, steps, own):
    here = lax.broadcasted_iota(jnp.int32, (latents, latents), 0)
    there = lax.broadcasted_iota(jnp.int32, (latents, latents), 1)
    return (there == (own ^ (here // steps)) * steps + here % steps).astype(BF16)


def modulation_parts(
    pos, x, condition, w_ada, b_ada, b_qkv, b_proj, b_fc2,
    out1, out2, out3, pack0, pack1, pack2, pack3, cond_out, w_ada_out,
):
    cut_tokens(pos, x, out1, out2, out3)
    own, col = pos[0] * 2 + pos[1], pos[1]
    latents = condition.shape[0]
    steps = latents // 4
    third = D // GROUPS
    quarter = D // 4
    value = condition[...]
    cond_low = (value * jax.nn.sigmoid(value)).astype(BF16)
    cond_out[...] = cond_low
    ordered = dot_nn(piece_order(latents, steps, own), cond_low).astype(BF16)
    zeros = jnp.zeros((6, quarter), F32)
    bias = b_ada[...].astype(F32)
    bias = jnp.where(
        col == 0, jnp.concatenate([bias, zeros], 1), jnp.concatenate([zeros, bias], 1)
    )
    rows = lax.broadcasted_iota(jnp.int32, (third * 6, third), 0)
    columns = lax.broadcasted_iota(jnp.int32, (third * 6, third), 1)
    packs = (pack0, pack1, pack2, pack3)
    for vector in range(6):
        select = (rows == columns * 6 + vector).astype(BF16)
        weight = dot_nn(w_ada[...], select).astype(BF16)
        w_ada_out[vector] = weight
        part = dot_nn(ordered, weight) + bias[vector : vector + 1]
        for step in range(4):
            for at in range(steps):
                packs[step][at * 8 + vector : at * 8 + vector + 1, :] = part[
                    step * steps + at : step * steps + at + 1
                ]
    for pack in packs:
        at = steps * 8
        pack[at : at + 2, :] = b_qkv[...].astype(F32)
        pack[at + 2 : at + 8, :] = jnp.zeros((6, third), F32)
        pack[at + 2 : at + 3, :quarter] = b_proj[...].astype(F32)
        pack[at + 3 : at + 4, :quarter] = b_fc2[...].astype(F32)
        for latent in range(steps):
            pack[latent * 8 + 6 : latent * 8 + 8, :] = jnp.zeros((2, third), F32)


def join_tokens(pos, x0, x1, x2, x3, out):
    for step, piece in enumerate((x0, x1, x2, x3)):

        @pl.when(pl.program_id(0) == step)
        def _():
            out[...] = piece[...].astype(out.dtype)


def group_vectors(pos, pack0, pack1, pack2, pack3, cond, w_ada, everyone, cond_part):
    own = pos[0] * 2 + pos[1]
    packs = (pack0, pack1, pack2, pack3)
    latents = cond.shape[0]
    steps = latents // 4
    low = jnp.concatenate([pack[: steps * 8, :].astype(BF16) for pack in packs], 0)
    wanted = lax.broadcasted_iota(jnp.int32, (6 * latents, 4 * steps * 8), 0)
    source = lax.broadcasted_iota(jnp.int32, (6 * latents, 4 * steps * 8), 1)
    latent = wanted % latents
    found = ((own ^ (latent // steps)) * steps + latent % steps) * 8 + wanted // latents
    rows = dot_nn((source == found).astype(BF16), low).astype(BF16)
    everyone[: 6 * latents] = rows
    total = None
    for vector in range(6):
        partial = dot_nt(rows[vector * latents : (vector + 1) * latents], w_ada[vector])
        total = partial if total is None else total + partial
    cond_part[...] = total
    sums = sum(pack[steps * 8 :, :] for pack in packs)
    sums = jnp.concatenate([sums, jnp.zeros_like(sums)], 0)
    everyone[6 * latents : 6 * latents + 2 * BIAS_ROWS] = sums.astype(BF16)
    everyone[6 * latents + 2 * BIAS_ROWS :] = cond[...]


def modulation_grads(pos, *refs):
    everyone, (w_out, b_out, fc1_out, qkv_out, proj_out, fc2_out) = refs[:-6], refs[-6:]
    third = D // GROUPS
    quarter = D // 4
    latents = (refs[0].shape[1] - 2 * BIAS_ROWS) // 7

    def rows_of(start, size):
        found = [ref[:, start : start + size, :].reshape(-1, third) for ref in everyone]
        return jnp.concatenate(found, 0)

    rows = lax.broadcasted_iota(jnp.int32, (third, third * 6), 0)
    columns = lax.broadcasted_iota(jnp.int32, (third, third * 6), 1)
    total = None
    for vector in range(6):
        grads = rows_of(vector * latents, latents)
        select = (columns == rows * 6 + vector).astype(BF16)
        partial = dot_nn(grads, select)
        total = partial if total is None else total + partial
        summed = jnp.sum(grads.astype(F32), axis=0, keepdims=True)
        b_out[vector : vector + 1, :] = jnp.where(
            pos[1] == 0, summed[:, :quarter], summed[:, quarter:]
        )
    cond = rows_of(6 * latents + 2 * BIAS_ROWS, latents)
    w_out[...] = dot_tn(cond, total.astype(BF16))
    sums = rows_of(6 * latents, 2 * BIAS_ROWS).astype(F32)
    sums = jnp.sum(sums.reshape(-1, 2 * BIAS_ROWS, third), axis=0)
    qkv_out[...] = sums[0:2]
    proj_out[...] = sums[2:3, :quarter]
    fc2_out[...] = sums[3:4, :quarter]
    fc1_out[...] = sums[4:8]


def place_features(pieces, target, pos):
    own = pos[0] * 2 + pos[1]
    for step, piece in enumerate(pieces):
        height = piece.shape[0]
        at = pl.multiple_of((own ^ step) * height, height)
        target[pl.ds(at, height), :] = piece[...].astype(target.dtype)


def split_features(source, pieces, pos):
    own = pos[0] * 2 + pos[1]
    for step, piece in enumerate(pieces):
        height = piece.shape[0]
        at = pl.multiple_of((own ^ step) * height, height)
        piece[...] = source[pl.ds(at, height), :].astype(piece.dtype)


def attention_forward(
    pos, x0, x1, x2, x3, wq0, wq1, wq2, wq3, wp0, wp1, wp2, wp3, pack0, pack1, pack2, pack3,
    x_out, mod_one_out, qkv_out, probs_out, attended_out, branch_out, mod,
    x_s, wq_s, wq_t, wp_s, wp_t, bias_q, bias_v, bias_p,
):
    @pl.when(pl.program_id(0) == 0)
    def _():
        place_split((wq0, wq1, wq2, wq3), wq_s, pos)
        place_proj((wp0, wp1, wp2, wp3), wp_s, pos)
        bias_columns((pack0, pack1, pack2, pack3), pos, bias_q, bias_v, bias_p, None)
        for part in range(GROUPS):
            wq_t[part] = wq_s[part].T
            wp_t[part] = wp_s[part].T

    third = D // GROUPS
    for first, second, who in ((pack0, pack1, pos[0]), (pack2, pack3, 1 - pos[0])):
        rows = pl.ds(pl.multiple_of(pl.program_id(0) * 8, 8), 8)
        at = pl.multiple_of(who * third, third)
        mod[0, pl.ds(at, third), :] = (first[rows, :] + second[rows, :]).T
    place_features((x0, x1, x2, x3), x_s, pos)
    x = x_s[...]
    x_out[...] = x.astype(BF16)
    normed, _ = norm_stats(x)
    mod_one = (normed * (1.0 + mod[0, :, 1:2]) + mod[0, :, 0:1]).astype(BF16)
    mod_one_out[...] = mod_one
    per_group = HEADS // GROUPS
    heads = []
    for part in range(GROUPS):
        qkv = dot_nn(wq_t[part], mod_one)
        base = part * third
        query = (qkv[:third] + bias_q[base : base + third]).astype(BF16)
        keys = qkv[third : 2 * third].astype(BF16)
        values = (qkv[2 * third :] + bias_v[base : base + third]).astype(BF16)
        qkv_out[part, :third] = query
        qkv_out[part, third : 2 * third] = keys
        qkv_out[part, 2 * third :] = values
        scaled = query * jnp.asarray(HD ** (-0.5), BF16)
        for head in range(per_group):
            rows = slice(head * HD, (head + 1) * HD)
            heads.append((keys[rows], scaled[rows], values[rows]))
    scores = [dot_nn(keys.T, query) for keys, query, _ in heads]
    probs = []
    for score in scores:
        raised = jnp.exp(score - jnp.max(score, axis=0, keepdims=True))
        total = jnp.sum(raised, axis=0, keepdims=True)
        probs.append((raised * (1.0 / total)).astype(BF16))
    for head, prob in enumerate(probs):
        probs_out[0, head] = prob
        attended_out[head * HD : (head + 1) * HD] = dot_nn(heads[head][2], prob).astype(BF16)
    attended = attended_out[...]
    for part in range(2):
        rows = slice(part * third, (part + 1) * third)
        branch_out[rows] = dot_nn(wp_t[part], attended) + bias_p[rows]


def mlp_forward(
    pos, x, branch, mod, w10, w11, w12, w13, w20, w21, w22, w23, pack0, pack1, pack2, pack3,
    b10, b11,
    out0, out1, out2, out3, mod_two_out, act_out, slope_out, mlp_out,
    w1_s, w1_t, w2_s, block_s, bias_1, bias_2,
):
    @pl.when(pl.program_id(0) == 0)
    def _():
        bias_columns((pack0, pack1, pack2, pack3), pos, None, None, None, bias_2)
        for step, piece in enumerate((b10, b11)):
            height = piece.shape[1]
            column = jnp.broadcast_to(piece[...].astype(F32), (8, height)).T
            at = pl.multiple_of((pos[1] ^ step) * height, height)
            bias_1[pl.ds(at, height), :] = column[:, 0:1]
        place_split((w10, w11, w12, w13), w1_s, pos)
        place_split((w20, w21, w22, w23), w2_s, pos)
        for part in range(GROUPS):
            w1_t[part] = w1_s[part].T

    hidden = x[...].astype(F32) + mod[0, :, 2:3] * branch[...]
    normed, _ = norm_stats(hidden)
    mod_two = (normed * (1.0 + mod[0, :, 4:5]) + mod[0, :, 3:4]).astype(BF16)
    mod_two_out[...] = mod_two
    half = FF // GROUPS
    slope = (2.0 / jnp.pi) ** 0.5
    parts = [slice(part * half, (part + 1) * half) for part in range(GROUPS)]
    pres = [dot_nn(w1_t[part], mod_two) + bias_1[rows] for part, rows in enumerate(parts)]
    acts = []
    for pre, rows in zip(pres, parts):
        square = pre * pre
        tanh = jnp.tanh(pre * (slope + (slope * 0.044715) * square))
        upper = 0.5 + 0.5 * tanh
        acts.append((pre * upper).astype(BF16))
        act_out[rows] = acts[-1]
        slope_out[rows] = (
            upper + pre * (1.0 - tanh * tanh) * (0.5 * slope + (1.5 * slope * 0.044715) * square)
        ).astype(BF16)
    total = dot_nn(w2_s[0], acts[0]) + dot_nn(w2_s[1], acts[1])
    mlp = total + bias_2[...]
    mlp_out[...] = mlp
    block_s[...] = hidden + mod[0, :, 5:6] * mlp
    split_features(block_s, (out0, out1, out2, out3), pos)


def mlp_backward(
    pos, g0, g1, g2, g3, x, branch, mod, mod_two, act, slope, mlp, attended,
    w10, w11, w12, w13, w20, w21, w22, w23, wp0, wp1, wp2, wp3,
    hidden_grad_out, context_out, mod_grad_out, send_t, send_m, keep_t, keep_m, sum1_out, sum2_out, sump_out,
    g_s, w1_s, w2_s, w2_t, wp_s, acc1, acc2, accp, sum1, sum2, sump,
):
    step = pl.program_id(0)

    @pl.when(step == 0)
    def _():
        place_split((w10, w11, w12, w13), w1_s, pos)
        place_split((w20, w21, w22, w23), w2_s, pos)
        place_proj((wp0, wp1, wp2, wp3), wp_s, pos)
        for part in range(GROUPS):
            w2_t[part] = w2_s[part].T
        for acc in (acc1, acc2, accp, sum1, sum2, sump):
            acc[...] = jnp.zeros_like(acc)

    place_features((g0, g1, g2, g3), g_s, pos)
    grad = g_s[...]
    gate_one = mod[0, :, 2:3]
    gate_two = mod[0, :, 5:6]
    hidden = x[...].astype(F32) + gate_one * branch[...]
    normed, inverse = norm_stats(hidden)
    mod_grad_out[0, :, 3:4] = lane_sum(grad * mlp[...])
    mlp_grad = (gate_two * grad).astype(BF16)
    sum2[...] += lane_fold(mlp_grad.astype(F32))
    half = FF // GROUPS
    third = D // GROUPS
    mod_two_low = mod_two[...]
    parts = [slice(part * half, (part + 1) * half) for part in range(GROUPS)]
    act_grads = [dot_nn(w2_t[part], mlp_grad) for part in range(GROUPS)]
    pre_grads = []
    for act_grad, rows in zip(act_grads, parts):
        pre_grads.append((act_grad * slope[rows].astype(F32)).astype(BF16))
        sum1[rows] += lane_fold(pre_grads[-1].astype(F32))
    back = dot_nn(w1_s[0], pre_grads[0]) + dot_nn(w1_s[1], pre_grads[1])
    for part, rows in enumerate(parts):
        acc2[part] += dot_nt(mlp_grad, act[rows])
        acc1[part] += dot_nt(mod_two_low, pre_grads[part])
    mod_grad_out[0, :, 1:2] = lane_sum(back)
    mod_grad_out[0, :, 2:3] = lane_sum(back * normed)
    hidden_grad = grad + norm_back(back * (1.0 + mod[0, :, 4:5]), normed, inverse)
    hidden_grad_out[...] = hidden_grad
    mod_grad_out[0, :, 0:1] = lane_sum(hidden_grad * branch[...])
    branch_grad = (gate_one * hidden_grad).astype(BF16)
    sump[...] += lane_fold(branch_grad.astype(F32))
    context = None
    for part in range(2):
        rows = slice(part * third, (part + 1) * third)
        accp[part] += dot_nt(attended[...], branch_grad[rows])
        partial = dot_nn(wp_s[part], branch_grad[rows])
        context = partial if context is None else context + partial
    context_out[...] = context.astype(BF16)

    @pl.when(step == pl.num_programs(0) - 1)
    def _():
        mine = pl.multiple_of(pos[0] * third, third)
        other = pl.multiple_of((1 - pos[0]) * third, third)
        for part, pair in ((pos[1], (send_m, keep_m)), (1 - pos[1], (send_t, keep_t))):
            rows = pl.ds(pl.multiple_of(part * third, third), third)
            for out, at, who in ((pair[0], other, 1 - pos[0]), (pair[1], mine, pos[0])):
                out[:, :half] = acc1[part, pl.ds(at, third), :].astype(out.dtype)
                out[:, half : 2 * half] = acc2[part, pl.ds(at, third), :].astype(out.dtype)
                out[:, 2 * half :] = accp[who, rows, :].astype(out.dtype)
        sum1_out[...] = lane_sum(sum1[...])
        sum2_out[...] = lane_sum(sum2[...])
        sump_out[...] = lane_sum(sump[...])


def attention_backward(
    pos, x, mod_one, mod, qkv, probs, context, hidden_grad, mod_grad, sum1, sum2, sump,
    wq0, wq1, wq2, wq3,
    left0, left1, left2, left3,
    out0, out1, out2, out3, send_t, send_m, keep_t, keep_m, pack0, pack1, pack2, pack3, joined,
    wq_s, acc, sumq, sumv, grad_s, block_s, mod_s, bias_s,
):
    step = pl.program_id(0)

    @pl.when(step == 0)
    def _():
        place_split((wq0, wq1, wq2, wq3), wq_s, pos)
        for item in (acc, sumq, sumv):
            item[...] = jnp.zeros_like(item)

    third = D // GROUPS
    scale = HD ** (-0.5)
    mod_one_low = mod_one[...]
    per_group = HEADS // GROUPS
    heads = []
    for head in range(HEADS):
        part, at = head // per_group, head % per_group * HD
        heads.append(
            (
                qkv[part, at : at + HD],
                qkv[part, third + at : third + at + HD],
                qkv[part, 2 * third + at : 2 * third + at + HD],
                context[head * HD : (head + 1) * HD],
                probs[0, head],
            )
        )
    prob_grads = [dot_nn(values.T, grad) for _, _, values, grad, _ in heads]
    score_grads = []
    for prob_grad, (_, _, _, _, weight) in zip(prob_grads, heads):
        wide = weight.astype(F32)
        product = wide * prob_grad
        row_dot = jnp.sum(product, axis=0, keepdims=True)
        score_grads.append((product - wide * row_dot).astype(BF16))
    for head, (query, keys, _, grad, weight) in enumerate(heads):
        part, at = head // per_group, head % per_group * HD
        parts = (
            dot_nn(keys, score_grads[head]) * scale,
            dot_nt(query, score_grads[head]) * scale,
            dot_nt(grad, weight),
        )
        for which, value in enumerate(parts):
            start = which * third + at
            grad_s[part, start : start + HD] = value.astype(BF16)
    back = dot_nn(wq_s[0], grad_s[0]) + dot_nn(wq_s[1], grad_s[1])
    for part in range(GROUPS):
        base = part * third
        qkv_grad = grad_s[part]
        sumq[base : base + third] += lane_fold(qkv_grad[:third].astype(F32))
        sumv[base : base + third] += lane_fold(qkv_grad[2 * third :].astype(F32))
        acc[part] += dot_nt(mod_one_low, qkv_grad)
    normed, inverse = norm_stats(x[...].astype(F32))
    mod_s[...] = jnp.zeros_like(mod_s)
    mod_s[:, 0:1] = lane_sum(back)
    mod_s[:, 1:2] = lane_sum(back * normed)
    mod_s[:, 2:6] = mod_grad[0]
    packs = (pack0, pack1, pack2, pack3)
    rows = pl.ds(pl.multiple_of(step * 8, 8), 8)
    mine = pl.multiple_of(pos[0] * third, third)
    other = pl.multiple_of((1 - pos[0]) * third, third)
    vectors = mod_s[pl.ds(mine, third), :].T
    pack0[rows, :] = vectors
    pack1[rows, :] = vectors
    vectors = mod_s[pl.ds(other, third), :].T
    pack2[rows, :] = vectors
    pack3[rows, :] = vectors
    block_s[...] = hidden_grad[...] + norm_back(back * (1.0 + mod[0, :, 1:2]), normed, inverse)
    split_features(block_s, (out0, out1, out2, out3), pos)
    join_tokens(pos, left0, left1, left2, left3, joined)

    @pl.when(step == pl.num_programs(0) - 1)
    def _():
        for part, send, keep in ((pos[1], send_m, keep_m), (1 - pos[1], send_t, keep_t)):
            send[...] = acc[part, pl.ds(other, third), :].astype(send.dtype)
            keep[...] = acc[part, pl.ds(mine, third), :].astype(keep.dtype)

        own = pos[0] * 2 + pos[1]
        quarter = D // 4
        half = FF // GROUPS
        sumq[:, 0:1] = lane_sum(sumq[...])
        sumv[:, 0:1] = lane_sum(sumv[...])
        for index, pack in enumerate(packs):
            col = pos[1] ^ (index & 1)
            bias_s[...] = jnp.zeros_like(bias_s)
            for part in range(4):
                at = pl.multiple_of(col * half + part * third, third)
                bias_s[:, 4 + part : 5 + part] = sum1[pl.ds(at, third), :]
            at = pl.multiple_of(col * third, third)
            bias_s[:, 0:1] = sumq[pl.ds(at, third), 0:1]
            bias_s[:, 1:2] = sumv[pl.ds(at, third), 0:1]
            at = pl.multiple_of((own ^ index) * quarter, quarter)
            bias_s[:quarter, 2:3] = sump[pl.ds(at, quarter), :]
            bias_s[:quarter, 3:4] = sum2[pl.ds(at, quarter), :]
            pack[pack.shape[0] - BIAS_ROWS :, :] = bias_s[...].T


def call(kernel, pos, steps, seq, inputs, outputs, scratch, micros, name):
    def spec(kind, shape):
        kind = kind[0]
        rank = len(shape)
        if kind == "t":
            lead = (0,) * (rank - 1)
            return pl.BlockSpec(shape[:-1] + (seq,), lambda i, p: lead + (i,))
        if kind == "o":
            return pl.BlockSpec(
                shape[:-1] + (seq,), lambda i, p: (0, (p[0] * 2 + p[1]) * steps + i)
            )
        if kind == "j":
            return pl.BlockSpec(
                shape[:-1] + (shape[-1] // 4,), lambda i, p: (0, (p[0] * 2 + p[1]) ^ i)
            )
        if kind == "l":
            tail = (0,) * (rank - 1)
            return pl.BlockSpec((1,) + shape[1:], lambda i, p: (i,) + tail)
        zeros = (0,) * rank
        if steps > 1:
            return pl.BlockSpec(shape, lambda i, p: zeros, pipeline_mode=pl.Buffered(1))
        return pl.BlockSpec(shape, lambda i, p: zeros)

    size = sum(a.size * a.dtype.itemsize for _, a in inputs)
    size += sum(a.size * jnp.dtype(a.dtype).itemsize for _, a in outputs)
    return pl.pallas_call(
        kernel,
        grid_spec=pltpu.PrefetchScalarGridSpec(
            num_scalar_prefetch=1,
            grid=(steps,),
            in_specs=[spec(kind, a.shape) for kind, a in inputs],
            out_specs=[spec(kind, a.shape) for kind, a in outputs],
            scratch_shapes=scratch,
        ),
        out_shape=[
            pltpu.VMEM(a.shape, a.dtype) if kind.endswith("v") else a for kind, a in outputs
        ],
        compiler_params=pltpu.CompilerParams(
            dimension_semantics=("arbitrary",), vmem_limit_bytes=LIMITS.get(name, 16) * 1024 * 1024
        ),
        cost_estimate=pl.CostEstimate(
            flops=int(micros * 1e9), bytes_accessed=size, transcendentals=0
        ),
        name=name,
    )(pos, *[a for _, a in inputs])


def swap(value, axis):
    return lax.ppermute(value, axis, [(0, 1), (1, 0)])


def group_step(value, step):
    return lax.ppermute(value, GROUP, [(at, at ^ step) for at in range(4)])


def gather_pieces(block, beside):
    return (block, beside, swap(block, "row"), swap(beside, "row"))


def in_order(own_first, other, index, axis):
    first = jnp.where(index == 0, own_first, other)
    second = jnp.where(index == 0, other, own_first)
    return jnp.stack([first, second], axis=axis)


def dp_bits():
    count = lax.axis_size("dp")
    return [1 << at for at in range(count.bit_length() - 1)]


def dp_step(value, bit):
    count = lax.axis_size("dp")
    return lax.ppermute(value, "dp", [(at, at ^ bit) for at in range(count)])


def scatter_terms(value):
    count = lax.axis_size("dp")
    rows, columns = value.shape
    return lax.all_to_all(value.reshape(count, rows // count, columns), "dp", 0, 0)


def add_low(*values):
    return sum(value.astype(F32) for value in values).astype(BF16)


def after(value, token):
    return lax.optimization_barrier((value, token))[0]


def double(value, bit):
    here = (lax.axis_index("dp") // bit) % 2
    return in_order(value, dp_step(value, bit), here, value.ndim - 2)


def local(
    block_input, condition, w_ada, b_ada, w_qkv, b_qkv, w_proj, b_proj, w_fc1, b_fc1, w_fc2,
    b_fc2, out_grad,
):
    row = lax.axis_index("row")
    col = lax.axis_index("col")
    pos = jnp.stack([row, col]).astype(jnp.int32)
    latents = condition.shape[0]
    tokens = block_input.shape[1]
    seq = tokens // latents
    steps = latents // 4
    width = tokens // 4
    third = D // GROUPS
    half = FF // GROUPS
    quarter = D // 4
    pack_rows = steps * 8 + BIAS_ROWS

    def shape(dims, kind):
        return jax.ShapeDtypeStruct(dims, kind)

    t_low = shape((D, width), BF16)
    t_wide = shape((D, width), F32)
    t_ff = shape((FF, width), BF16)
    t_piece = shape((quarter, width), BF16)
    pack = ("w", shape((pack_rows, third), F32))

    wq_beside, wp_beside = swap(w_qkv, "col"), swap(w_proj, "col")
    cut1, cut2, cut3, *packs, cond_low, w_ada_by_vector = call(
        modulation_parts, pos, 1, seq,
        [("w", block_input), ("w", condition), ("w", w_ada), ("w", b_ada), ("w", b_qkv),
         ("w", b_proj.reshape(1, -1)), ("w", b_fc2.reshape(1, -1))],
        [("w", t_piece)] * 3 + [pack] * 4 + [("w", shape(condition.shape, BF16)), ("w", shape((6, third, third), BF16))],
        [], 6, "modulation_parts",
    )

    def cut(value, name):
        return call(
            cut_tokens, pos, 1, seq, [("w", value)], [("w", t_piece)] * 3, [], 3, name
        )

    packs, wq_beside, wp_beside, x_cuts = lax.optimization_barrier(
        (packs, wq_beside, wp_beside, (cut1, cut2, cut3))
    )
    x_moved = [group_step(piece, step) for step, piece in zip((1, 2, 3), x_cuts)]
    packs = [packs[0]] + [group_step(packs[step], step) for step in (1, 2, 3)]
    wq = gather_pieces(w_qkv, wq_beside)
    wp = gather_pieces(w_proj, wp_beside)
    out_late, b_fc1 = after((out_grad, b_fc1), x_cuts[0])
    g_cuts = cut(out_late, "cut_grad")
    b_fc1 = b_fc1.reshape(1, -1)
    x_moved, wq, wp, packs, g_cuts, w_fc1, w_fc2, b_fc1 = lax.optimization_barrier(
        (x_moved, wq, wp, packs, g_cuts, w_fc1, w_fc2, b_fc1)
    )
    w1_beside, w2_beside = swap(w_fc1, "col"), swap(w_fc2, "col")
    w1_row, w2_row = swap(w_fc1, "row"), swap(w_fc2, "row")
    b_fc1 = (b_fc1, swap(b_fc1, "col"))
    x, mod_one, qkv, probs, attended, branch, mod = call(
        attention_forward, pos, steps, seq,
        [("o", block_input)] + [("t", a) for a in x_moved]
        + [("w", a) for a in (*wq, *wp, *packs)],
        [("tv", t_low), ("tv", t_low), ("tv", shape((2, 3 * third, width), BF16)),
         ("lv", shape((steps, HEADS, seq, seq), BF16)), ("tv", t_low), ("tv", t_wide),
         ("lv", shape((steps, D, 8), F32))],
        [pltpu.VMEM((D, seq), F32), pltpu.VMEM((2, D, 3 * third), BF16),
         pltpu.VMEM((2, 3 * third, D), BF16), pltpu.VMEM((2, D, third), BF16),
         pltpu.VMEM((2, third, D), BF16), pltpu.VMEM((D, 1), F32), pltpu.VMEM((D, 1), F32),
         pltpu.VMEM((D, 1), F32)],
        16, "attention_forward",
    )

    g_cuts, branch, w1_beside, w2_beside, w1_row, w2_row, b_fc1 = lax.optimization_barrier(
        (g_cuts, branch, w1_beside, w2_beside, w1_row, w2_row, b_fc1)
    )
    w1 = (w_fc1, w1_beside, w1_row, swap(w1_beside, "row"))
    w2 = (w_fc2, w2_beside, w2_row, swap(w2_beside, "row"))
    g_moved = [group_step(piece, step) for step, piece in zip((1, 2, 3), g_cuts)]
    *outs, mod_two, act, slope, mlp = call(
        mlp_forward, pos, steps, seq,
        [("t", x), ("t", branch), ("l", mod)] + [("w", a) for a in w1 + w2]
        + [("w", a) for a in (*packs, *b_fc1)],
        [("t", t_piece)] * 4 + [("tv", t_low), ("tv", t_ff), ("tv", t_ff), ("tv", t_wide)],
        [pltpu.VMEM((2, D, half), BF16), pltpu.VMEM((2, half, D), BF16),
         pltpu.VMEM((2, D, half), BF16), pltpu.VMEM((D, seq), F32), pltpu.VMEM((FF, 1), F32),
         pltpu.VMEM((D, 1), F32)],
        12, "mlp_forward",
    )
    outs, g_moved, mlp = lax.optimization_barrier((outs, g_moved, mlp))
    outs = [outs[0]] + [group_step(outs[step], step) for step in (1, 2, 3)]
    fc_block = (third, 2 * half + third)
    qkv_block = (third, 3 * third)
    blocks = lambda dims: [("w", shape(dims, BF16))] * 4
    hidden_grad, context, mod_grad, send_t, send_m, keep_t, keep_m, sum1, sum2, sump = call(
        mlp_backward, pos, steps, seq,
        [("o", out_grad)] + [("t", a) for a in g_moved]
        + [("t", x), ("t", branch), ("l", mod), ("t", mod_two), ("t", act), ("t", slope),
           ("t", mlp), ("t", attended)]
        + [("w", a) for a in w1 + w2 + wp],
        [("tv", t_wide), ("tv", t_low), ("lv", shape((steps, D, 4), F32))] + blocks(fc_block)
        + [("w", shape((FF, 1), F32)), ("w", shape((D, 1), F32)), ("w", shape((D, 1), F32))],
        [pltpu.VMEM((D, seq), F32), pltpu.VMEM((2, D, half), BF16), pltpu.VMEM((2, D, half), BF16),
         pltpu.VMEM((2, half, D), BF16), pltpu.VMEM((2, D, third), BF16),
         pltpu.VMEM((2, D, half), F32), pltpu.VMEM((2, D, half), F32),
         pltpu.VMEM((2, D, third), F32), pltpu.VMEM((FF, 128), F32),
         pltpu.VMEM((D, 128), F32), pltpu.VMEM((D, 128), F32)],
        20, "mlp_backward",
    )
    outs, send_t = lax.optimization_barrier((outs, send_t))
    theirs = add_low(keep_t, swap(send_t, "row"))
    theirs, context, send_m = lax.optimization_barrier((theirs, context, send_m))
    fc_terms = (keep_m, swap(send_m, "row"), swap(theirs, "col"))

    *ins, send_t, send_m, keep_t, keep_m, back0, back1, back2, back3, block_output = call(
        attention_backward, pos, steps, seq,
        [("t", x), ("t", mod_one), ("l", mod), ("t", qkv), ("l", probs), ("t", context),
         ("t", hidden_grad), ("l", mod_grad), ("w", sum1), ("w", sum2), ("w", sump)]
        + [("w", a) for a in (*wq, *outs)],
        [("t", t_piece)] * 4 + blocks(qkv_block) + [pack] * 4
        + [("j", shape((quarter, tokens), F32))],
        [pltpu.VMEM((2, D, 3 * third), BF16), pltpu.VMEM((2, D, 3 * third), F32),
         pltpu.VMEM((D, 128), F32), pltpu.VMEM((D, 128), F32),
         pltpu.VMEM((2, 3 * third, seq), BF16), pltpu.VMEM((D, seq), F32), pltpu.VMEM((D, 8), F32),
         pltpu.VMEM((third, 8), F32)],
        16, "attention_backward",
    )
    bits = list(reversed(dp_bits()))
    count = lax.axis_size("dp")
    fc_terms, send_t = lax.optimization_barrier((fc_terms, send_t))
    fc_parts = scatter_terms(add_low(*fc_terms))
    theirs = add_low(keep_t, swap(send_t, "row"))
    qkv = add_low(keep_m, swap(send_m, "row"), swap(theirs, "col"))
    backs = [back0] + [group_step(a, step) for step, a in ((1, back1), (2, back2), (3, back3))]
    ins = [ins[0]] + [group_step(ins[step], step) for step in (1, 2, 3)]
    rows = 7 * latents + 2 * BIAS_ROWS
    everyone, cond_part = call(
        group_vectors, pos, 1, seq,
        [("w", a) for a in backs] + [("w", cond_low), ("w", w_ada_by_vector)],
        [("w", shape((rows, third), BF16)), ("w", shape(condition.shape, F32))], [], 2,
        "group_vectors",
    )
    everyone, ins = lax.optimization_barrier((everyone[None], ins))
    for bit in bits[:-2]:
        everyone = jnp.concatenate([everyone, dp_step(everyone, bit)])
    cond_part = cond_part + swap(cond_part, "row")
    fc_parts, qkv, ins, everyone, cond_part = lax.optimization_barrier(
        (fc_parts, qkv, ins, everyone, cond_part)
    )
    qkv_parts = scatter_terms(qkv)
    fc = jnp.sum(fc_parts.astype(F32), axis=0).astype(BF16)
    for bit in bits[:-1]:
        fc = double(fc, bit)
    for bit in bits[-2:-1]:
        everyone = jnp.concatenate([everyone, dp_step(everyone, bit)])
    input_grad = call(
        join_tokens, pos, 4, seq, [("w", a) for a in ins],
        [("j", shape((quarter, tokens), F32))], [], 2, "join_tokens",
    )[0]
    qkv_parts, fc, everyone, input_grad = lax.optimization_barrier(
        (qkv_parts, fc, everyone, input_grad)
    )
    qkv = jnp.sum(qkv_parts.astype(F32), axis=0).astype(BF16)
    qkv = lax.all_to_all(jnp.broadcast_to(qkv[None], (count,) + qkv.shape), "dp", 0, 0)
    for bit in bits[-1:]:
        fc = double(fc, bit)
    for bit in bits[-1:]:
        everyone = jnp.concatenate([everyone, dp_step(everyone, bit)])
    grads_fc = fc.reshape(fc_block).astype(F32)
    grad_w_ada, grad_b_ada, grad_b_fc1, grad_b_qkv, grad_b_proj, grad_b_fc2 = call(
        modulation_grads, pos, 1, seq, [("w", everyone)],
        [("w", shape((third, 6 * third), F32)), ("w", shape((6, quarter), F32)),
         ("w", shape((4, third), F32)), ("w", shape((2, third), F32)),
         ("w", shape((1, quarter), F32)), ("w", shape((1, quarter), F32))], [], 2,
        "modulation_grads",
    )
    grads_qkv = qkv.reshape(qkv_block).astype(F32)
    silu_back = jax.vjp(jax.nn.silu, condition)[1]
    cond_grad = silu_back(cond_part)[0]
    return (
        block_output,
        input_grad,
        cond_grad,
        grad_w_ada,
        grad_b_ada,
        grads_qkv,
        grad_b_qkv,
        grads_fc[:, 2 * half :],
        grad_b_proj.reshape(-1),
        grads_fc[:, :half],
        grad_b_fc1.reshape(-1),
        grads_fc[:, half : 2 * half],
        grad_b_fc2.reshape(-1),
    )


def solution(mesh):
    return jax.shard_map(
        local,
        mesh=mesh,
        in_specs=(
            P(("row", "col"), "dp"),
            P("dp", "col"),
            P("col", "row"),
            P(None, ("row", "col")),
            P("row", "col"),
            P(None, "col"),
            P("col", "row"),
            P(("row", "col")),
            P("row", "col"),
            P("col"),
            P("row", "col"),
            P(("row", "col")),
            P(("row", "col"), "dp"),
        ),
        out_specs=(
            P(("row", "col"), "dp"),
            P(("row", "col"), "dp"),
            P("dp", "col"),
            P("col", "row"),
            P(None, ("row", "col")),
            P("row", "col"),
            P(None, "col"),
            P("col", "row"),
            P(("row", "col")),
            P("row", "col"),
            P("col"),
            P("row", "col"),
            P(("row", "col")),
        ),
        check_vma=False,
    )
```

```python
import jax
import jax.numpy as jnp
from jax import lax
from jax.experimental import pallas as pl
from jax.experimental.pallas import tpu as pltpu
from jax.sharding import PartitionSpec as P

D = 384
HEADS = 6
HD = 64
FF = 1536
GROUPS = 2
EPSILON = 1e-06
BF16 = jnp.bfloat16
F32 = jnp.float32
GROUP = ("row", "col")
LIMITS = {"modulation_parts": 60, "attention_forward": 18, "mlp_forward": 22, "mlp_backward": 30, "attention_backward": 24}
TOGETHER = {"attention_forward": 2, "mlp_forward": 2, "mlp_backward": 2, "attention_backward": 2}


def dot_nn(left, right):
    return lax.dot_general(left, right, (((1,), (0,)), ((), ())), preferred_element_type=F32)


def dot_nt(left, right):
    return lax.dot_general(left, right, (((1,), (1,)), ((), ())), preferred_element_type=F32)


def dot_tn(left, right):
    return lax.dot_general(left, right, (((0,), (0,)), ((), ())), preferred_element_type=F32)


def lane_sum(value):
    return jnp.sum(value, axis=1, keepdims=True)


def lane_fold(value):
    parts = [value[:, at : at + 128] for at in range(0, value.shape[1], 128)]
    return sum(parts[1:], parts[0])


def latent_columns(mod, width):
    seq = width // mod.shape[0]
    return [slice(at * seq, (at + 1) * seq) for at in range(mod.shape[0])]


def spread(mod, vector, width):
    shape = (mod.shape[1], width // mod.shape[0])
    parts = [
        jnp.broadcast_to(mod[at, :, vector : vector + 1], shape) for at in range(mod.shape[0])
    ]
    return parts[0] if len(parts) == 1 else jnp.concatenate(parts, axis=1)


def norm_stats(value):
    center = jnp.sum(value, axis=0, keepdims=True) * (1.0 / D)
    square = jnp.sum(value * value, axis=0, keepdims=True) * (1.0 / D)
    inverse = lax.rsqrt(square - center * center + EPSILON)
    return (value - center) * inverse, inverse


def norm_back(grad, normed, inverse):
    first = jnp.sum(grad, axis=0, keepdims=True) * (1.0 / D)
    second = jnp.sum(grad * normed, axis=0, keepdims=True) * (1.0 / D)
    return inverse * (grad - first - normed * second)


PIECES = ((0, 0), (0, 1), (1, 0), (1, 1))


def place_split(pieces, target, pos):
    row, col = pos[0], pos[1]
    for piece, (step_row, step_col) in zip(pieces, PIECES):
        height = piece.shape[0]
        at = pl.multiple_of((row ^ step_row) * height, height)
        target[col ^ step_col, pl.ds(at, height), :] = piece[...]


def place_proj(pieces, target, pos):
    row, col = pos[0], pos[1]
    for piece, (step_row, step_col) in zip(pieces, PIECES):
        height = piece.shape[0]
        at = pl.multiple_of((col ^ step_col) * height, height)
        target[row ^ step_row, pl.ds(at, height), :] = piece[...]


BIAS_ROWS = 8


def bias_columns(packs, pos, query_s, value_s, proj_s, last_s):
    own, col = pos[0] * 2 + pos[1], pos[1]
    third = D // GROUPS
    quarter = D // 4
    for step, pack in enumerate(packs):
        columns = pack[pack.shape[0] - BIAS_ROWS :, :].T
        if step < 2 and query_s is not None:
            at = pl.multiple_of((col ^ step) * third, third)
            query_s[pl.ds(at, third), :] = columns[:, 0:1]
            value_s[pl.ds(at, third), :] = columns[:, 1:2]
        at = pl.multiple_of((own ^ step) * quarter, quarter)
        if proj_s is not None:
            proj_s[pl.ds(at, quarter), :] = columns[:quarter, 2:3]
        if last_s is not None:
            last_s[pl.ds(at, quarter), :] = columns[:quarter, 3:4]


def cut_tokens(pos, x, out1, out2, out3):
    own = pos[0] * 2 + pos[1]
    width = out1.shape[1]
    for step, out in ((1, out1), (2, out2), (3, out3)):
        at = pl.multiple_of((own ^ step) * width, width)
        out[...] = x[:, pl.ds(at, width)]


def piece_order(latents, steps, own):
    here = lax.broadcasted_iota(jnp.int32, (latents, latents), 0)
    there = lax.broadcasted_iota(jnp.int32, (latents, latents), 1)
    return (there == (own ^ (here // steps)) * steps + here % steps).astype(BF16)


def modulation_parts(
    pos, x, condition, w_ada, b_ada, b_qkv, b_proj, b_fc2,
    out1, out2, out3, pack0, pack1, pack2, pack3, cond_out, w_ada_out,
):
    cut_tokens(pos, x, out1, out2, out3)
    own, col = pos[0] * 2 + pos[1], pos[1]
    latents = condition.shape[0]
    steps = latents // 4
    third = D // GROUPS
    quarter = D // 4
    value = condition[...]
    cond_low = (value * jax.nn.sigmoid(value)).astype(BF16)
    cond_out[...] = cond_low
    ordered = dot_nn(piece_order(latents, steps, own), cond_low).astype(BF16)
    zeros = jnp.zeros((6, quarter), F32)
    bias = b_ada[...].astype(F32)
    bias = jnp.where(
        col == 0, jnp.concatenate([bias, zeros], 1), jnp.concatenate([zeros, bias], 1)
    )
    rows = lax.broadcasted_iota(jnp.int32, (third * 6, third), 0)
    columns = lax.broadcasted_iota(jnp.int32, (third * 6, third), 1)
    packs = (pack0, pack1, pack2, pack3)
    for vector in range(6):
        select = (rows == columns * 6 + vector).astype(BF16)
        weight = dot_nn(w_ada[...], select).astype(BF16)
        w_ada_out[vector] = weight
        part = dot_nn(ordered, weight) + bias[vector : vector + 1]
        for step in range(4):
            for at in range(steps):
                packs[step][at * 8 + vector : at * 8 + vector + 1, :] = part[
                    step * steps + at : step * steps + at + 1
                ]
    for pack in packs:
        at = steps * 8
        pack[at : at + 2, :] = b_qkv[...].astype(F32)
        pack[at + 2 : at + 8, :] = jnp.zeros((6, third), F32)
        pack[at + 2 : at + 3, :quarter] = b_proj[...].astype(F32)
        pack[at + 3 : at + 4, :quarter] = b_fc2[...].astype(F32)
        for latent in range(steps):
            pack[latent * 8 + 6 : latent * 8 + 8, :] = jnp.zeros((2, third), F32)


def join_tokens(pos, x0, x1, x2, x3, out):
    own = pos[0] * 2 + pos[1]
    width = x0.shape[1]
    here = out.shape[1] // width
    for step, piece in enumerate((x0, x1, x2, x3)):

        @pl.when(pl.program_id(0) == step // here)
        def _():
            at = pl.multiple_of(((own ^ step) & (here - 1)) * width, width)
            out[:, pl.ds(at, width)] = piece[...].astype(out.dtype)


def group_vectors(pos, pack0, pack1, pack2, pack3, cond, w_ada, everyone, cond_part):
    own = pos[0] * 2 + pos[1]
    packs = (pack0, pack1, pack2, pack3)
    latents = cond.shape[0]
    steps = latents // 4
    low = jnp.concatenate([pack[: steps * 8, :].astype(BF16) for pack in packs], 0)
    wanted = lax.broadcasted_iota(jnp.int32, (6 * latents, 4 * steps * 8), 0)
    source = lax.broadcasted_iota(jnp.int32, (6 * latents, 4 * steps * 8), 1)
    latent = wanted % latents
    found = ((own ^ (latent // steps)) * steps + latent % steps) * 8 + wanted // latents
    rows = dot_nn((source == found).astype(BF16), low).astype(BF16)
    everyone[: 6 * latents] = rows
    total = None
    for vector in range(6):
        partial = dot_nt(rows[vector * latents : (vector + 1) * latents], w_ada[vector])
        total = partial if total is None else total + partial
    cond_part[...] = total
    sums = sum(pack[steps * 8 :, :] for pack in packs)
    sums = jnp.concatenate([sums, jnp.zeros_like(sums)], 0)
    everyone[6 * latents : 6 * latents + 2 * BIAS_ROWS] = sums.astype(BF16)
    everyone[6 * latents + 2 * BIAS_ROWS :] = cond[...]


def modulation_grads(pos, *refs):
    everyone, (w_out, b_out, fc1_out, qkv_out, proj_out, fc2_out) = refs[:-6], refs[-6:]
    third = D // GROUPS
    quarter = D // 4
    latents = (refs[0].shape[1] - 2 * BIAS_ROWS) // 7

    def rows_of(start, size):
        found = [ref[:, start : start + size, :].reshape(-1, third) for ref in everyone]
        return jnp.concatenate(found, 0)

    rows = lax.broadcasted_iota(jnp.int32, (third, third * 6), 0)
    columns = lax.broadcasted_iota(jnp.int32, (third, third * 6), 1)
    total = None
    for vector in range(6):
        grads = rows_of(vector * latents, latents)
        select = (columns == rows * 6 + vector).astype(BF16)
        partial = dot_nn(grads, select)
        total = partial if total is None else total + partial
        summed = jnp.sum(grads.astype(F32), axis=0, keepdims=True)
        b_out[vector : vector + 1, :] = jnp.where(
            pos[1] == 0, summed[:, :quarter], summed[:, quarter:]
        )
    cond = rows_of(6 * latents + 2 * BIAS_ROWS, latents)
    w_out[...] = dot_tn(cond, total.astype(BF16))
    sums = rows_of(6 * latents, 2 * BIAS_ROWS).astype(F32)
    sums = jnp.sum(sums.reshape(-1, 2 * BIAS_ROWS, third), axis=0)
    qkv_out[...] = sums[0:2]
    proj_out[...] = sums[2:3, :quarter]
    fc2_out[...] = sums[3:4, :quarter]
    fc1_out[...] = sums[4:8]


def place_features(pieces, target, pos):
    own = pos[0] * 2 + pos[1]
    for step, piece in enumerate(pieces):
        height = piece.shape[0]
        at = pl.multiple_of((own ^ step) * height, height)
        target[pl.ds(at, height), :] = piece[...].astype(target.dtype)


def split_features(source, pieces, pos):
    own = pos[0] * 2 + pos[1]
    for step, piece in enumerate(pieces):
        height = piece.shape[0]
        at = pl.multiple_of((own ^ step) * height, height)
        piece[...] = source[pl.ds(at, height), :].astype(piece.dtype)


def attention_forward(
    pos, x0, x1, x2, x3, wq0, wq1, wq2, wq3, wp0, wp1, wp2, wp3, pack0, pack1, pack2, pack3,
    x_out, mod_one_out, qkv_out, probs_out, attended_out, branch_out, mod,
    x_s, wq_s, wq_t, wp_s, wp_t, bias_q, bias_v, bias_p,
):
    @pl.when(pl.program_id(0) == 0)
    def _():
        place_split((wq0, wq1, wq2, wq3), wq_s, pos)
        place_proj((wp0, wp1, wp2, wp3), wp_s, pos)
        bias_columns((pack0, pack1, pack2, pack3), pos, bias_q, bias_v, bias_p, None)
        for part in range(GROUPS):
            wq_t[part] = wq_s[part].T
            wp_t[part] = wp_s[part].T

    third = D // GROUPS
    for first, second, who in ((pack0, pack1, pos[0]), (pack2, pack3, 1 - pos[0])):
        at = pl.multiple_of(who * third, third)
        for latent in range(mod.shape[0]):
            rows = pl.multiple_of((pl.program_id(0) * mod.shape[0] + latent) * 8, 8)
            rows = pl.ds(rows, 8)
            mod[latent, pl.ds(at, third), :] = (first[rows, :] + second[rows, :]).T
    place_features((x0, x1, x2, x3), x_s, pos)
    x = x_s[...]
    x_out[...] = x.astype(BF16)
    normed, _ = norm_stats(x)
    width = x.shape[1]
    columns = latent_columns(mod, width)
    mod_one = (normed * (1.0 + spread(mod, 1, width)) + spread(mod, 0, width)).astype(BF16)
    mod_one_out[...] = mod_one
    per_group = HEADS // GROUPS
    heads = []
    for part in range(GROUPS):
        qkv = dot_nn(wq_t[part], mod_one)
        base = part * third
        query = (qkv[:third] + bias_q[base : base + third]).astype(BF16)
        keys = qkv[third : 2 * third].astype(BF16)
        values = (qkv[2 * third :] + bias_v[base : base + third]).astype(BF16)
        qkv_out[part, :third] = query
        qkv_out[part, third : 2 * third] = keys
        qkv_out[part, 2 * third :] = values
        scaled = query * jnp.asarray(HD ** (-0.5), BF16)
        for head in range(per_group):
            rows = slice(head * HD, (head + 1) * HD)
            for latent, tokens in enumerate(columns):
                place = (latent, part * per_group + head, tokens)
                heads.append((place, keys[rows, tokens], scaled[rows, tokens], values[rows, tokens]))
    scores = [dot_nn(keys.T, query) for _, keys, query, _ in heads]
    probs = []
    for score in scores:
        raised = jnp.exp(score - jnp.max(score, axis=0, keepdims=True))
        total = jnp.sum(raised, axis=0, keepdims=True)
        probs.append((raised * (1.0 / total)).astype(BF16))
    for ((latent, head, tokens), _, _, values), prob in zip(heads, probs):
        probs_out[latent, head] = prob
        attended_out[head * HD : (head + 1) * HD, tokens] = dot_nn(values, prob).astype(BF16)
    attended = attended_out[...]
    for part in range(2):
        rows = slice(part * third, (part + 1) * third)
        branch_out[rows] = dot_nn(wp_t[part], attended) + bias_p[rows]


def mlp_forward(
    pos, x, branch, mod, w10, w11, w12, w13, w20, w21, w22, w23, pack0, pack1, pack2, pack3,
    b10, b11,
    out0, out1, out2, out3, mod_two_out, act_out, slope_out, mlp_out,
    w1_s, w1_t, w2_s, block_s, bias_1, bias_2,
):
    @pl.when(pl.program_id(0) == 0)
    def _():
        bias_columns((pack0, pack1, pack2, pack3), pos, None, None, None, bias_2)
        for step, piece in enumerate((b10, b11)):
            height = piece.shape[1]
            column = jnp.broadcast_to(piece[...].astype(F32), (8, height)).T
            at = pl.multiple_of((pos[1] ^ step) * height, height)
            bias_1[pl.ds(at, height), :] = column[:, 0:1]
        place_split((w10, w11, w12, w13), w1_s, pos)
        place_split((w20, w21, w22, w23), w2_s, pos)
        for part in range(GROUPS):
            w1_t[part] = w1_s[part].T

    width = x.shape[1]
    hidden = x[...].astype(F32) + spread(mod, 2, width) * branch[...]
    normed, _ = norm_stats(hidden)
    mod_two = (normed * (1.0 + spread(mod, 4, width)) + spread(mod, 3, width)).astype(BF16)
    mod_two_out[...] = mod_two
    half = FF // GROUPS
    slope = (2.0 / jnp.pi) ** 0.5
    parts = [slice(part * half, (part + 1) * half) for part in range(GROUPS)]
    pres = [dot_nn(w1_t[part], mod_two) + bias_1[rows] for part, rows in enumerate(parts)]
    acts = []
    for pre, rows in zip(pres, parts):
        square = pre * pre
        tanh = jnp.tanh(pre * (slope + (slope * 0.044715) * square))
        upper = 0.5 + 0.5 * tanh
        acts.append((pre * upper).astype(BF16))
        act_out[rows] = acts[-1]
        slope_out[rows] = (
            upper + pre * (1.0 - tanh * tanh) * (0.5 * slope + (1.5 * slope * 0.044715) * square)
        ).astype(BF16)
    total = dot_nn(w2_s[0], acts[0]) + dot_nn(w2_s[1], acts[1])
    mlp = total + bias_2[...]
    mlp_out[...] = mlp.astype(BF16)
    block_s[...] = hidden + spread(mod, 5, width) * mlp
    split_features(block_s, (out0, out1, out2, out3), pos)


def mlp_backward(
    pos, g0, g1, g2, g3, x, branch, mod, mod_two, act, slope, mlp, attended,
    w10, w11, w12, w13, w20, w21, w22, w23, wp0, wp1, wp2, wp3,
    hidden_grad_out, context_out, mod_grad_out, send_t, send_m, keep_t, keep_m, sum1_out, sum2_out, sump_out,
    g_s, w1_s, w2_s, w2_t, wp_s, acc1, acc2, accp, sum1, sum2, sump,
):
    step = pl.program_id(0)

    @pl.when(step == 0)
    def _():
        place_split((w10, w11, w12, w13), w1_s, pos)
        place_split((w20, w21, w22, w23), w2_s, pos)
        place_proj((wp0, wp1, wp2, wp3), wp_s, pos)
        for part in range(GROUPS):
            w2_t[part] = w2_s[part].T
        for acc in (acc1, acc2, accp, sum1, sum2, sump):
            acc[...] = jnp.zeros_like(acc)

    place_features((g0, g1, g2, g3), g_s, pos)
    grad = g_s[...]
    width = x.shape[1]
    columns = latent_columns(mod, width)
    gate_one = spread(mod, 2, width)
    gate_two = spread(mod, 5, width)

    def latent_sums(vector, value):
        for latent, tokens in enumerate(columns):
            mod_grad_out[latent, :, vector : vector + 1] = lane_sum(value[:, tokens])

    hidden = x[...].astype(F32) + gate_one * branch[...]
    normed, inverse = norm_stats(hidden)
    latent_sums(3, grad * mlp[...])
    mlp_grad = (gate_two * grad).astype(BF16)
    sum2[...] += lane_fold(mlp_grad.astype(F32))
    half = FF // GROUPS
    third = D // GROUPS
    mod_two_low = mod_two[...]
    parts = [slice(part * half, (part + 1) * half) for part in range(GROUPS)]
    act_grads = [dot_nn(w2_t[part], mlp_grad) for part in range(GROUPS)]
    pre_grads = []
    for act_grad, rows in zip(act_grads, parts):
        pre_grads.append((act_grad * slope[rows].astype(F32)).astype(BF16))
        sum1[rows] += lane_fold(pre_grads[-1].astype(F32))
    back = dot_nn(w1_s[0], pre_grads[0]) + dot_nn(w1_s[1], pre_grads[1])
    for part, rows in enumerate(parts):
        acc2[part] += dot_nt(mlp_grad, act[rows])
        acc1[part] += dot_nt(mod_two_low, pre_grads[part])
    latent_sums(1, back)
    latent_sums(2, back * normed)
    hidden_grad = grad + norm_back(back * (1.0 + spread(mod, 4, width)), normed, inverse)
    hidden_grad_out[...] = hidden_grad.astype(BF16)
    latent_sums(0, hidden_grad * branch[...])
    branch_grad = (gate_one * hidden_grad).astype(BF16)
    sump[...] += lane_fold(branch_grad.astype(F32))
    context = None
    for part in range(2):
        rows = slice(part * third, (part + 1) * third)
        accp[part] += dot_nt(attended[...], branch_grad[rows])
        partial = dot_nn(wp_s[part], branch_grad[rows])
        context = partial if context is None else context + partial
    context_out[...] = context.astype(BF16)

    @pl.when(step == pl.num_programs(0) - 1)
    def _():
        mine = pl.multiple_of(pos[0] * third, third)
        other = pl.multiple_of((1 - pos[0]) * third, third)
        for part, pair in ((pos[1], (send_m, keep_m)), (1 - pos[1], (send_t, keep_t))):
            rows = pl.ds(pl.multiple_of(part * third, third), third)
            for out, at, who in ((pair[0], other, 1 - pos[0]), (pair[1], mine, pos[0])):
                out[:, :half] = acc1[part, pl.ds(at, third), :].astype(out.dtype)
                out[:, half : 2 * half] = acc2[part, pl.ds(at, third), :].astype(out.dtype)
                out[:, 2 * half :] = accp[who, rows, :].astype(out.dtype)
        sum1_out[...] = lane_sum(sum1[...])
        sum2_out[...] = lane_sum(sum2[...])
        sump_out[...] = lane_sum(sump[...])


def attention_backward(
    pos, x, mod_one, mod, qkv, probs, context, hidden_grad, mod_grad, sum1, sum2, sump,
    wq0, wq1, wq2, wq3,
    left0, left1, left2, left3,
    out0, out1, out2, out3, send_t, send_m, keep_t, keep_m, pack0, pack1, pack2, pack3, joined,
    wq_s, acc, sumq, sumv, grad_s, block_s, mod_s, bias_s,
):
    step = pl.program_id(0)

    @pl.when(step == 0)
    def _():
        place_split((wq0, wq1, wq2, wq3), wq_s, pos)
        for item in (acc, sumq, sumv):
            item[...] = jnp.zeros_like(item)

    third = D // GROUPS
    scale = HD ** (-0.5)
    mod_one_low = mod_one[...]
    per_group = HEADS // GROUPS
    heads = []
    width = x.shape[1]
    columns = latent_columns(mod, width)
    for head in range(HEADS):
        part, at = head // per_group, head % per_group * HD
        for latent, tokens in enumerate(columns):
            heads.append(
                (
                    (part, at, tokens),
                    qkv[part, at : at + HD, tokens],
                    qkv[part, third + at : third + at + HD, tokens],
                    qkv[part, 2 * third + at : 2 * third + at + HD, tokens],
                    context[head * HD : (head + 1) * HD, tokens],
                    probs[latent, head],
                )
            )
    prob_grads = [dot_nn(values.T, grad) for _, _, _, values, grad, _ in heads]
    score_grads = []
    for prob_grad, (_, _, _, _, _, weight) in zip(prob_grads, heads):
        wide = weight.astype(F32)
        product = wide * prob_grad
        row_dot = jnp.sum(product, axis=0, keepdims=True)
        score_grads.append((product - wide * row_dot).astype(BF16))
    for ((part, at, tokens), query, keys, _, grad, weight), score_grad in zip(heads, score_grads):
        parts = (
            dot_nn(keys, score_grad) * scale,
            dot_nt(query, score_grad) * scale,
            dot_nt(grad, weight),
        )
        for which, value in enumerate(parts):
            start = which * third + at
            grad_s[part, start : start + HD, tokens] = value.astype(BF16)
    back = dot_nn(wq_s[0], grad_s[0]) + dot_nn(wq_s[1], grad_s[1])
    for part in range(GROUPS):
        base = part * third
        qkv_grad = grad_s[part]
        sumq[base : base + third] += lane_fold(qkv_grad[:third].astype(F32))
        sumv[base : base + third] += lane_fold(qkv_grad[2 * third :].astype(F32))
        acc[part] += dot_nt(mod_one_low, qkv_grad)
    normed, inverse = norm_stats(x[...].astype(F32))
    scaled = back * normed
    packs = (pack0, pack1, pack2, pack3)
    mine = pl.multiple_of(pos[0] * third, third)
    other = pl.multiple_of((1 - pos[0]) * third, third)
    for latent, tokens in enumerate(columns):
        mod_s[latent] = jnp.zeros_like(mod_s[latent])
        mod_s[latent, :, 0:1] = lane_sum(back[:, tokens])
        mod_s[latent, :, 1:2] = lane_sum(scaled[:, tokens])
        mod_s[latent, :, 2:6] = mod_grad[latent]
        rows = pl.ds(pl.multiple_of((step * mod.shape[0] + latent) * 8, 8), 8)
        vectors = mod_s[latent, pl.ds(mine, third), :].T
        pack0[rows, :] = vectors
        pack1[rows, :] = vectors
        vectors = mod_s[latent, pl.ds(other, third), :].T
        pack2[rows, :] = vectors
        pack3[rows, :] = vectors
    block_s[...] = hidden_grad[...] + norm_back(
        back * (1.0 + spread(mod, 1, width)), normed, inverse
    )
    split_features(block_s, (out0, out1, out2, out3), pos)
    join_tokens(pos, left0, left1, left2, left3, joined)

    @pl.when(step == pl.num_programs(0) - 1)
    def _():
        for part, send, keep in ((pos[1], send_m, keep_m), (1 - pos[1], send_t, keep_t)):
            send[...] = acc[part, pl.ds(other, third), :].astype(send.dtype)
            keep[...] = acc[part, pl.ds(mine, third), :].astype(keep.dtype)

        own = pos[0] * 2 + pos[1]
        quarter = D // 4
        half = FF // GROUPS
        sumq[:, 0:1] = lane_sum(sumq[...])
        sumv[:, 0:1] = lane_sum(sumv[...])
        for index, pack in enumerate(packs):
            col = pos[1] ^ (index & 1)
            bias_s[...] = jnp.zeros_like(bias_s)
            for part in range(4):
                at = pl.multiple_of(col * half + part * third, third)
                bias_s[:, 4 + part : 5 + part] = sum1[pl.ds(at, third), :]
            at = pl.multiple_of(col * third, third)
            bias_s[:, 0:1] = sumq[pl.ds(at, third), 0:1]
            bias_s[:, 1:2] = sumv[pl.ds(at, third), 0:1]
            at = pl.multiple_of((own ^ index) * quarter, quarter)
            bias_s[:quarter, 2:3] = sump[pl.ds(at, quarter), :]
            bias_s[:quarter, 3:4] = sum2[pl.ds(at, quarter), :]
            pack[pack.shape[0] - BIAS_ROWS :, :] = bias_s[...].T


def call(kernel, pos, steps, seq, inputs, outputs, scratch, micros, name):
    together = TOGETHER.get(name, 1)
    steps, seq = steps // together, seq * together

    def spec(kind, shape):
        kind = kind[0]
        rank = len(shape)
        if kind == "t":
            lead = (0,) * (rank - 1)
            return pl.BlockSpec(shape[:-1] + (seq,), lambda i, p: lead + (i,))
        if kind == "o":
            return pl.BlockSpec(
                shape[:-1] + (seq,), lambda i, p: (0, (p[0] * 2 + p[1]) * steps + i)
            )
        if kind == "j":
            return pl.BlockSpec(
                shape[:-1] + (shape[-1] // 4 * together,),
                lambda i, p: (0, (p[0] * 2 + p[1]) // together ^ i),
            )
        if kind == "l":
            tail = (0,) * (rank - 1)
            return pl.BlockSpec((together,) + shape[1:], lambda i, p: (i,) + tail)
        zeros = (0,) * rank
        if steps > 1:
            return pl.BlockSpec(shape, lambda i, p: zeros, pipeline_mode=pl.Buffered(1))
        return pl.BlockSpec(shape, lambda i, p: zeros)

    size = sum(a.size * a.dtype.itemsize for _, a in inputs)
    size += sum(a.size * jnp.dtype(a.dtype).itemsize for _, a in outputs)
    return pl.pallas_call(
        kernel,
        grid_spec=pltpu.PrefetchScalarGridSpec(
            num_scalar_prefetch=1,
            grid=(steps,),
            in_specs=[spec(kind, a.shape) for kind, a in inputs],
            out_specs=[spec(kind, a.shape) for kind, a in outputs],
            scratch_shapes=scratch,
        ),
        out_shape=[
            pltpu.VMEM(a.shape, a.dtype) if kind.endswith("v") else a for kind, a in outputs
        ],
        compiler_params=pltpu.CompilerParams(
            dimension_semantics=("arbitrary",), vmem_limit_bytes=LIMITS.get(name, 16) * 1024 * 1024
        ),
        cost_estimate=pl.CostEstimate(
            flops=int(micros * 1e9), bytes_accessed=size, transcendentals=0
        ),
        name=name,
    )(pos, *[a for _, a in inputs])


def swap(value, axis):
    return lax.ppermute(value, axis, [(0, 1), (1, 0)])


def group_step(value, step):
    return lax.ppermute(value, GROUP, [(at, at ^ step) for at in range(4)])


def gather_pieces(block, beside):
    return (block, beside, swap(block, "row"), swap(beside, "row"))


def in_order(own_first, other, index, axis):
    first = jnp.where(index == 0, own_first, other)
    second = jnp.where(index == 0, other, own_first)
    return jnp.stack([first, second], axis=axis)


def dp_bits():
    count = lax.axis_size("dp")
    return [1 << at for at in range(count.bit_length() - 1)]


def dp_step(value, bit):
    count = lax.axis_size("dp")
    return lax.ppermute(value, "dp", [(at, at ^ bit) for at in range(count)])


def scatter_terms(value):
    count = lax.axis_size("dp")
    rows, columns = value.shape
    return lax.all_to_all(value.reshape(count, rows // count, columns), "dp", 0, 0)


def add_low(*values):
    return sum(value.astype(F32) for value in values).astype(BF16)


def after(value, token):
    return lax.optimization_barrier((value, token))[0]


def double(value, bit):
    here = (lax.axis_index("dp") // bit) % 2
    return in_order(value, dp_step(value, bit), here, value.ndim - 2)


def local(
    block_input, condition, w_ada, b_ada, w_qkv, b_qkv, w_proj, b_proj, w_fc1, b_fc1, w_fc2,
    b_fc2, out_grad,
):
    row = lax.axis_index("row")
    col = lax.axis_index("col")
    pos = jnp.stack([row, col]).astype(jnp.int32)
    latents = condition.shape[0]
    tokens = block_input.shape[1]
    seq = tokens // latents
    steps = latents // 4
    width = tokens // 4
    third = D // GROUPS
    half = FF // GROUPS
    quarter = D // 4
    pack_rows = steps * 8 + BIAS_ROWS

    def shape(dims, kind):
        return jax.ShapeDtypeStruct(dims, kind)

    t_low = shape((D, width), BF16)
    t_wide = shape((D, width), F32)
    t_ff = shape((FF, width), BF16)
    t_piece = shape((quarter, width), BF16)
    pack = ("w", shape((pack_rows, third), F32))

    wq_beside, wp_beside = swap(w_qkv, "col"), swap(w_proj, "col")
    cut1, cut2, cut3, *packs, cond_low, w_ada_by_vector = call(
        modulation_parts, pos, 1, seq,
        [("w", block_input), ("w", condition), ("w", w_ada), ("w", b_ada), ("w", b_qkv),
         ("w", b_proj.reshape(1, -1)), ("w", b_fc2.reshape(1, -1))],
        [("w", t_piece)] * 3 + [pack] * 4 + [("w", shape(condition.shape, BF16)), ("w", shape((6, third, third), BF16))],
        [], 6, "modulation_parts",
    )

    def cut(value, name):
        return call(
            cut_tokens, pos, 1, seq, [("w", value)], [("w", t_piece)] * 3, [], 3, name
        )

    packs, wq_beside, wp_beside, x_cuts = lax.optimization_barrier(
        (packs, wq_beside, wp_beside, (cut1, cut2, cut3))
    )
    x_moved = [group_step(piece, step) for step, piece in zip((1, 2, 3), x_cuts)]
    packs = [packs[0]] + [group_step(packs[step], step) for step in (1, 2, 3)]
    wq = gather_pieces(w_qkv, wq_beside)
    wp = gather_pieces(w_proj, wp_beside)
    out_late, b_fc1 = after((out_grad, b_fc1), x_cuts[0])
    g_cuts = cut(out_late, "cut_grad")
    b_fc1 = b_fc1.reshape(1, -1)
    x_moved, wq, wp, packs, g_cuts, w_fc1, w_fc2, b_fc1 = lax.optimization_barrier(
        (x_moved, wq, wp, packs, g_cuts, w_fc1, w_fc2, b_fc1)
    )
    w1_beside, w2_beside = swap(w_fc1, "col"), swap(w_fc2, "col")
    w1_row, w2_row = swap(w_fc1, "row"), swap(w_fc2, "row")
    b_fc1 = (b_fc1, swap(b_fc1, "col"))
    x, mod_one, qkv, probs, attended, branch, mod = call(
        attention_forward, pos, steps, seq,
        [("o", block_input)] + [("t", a) for a in x_moved]
        + [("w", a) for a in (*wq, *wp, *packs)],
        [("tv", t_low), ("tv", t_low), ("tv", shape((2, 3 * third, width), BF16)),
         ("lv", shape((steps, HEADS, seq, seq), BF16)), ("tv", t_low), ("tv", t_wide),
         ("lv", shape((steps, D, 8), F32))],
        [pltpu.VMEM((D, seq * TOGETHER.get("attention_forward", 1)), F32),
         pltpu.VMEM((2, D, 3 * third), BF16), pltpu.VMEM((2, 3 * third, D), BF16), pltpu.VMEM((2, D, third), BF16),
         pltpu.VMEM((2, third, D), BF16), pltpu.VMEM((D, 1), F32), pltpu.VMEM((D, 1), F32),
         pltpu.VMEM((D, 1), F32)],
        16, "attention_forward",
    )

    g_cuts, branch, w1_beside, w2_beside, w1_row, w2_row, b_fc1 = lax.optimization_barrier(
        (g_cuts, branch, w1_beside, w2_beside, w1_row, w2_row, b_fc1)
    )
    w1 = (w_fc1, w1_beside, w1_row, swap(w1_beside, "row"))
    w2 = (w_fc2, w2_beside, w2_row, swap(w2_beside, "row"))
    g_moved = [group_step(piece, step) for step, piece in zip((1, 2, 3), g_cuts)]
    *outs, mod_two, act, slope, mlp = call(
        mlp_forward, pos, steps, seq,
        [("t", x), ("t", branch), ("l", mod)] + [("w", a) for a in w1 + w2]
        + [("w", a) for a in (*packs, *b_fc1)],
        [("t", t_piece)] * 4 + [("tv", t_low), ("tv", t_ff), ("tv", t_ff), ("tv", t_low)],
        [pltpu.VMEM((2, D, half), BF16), pltpu.VMEM((2, half, D), BF16),
         pltpu.VMEM((2, D, half), BF16),
         pltpu.VMEM((D, seq * TOGETHER.get("mlp_forward", 1)), F32), pltpu.VMEM((FF, 1), F32),
         pltpu.VMEM((D, 1), F32)],
        12, "mlp_forward",
    )
    outs, g_moved, mlp = lax.optimization_barrier((outs, g_moved, mlp))
    outs = [outs[0]] + [group_step(outs[step], step) for step in (1, 2, 3)]
    fc_block = (third, 2 * half + third)
    qkv_block = (third, 3 * third)
    blocks = lambda dims: [("w", shape(dims, BF16))] * 4
    hidden_grad, context, mod_grad, send_t, send_m, keep_t, keep_m, sum1, sum2, sump = call(
        mlp_backward, pos, steps, seq,
        [("o", out_grad)] + [("t", a) for a in g_moved]
        + [("t", x), ("t", branch), ("l", mod), ("t", mod_two), ("t", act), ("t", slope),
           ("t", mlp), ("t", attended)]
        + [("w", a) for a in w1 + w2 + wp],
        [("tv", t_low), ("tv", t_low), ("lv", shape((steps, D, 4), F32))] + blocks(fc_block)
        + [("w", shape((FF, 1), F32)), ("w", shape((D, 1), F32)), ("w", shape((D, 1), F32))],
        [pltpu.VMEM((D, seq * TOGETHER.get("mlp_backward", 1)), F32),
         pltpu.VMEM((2, D, half), BF16), pltpu.VMEM((2, D, half), BF16),
         pltpu.VMEM((2, half, D), BF16), pltpu.VMEM((2, D, third), BF16),
         pltpu.VMEM((2, D, half), F32), pltpu.VMEM((2, D, half), F32),
         pltpu.VMEM((2, D, third), F32), pltpu.VMEM((FF, 128), F32),
         pltpu.VMEM((D, 128), F32), pltpu.VMEM((D, 128), F32)],
        20, "mlp_backward",
    )
    outs, send_t = lax.optimization_barrier((outs, send_t))
    theirs = add_low(keep_t, swap(send_t, "row"))
    theirs, context, send_m = lax.optimization_barrier((theirs, context, send_m))
    fc_terms = (keep_m, swap(send_m, "row"), swap(theirs, "col"))

    *ins, send_t, send_m, keep_t, keep_m, back0, back1, back2, back3, block_output = call(
        attention_backward, pos, steps, seq,
        [("t", x), ("t", mod_one), ("l", mod), ("t", qkv), ("l", probs), ("t", context),
         ("t", hidden_grad), ("l", mod_grad), ("w", sum1), ("w", sum2), ("w", sump)]
        + [("w", a) for a in (*wq, *outs)],
        [("t", t_piece)] * 4 + blocks(qkv_block) + [pack] * 4
        + [("j", shape((quarter, tokens), F32))],
        [pltpu.VMEM((2, D, 3 * third), BF16), pltpu.VMEM((2, D, 3 * third), F32),
         pltpu.VMEM((D, 128), F32), pltpu.VMEM((D, 128), F32),
         pltpu.VMEM((2, 3 * third, seq * TOGETHER.get("attention_backward", 1)), BF16),
         pltpu.VMEM((D, seq * TOGETHER.get("attention_backward", 1)), F32),
         pltpu.VMEM((TOGETHER.get("attention_backward", 1), D, 8), F32),
         pltpu.VMEM((third, 8), F32)],
        16, "attention_backward",
    )
    bits = list(reversed(dp_bits()))
    count = lax.axis_size("dp")
    fc_terms, send_t = lax.optimization_barrier((fc_terms, send_t))
    fc_parts = scatter_terms(add_low(*fc_terms))
    theirs = add_low(keep_t, swap(send_t, "row"))
    qkv = add_low(keep_m, swap(send_m, "row"), swap(theirs, "col"))
    backs = [back0] + [group_step(a, step) for step, a in ((1, back1), (2, back2), (3, back3))]
    ins = [ins[0]] + [group_step(ins[step], step) for step in (1, 2, 3)]
    rows = 7 * latents + 2 * BIAS_ROWS
    everyone, cond_part = call(
        group_vectors, pos, 1, seq,
        [("w", a) for a in backs] + [("w", cond_low), ("w", w_ada_by_vector)],
        [("w", shape((rows, third), BF16)), ("w", shape(condition.shape, F32))], [], 2,
        "group_vectors",
    )
    everyone, ins = lax.optimization_barrier((everyone[None], ins))
    for bit in bits[:-2]:
        everyone = jnp.concatenate([everyone, dp_step(everyone, bit)])
    cond_part = cond_part + swap(cond_part, "row")
    fc_parts, qkv, ins, everyone, cond_part = lax.optimization_barrier(
        (fc_parts, qkv, ins, everyone, cond_part)
    )
    qkv_parts = scatter_terms(qkv)
    fc = jnp.sum(fc_parts.astype(F32), axis=0).astype(BF16)
    for bit in bits[:-1]:
        fc = double(fc, bit)
    for bit in bits[-2:-1]:
        everyone = jnp.concatenate([everyone, dp_step(everyone, bit)])
    input_grad = call(
        join_tokens, pos, 4, seq, [("w", a) for a in ins],
        [("j", shape((quarter, tokens), F32))], [], 2, "join_tokens",
    )[0]
    qkv_parts, fc, everyone, input_grad = lax.optimization_barrier(
        (qkv_parts, fc, everyone, input_grad)
    )
    qkv = jnp.sum(qkv_parts.astype(F32), axis=0).astype(BF16)
    qkv = lax.all_to_all(jnp.broadcast_to(qkv[None], (count,) + qkv.shape), "dp", 0, 0)
    for bit in bits[-1:]:
        fc = double(fc, bit)
    for bit in bits[-1:]:
        everyone = jnp.concatenate([everyone, dp_step(everyone, bit)])
    grads_fc = fc.reshape(fc_block).astype(F32)
    grad_w_ada, grad_b_ada, grad_b_fc1, grad_b_qkv, grad_b_proj, grad_b_fc2 = call(
        modulation_grads, pos, 1, seq, [("w", everyone)],
        [("w", shape((third, 6 * third), F32)), ("w", shape((6, quarter), F32)),
         ("w", shape((4, third), F32)), ("w", shape((2, third), F32)),
         ("w", shape((1, quarter), F32)), ("w", shape((1, quarter), F32))], [], 2,
        "modulation_grads",
    )
    grads_qkv = qkv.reshape(qkv_block).astype(F32)
    silu_back = jax.vjp(jax.nn.silu, condition)[1]
    cond_grad = silu_back(cond_part)[0]
    return (
        block_output,
        input_grad,
        cond_grad,
        grad_w_ada,
        grad_b_ada,
        grads_qkv,
        grad_b_qkv,
        grads_fc[:, 2 * half :],
        grad_b_proj.reshape(-1),
        grads_fc[:, :half],
        grad_b_fc1.reshape(-1),
        grads_fc[:, half : 2 * half],
        grad_b_fc2.reshape(-1),
    )


def solution(mesh):
    return jax.shard_map(
        local,
        mesh=mesh,
        in_specs=(
            P(("row", "col"), "dp"),
            P("dp", "col"),
            P("col", "row"),
            P(None, ("row", "col")),
            P("row", "col"),
            P(None, "col"),
            P("col", "row"),
            P(("row", "col")),
            P("row", "col"),
            P("col"),
            P("row", "col"),
            P(("row", "col")),
            P(("row", "col"), "dp"),
        ),
        out_specs=(
            P(("row", "col"), "dp"),
            P(("row", "col"), "dp"),
            P("dp", "col"),
            P("col", "row"),
            P(None, ("row", "col")),
            P("row", "col"),
            P(None, "col"),
            P("col", "row"),
            P(("row", "col")),
            P("row", "col"),
            P("col"),
            P("row", "col"),
            P(("row", "col")),
        ),
        check_vma=False,
    )
```

```python
import jax
import jax.numpy as jnp
from jax import lax
from jax.experimental import pallas as pl
from jax.experimental.pallas import tpu as pltpu
from jax.sharding import PartitionSpec as P

D = 384
HEADS = 6
HD = 64
FF = 1536
GROUPS = 2
EPSILON = 1e-06
BF16 = jnp.bfloat16
F32 = jnp.float32
GROUP = ("row", "col")
LIMITS = {"modulation_parts": 60, "attention_forward": 18, "mlp_forward": 22, "mlp_backward": 30, "attention_backward": 24}
TOGETHER = {"attention_forward": 2, "mlp_forward": 2, "mlp_backward": 2, "attention_backward": 2}


def dot_nn(left, right):
    return lax.dot_general(left, right, (((1,), (0,)), ((), ())), preferred_element_type=F32)


def dot_nt(left, right):
    return lax.dot_general(left, right, (((1,), (1,)), ((), ())), preferred_element_type=F32)


def dot_tn(left, right):
    return lax.dot_general(left, right, (((0,), (0,)), ((), ())), preferred_element_type=F32)


def lane_sum(value):
    return jnp.sum(value, axis=1, keepdims=True)


def lane_fold(value):
    parts = [value[:, at : at + 128] for at in range(0, value.shape[1], 128)]
    return sum(parts[1:], parts[0])


def latent_columns(mod, width):
    seq = width // mod.shape[0]
    return [slice(at * seq, (at + 1) * seq) for at in range(mod.shape[0])]


def spread(mod, vector, width):
    shape = (mod.shape[1], width // mod.shape[0])
    parts = [
        jnp.broadcast_to(mod[at, :, vector : vector + 1], shape) for at in range(mod.shape[0])
    ]
    return parts[0] if len(parts) == 1 else jnp.concatenate(parts, axis=1)


def norm_stats(value):
    center = jnp.sum(value, axis=0, keepdims=True) * (1.0 / D)
    square = jnp.sum(value * value, axis=0, keepdims=True) * (1.0 / D)
    inverse = lax.rsqrt(square - center * center + EPSILON)
    return (value - center) * inverse, inverse


def norm_back(grad, normed, inverse):
    first = jnp.sum(grad, axis=0, keepdims=True) * (1.0 / D)
    second = jnp.sum(grad * normed, axis=0, keepdims=True) * (1.0 / D)
    return inverse * (grad - first - normed * second)


PIECES = ((0, 0), (0, 1), (1, 0), (1, 1))


def place_split(pieces, target, pos):
    row, col = pos[0], pos[1]
    for piece, (step_row, step_col) in zip(pieces, PIECES):
        height = piece.shape[0]
        at = pl.multiple_of((row ^ step_row) * height, height)
        target[col ^ step_col, pl.ds(at, height), :] = piece[...]


def place_proj(pieces, target, pos):
    row, col = pos[0], pos[1]
    for piece, (step_row, step_col) in zip(pieces, PIECES):
        height = piece.shape[0]
        at = pl.multiple_of((col ^ step_col) * height, height)
        target[row ^ step_row, pl.ds(at, height), :] = piece[...]


BIAS_ROWS = 8


def bias_columns(packs, pos, query_s, value_s, proj_s, last_s):
    own, col = pos[0] * 2 + pos[1], pos[1]
    third = D // GROUPS
    quarter = D // 4
    for step, pack in enumerate(packs):
        columns = pack[pack.shape[0] - BIAS_ROWS :, :].T
        if step < 2 and query_s is not None:
            at = pl.multiple_of((col ^ step) * third, third)
            query_s[pl.ds(at, third), :] = columns[:, 0:1]
            value_s[pl.ds(at, third), :] = columns[:, 1:2]
        at = pl.multiple_of((own ^ step) * quarter, quarter)
        if proj_s is not None:
            proj_s[pl.ds(at, quarter), :] = columns[:quarter, 2:3]
        if last_s is not None:
            last_s[pl.ds(at, quarter), :] = columns[:quarter, 3:4]


def cut_tokens(pos, x, out1, out2, out3):
    own = pos[0] * 2 + pos[1]
    width = out1.shape[1]
    for step, out in ((1, out1), (2, out2), (3, out3)):
        at = pl.multiple_of((own ^ step) * width, width)
        out[...] = x[:, pl.ds(at, width)]


def piece_order(latents, steps, own):
    here = lax.broadcasted_iota(jnp.int32, (latents, latents), 0)
    there = lax.broadcasted_iota(jnp.int32, (latents, latents), 1)
    return (there == (own ^ (here // steps)) * steps + here % steps).astype(BF16)


def modulation_parts(
    pos, x, condition, w_ada, b_ada, b_qkv, b_proj, b_fc2,
    out1, out2, out3, pack0, pack1, pack2, pack3, cond_out, w_ada_out,
):
    cut_tokens(pos, x, out1, out2, out3)
    own, col = pos[0] * 2 + pos[1], pos[1]
    latents = condition.shape[0]
    steps = latents // 4
    third = D // GROUPS
    quarter = D // 4
    value = condition[...]
    cond_low = (value * jax.nn.sigmoid(value)).astype(BF16)
    cond_out[...] = cond_low
    ordered = dot_nn(piece_order(latents, steps, own), cond_low).astype(BF16)
    zeros = jnp.zeros((6, quarter), F32)
    bias = b_ada[...].astype(F32)
    bias = jnp.where(
        col == 0, jnp.concatenate([bias, zeros], 1), jnp.concatenate([zeros, bias], 1)
    )
    rows = lax.broadcasted_iota(jnp.int32, (third * 6, third), 0)
    columns = lax.broadcasted_iota(jnp.int32, (third * 6, third), 1)
    packs = (pack0, pack1, pack2, pack3)
    for vector in range(6):
        select = (rows == columns * 6 + vector).astype(BF16)
        weight = dot_nn(w_ada[...], select).astype(BF16)
        w_ada_out[vector] = weight
        part = dot_nn(ordered, weight) + bias[vector : vector + 1]
        for step in range(4):
            for at in range(steps):
                packs[step][at * 8 + vector : at * 8 + vector + 1, :] = part[
                    step * steps + at : step * steps + at + 1
                ]
    for pack in packs:
        at = steps * 8
        pack[at : at + 2, :] = b_qkv[...].astype(F32)
        pack[at + 2 : at + 8, :] = jnp.zeros((6, third), F32)
        pack[at + 2 : at + 3, :quarter] = b_proj[...].astype(F32)
        pack[at + 3 : at + 4, :quarter] = b_fc2[...].astype(F32)
        for latent in range(steps):
            pack[latent * 8 + 6 : latent * 8 + 8, :] = jnp.zeros((2, third), F32)


def join_tokens(pos, x0, x1, x2, x3, out):
    own = pos[0] * 2 + pos[1]
    width = x0.shape[1]
    here = out.shape[1] // width
    for step, piece in enumerate((x0, x1, x2, x3)):

        @pl.when(pl.program_id(0) == step // here)
        def _():
            at = pl.multiple_of(((own ^ step) & (here - 1)) * width, width)
            out[:, pl.ds(at, width)] = piece[...].astype(out.dtype)


def group_vectors(pos, pack0, pack1, pack2, pack3, cond, w_ada, everyone, cond_part):
    own = pos[0] * 2 + pos[1]
    packs = (pack0, pack1, pack2, pack3)
    latents = cond.shape[0]
    steps = latents // 4
    low = jnp.concatenate([pack[: steps * 8, :].astype(BF16) for pack in packs], 0)
    wanted = lax.broadcasted_iota(jnp.int32, (6 * latents, 4 * steps * 8), 0)
    source = lax.broadcasted_iota(jnp.int32, (6 * latents, 4 * steps * 8), 1)
    latent = wanted % latents
    found = ((own ^ (latent // steps)) * steps + latent % steps) * 8 + wanted // latents
    rows = dot_nn((source == found).astype(BF16), low).astype(BF16)
    everyone[: 6 * latents] = rows
    total = None
    for vector in range(6):
        partial = dot_nt(rows[vector * latents : (vector + 1) * latents], w_ada[vector])
        total = partial if total is None else total + partial
    cond_part[...] = total
    sums = sum(pack[steps * 8 :, :] for pack in packs)
    sums = jnp.concatenate([sums, jnp.zeros_like(sums)], 0)
    everyone[6 * latents : 6 * latents + 2 * BIAS_ROWS] = sums.astype(BF16)
    everyone[6 * latents + 2 * BIAS_ROWS :] = cond[...]


def modulation_grads(pos, *refs):
    everyone, (w_out, b_out, fc1_out, qkv_out, proj_out, fc2_out) = refs[:-6], refs[-6:]
    third = D // GROUPS
    quarter = D // 4
    latents = (refs[0].shape[1] - 2 * BIAS_ROWS) // 7

    def rows_of(start, size):
        found = [ref[:, start : start + size, :].reshape(-1, third) for ref in everyone]
        return jnp.concatenate(found, 0)

    rows = lax.broadcasted_iota(jnp.int32, (third, third * 6), 0)
    columns = lax.broadcasted_iota(jnp.int32, (third, third * 6), 1)
    total = None
    for vector in range(6):
        grads = rows_of(vector * latents, latents)
        select = (columns == rows * 6 + vector).astype(BF16)
        partial = dot_nn(grads, select)
        total = partial if total is None else total + partial
        summed = jnp.sum(grads.astype(F32), axis=0, keepdims=True)
        b_out[vector : vector + 1, :] = jnp.where(
            pos[1] == 0, summed[:, :quarter], summed[:, quarter:]
        )
    cond = rows_of(6 * latents + 2 * BIAS_ROWS, latents)
    w_out[...] = dot_tn(cond, total.astype(BF16))
    sums = rows_of(6 * latents, 2 * BIAS_ROWS).astype(F32)
    sums = jnp.sum(sums.reshape(-1, 2 * BIAS_ROWS, third), axis=0)
    qkv_out[...] = sums[0:2]
    proj_out[...] = sums[2:3, :quarter]
    fc2_out[...] = sums[3:4, :quarter]
    fc1_out[...] = sums[4:8]


def place_features(pieces, target, pos):
    own = pos[0] * 2 + pos[1]
    for step, piece in enumerate(pieces):
        height = piece.shape[0]
        at = pl.multiple_of((own ^ step) * height, height)
        target[pl.ds(at, height), :] = piece[...].astype(target.dtype)


def split_features(source, pieces, pos):
    own = pos[0] * 2 + pos[1]
    for step, piece in enumerate(pieces):
        height = piece.shape[0]
        at = pl.multiple_of((own ^ step) * height, height)
        piece[...] = source[pl.ds(at, height), :].astype(piece.dtype)


def attention_forward(
    pos, x0, x1, x2, x3, wq0, wq1, wq2, wq3, wp0, wp1, wp2, wp3, pack0, pack1, pack2, pack3,
    x_out, mod_one_out, qkv_out, probs_out, attended_out, branch_out, mod,
    x_s, wq_s, wq_t, wp_s, wp_t, bias_q, bias_v, bias_p,
):
    @pl.when(pl.program_id(0) == 0)
    def _():
        place_split((wq0, wq1, wq2, wq3), wq_s, pos)
        place_proj((wp0, wp1, wp2, wp3), wp_s, pos)
        bias_columns((pack0, pack1, pack2, pack3), pos, bias_q, bias_v, bias_p, None)
        for part in range(GROUPS):
            wq_t[part] = wq_s[part].T
            wp_t[part] = wp_s[part].T

    third = D // GROUPS
    for first, second, who in ((pack0, pack1, pos[0]), (pack2, pack3, 1 - pos[0])):
        at = pl.multiple_of(who * third, third)
        for latent in range(mod.shape[0]):
            rows = pl.multiple_of((pl.program_id(0) * mod.shape[0] + latent) * 8, 8)
            rows = pl.ds(rows, 8)
            mod[latent, pl.ds(at, third), :] = (first[rows, :] + second[rows, :]).T
    place_features((x0, x1, x2, x3), x_s, pos)
    x = x_s[...]
    x_out[...] = x.astype(BF16)
    normed, _ = norm_stats(x)
    width = x.shape[1]
    columns = latent_columns(mod, width)
    mod_one = (normed * (1.0 + spread(mod, 1, width)) + spread(mod, 0, width)).astype(BF16)
    mod_one_out[...] = mod_one
    per_group = HEADS // GROUPS
    heads = []
    for part in range(GROUPS):
        qkv = dot_nn(wq_t[part], mod_one)
        base = part * third
        query = (qkv[:third] + bias_q[base : base + third]).astype(BF16)
        keys = qkv[third : 2 * third].astype(BF16)
        values = (qkv[2 * third :] + bias_v[base : base + third]).astype(BF16)
        qkv_out[part, :third] = query
        qkv_out[part, third : 2 * third] = keys
        qkv_out[part, 2 * third :] = values
        scaled = query * jnp.asarray(HD ** (-0.5), BF16)
        for head in range(per_group):
            rows = slice(head * HD, (head + 1) * HD)
            for latent, tokens in enumerate(columns):
                place = (latent, part * per_group + head, tokens)
                heads.append((place, keys[rows, tokens], scaled[rows, tokens], values[rows, tokens]))
    scores = [dot_nn(keys.T, query) for _, keys, query, _ in heads]
    probs = []
    for score in scores:
        raised = jnp.exp(score - jnp.max(score, axis=0, keepdims=True))
        total = jnp.sum(raised, axis=0, keepdims=True)
        probs.append((raised * (1.0 / total)).astype(BF16))
    for ((latent, head, tokens), _, _, values), prob in zip(heads, probs):
        probs_out[latent, head] = prob
        attended_out[head * HD : (head + 1) * HD, tokens] = dot_nn(values, prob).astype(BF16)
    attended = attended_out[...]
    for part in range(2):
        rows = slice(part * third, (part + 1) * third)
        branch_out[rows] = dot_nn(wp_t[part], attended) + bias_p[rows]


def mlp_forward(
    pos, x, branch, mod, w10, w11, w12, w13, w20, w21, w22, w23, pack0, pack1, pack2, pack3,
    b10, b11,
    out0, out1, out2, out3, mod_two_out, act_out, slope_out, mlp_out,
    w1_s, w1_t, w2_s, block_s, bias_1, bias_2,
):
    @pl.when(pl.program_id(0) == 0)
    def _():
        bias_columns((pack0, pack1, pack2, pack3), pos, None, None, None, bias_2)
        for step, piece in enumerate((b10, b11)):
            height = piece.shape[1]
            column = jnp.broadcast_to(piece[...].astype(F32), (8, height)).T
            at = pl.multiple_of((pos[1] ^ step) * height, height)
            bias_1[pl.ds(at, height), :] = column[:, 0:1]
        place_split((w10, w11, w12, w13), w1_s, pos)
        place_split((w20, w21, w22, w23), w2_s, pos)
        for part in range(GROUPS):
            w1_t[part] = w1_s[part].T

    width = x.shape[1]
    hidden = x[...].astype(F32) + spread(mod, 2, width) * branch[...]
    normed, _ = norm_stats(hidden)
    mod_two = (normed * (1.0 + spread(mod, 4, width)) + spread(mod, 3, width)).astype(BF16)
    mod_two_out[...] = mod_two
    half = FF // GROUPS
    slope = (2.0 / jnp.pi) ** 0.5
    parts = [slice(part * half, (part + 1) * half) for part in range(GROUPS)]
    pres = [dot_nn(w1_t[part], mod_two) + bias_1[rows] for part, rows in enumerate(parts)]
    acts = []
    for pre, rows in zip(pres, parts):
        square = pre * pre
        tanh = jnp.tanh(pre * (slope + (slope * 0.044715) * square))
        upper = 0.5 + 0.5 * tanh
        acts.append((pre * upper).astype(BF16))
        act_out[rows] = acts[-1]
        slope_out[rows] = (
            upper + pre * (1.0 - tanh * tanh) * (0.5 * slope + (1.5 * slope * 0.044715) * square)
        ).astype(BF16)
    total = dot_nn(w2_s[0], acts[0]) + dot_nn(w2_s[1], acts[1])
    mlp = total + bias_2[...]
    mlp_out[...] = mlp.astype(BF16)
    block_s[...] = hidden + spread(mod, 5, width) * mlp
    split_features(block_s, (out0, out1, out2, out3), pos)


def mlp_backward(
    pos, g0, g1, g2, g3, x, branch, mod, mod_two, act, slope, mlp, attended,
    w10, w11, w12, w13, w20, w21, w22, w23, wp0, wp1, wp2, wp3,
    hidden_grad_out, context_out, mod_grad_out, send_t, send_m, keep_t, keep_m, sum1_out, sum2_out, sump_out,
    g_s, w1_s, w2_s, w2_t, wp_s, acc1, acc2, accp, sum1, sum2, sump,
):
    step = pl.program_id(0)

    @pl.when(step == 0)
    def _():
        place_split((w10, w11, w12, w13), w1_s, pos)
        place_split((w20, w21, w22, w23), w2_s, pos)
        place_proj((wp0, wp1, wp2, wp3), wp_s, pos)
        for part in range(GROUPS):
            w2_t[part] = w2_s[part].T
        for acc in (acc1, acc2, accp, sum1, sum2, sump):
            acc[...] = jnp.zeros_like(acc)

    place_features((g0, g1, g2, g3), g_s, pos)
    grad = g_s[...]
    width = x.shape[1]
    columns = latent_columns(mod, width)
    gate_one = spread(mod, 2, width)
    gate_two = spread(mod, 5, width)

    def latent_sums(vector, value):
        for latent, tokens in enumerate(columns):
            mod_grad_out[latent, :, vector : vector + 1] = lane_sum(value[:, tokens])

    hidden = x[...].astype(F32) + gate_one * branch[...]
    normed, inverse = norm_stats(hidden)
    latent_sums(3, grad * mlp[...])
    mlp_grad = (gate_two * grad).astype(BF16)
    sum2[...] += lane_fold(mlp_grad.astype(F32))
    half = FF // GROUPS
    third = D // GROUPS
    mod_two_low = mod_two[...]
    parts = [slice(part * half, (part + 1) * half) for part in range(GROUPS)]
    act_grads = [dot_nn(w2_t[part], mlp_grad) for part in range(GROUPS)]
    pre_grads = []
    for act_grad, rows in zip(act_grads, parts):
        pre_grads.append((act_grad * slope[rows].astype(F32)).astype(BF16))
        sum1[rows] += lane_fold(pre_grads[-1].astype(F32))
    back = dot_nn(w1_s[0], pre_grads[0]) + dot_nn(w1_s[1], pre_grads[1])
    for part, rows in enumerate(parts):
        acc2[part] += dot_nt(mlp_grad, act[rows])
        acc1[part] += dot_nt(mod_two_low, pre_grads[part])
    latent_sums(1, back)
    latent_sums(2, back * normed)
    hidden_grad = grad + norm_back(back * (1.0 + spread(mod, 4, width)), normed, inverse)
    hidden_grad_out[...] = hidden_grad.astype(BF16)
    latent_sums(0, hidden_grad * branch[...])
    branch_grad = (gate_one * hidden_grad).astype(BF16)
    sump[...] += lane_fold(branch_grad.astype(F32))
    context = None
    for part in range(2):
        rows = slice(part * third, (part + 1) * third)
        accp[part] += dot_nt(attended[...], branch_grad[rows])
        partial = dot_nn(wp_s[part], branch_grad[rows])
        context = partial if context is None else context + partial
    context_out[...] = context.astype(BF16)

    @pl.when(step == pl.num_programs(0) - 1)
    def _():
        mine = pl.multiple_of(pos[0] * third, third)
        other = pl.multiple_of((1 - pos[0]) * third, third)
        for part, pair in ((pos[1], (send_m, keep_m)), (1 - pos[1], (send_t, keep_t))):
            rows = pl.ds(pl.multiple_of(part * third, third), third)
            for out, at, who in ((pair[0], other, 1 - pos[0]), (pair[1], mine, pos[0])):
                out[:, :half] = acc1[part, pl.ds(at, third), :].astype(out.dtype)
                out[:, half : 2 * half] = acc2[part, pl.ds(at, third), :].astype(out.dtype)
                out[:, 2 * half :] = accp[who, rows, :].astype(out.dtype)
        sum1_out[...] = lane_sum(sum1[...])
        sum2_out[...] = lane_sum(sum2[...])
        sump_out[...] = lane_sum(sump[...])


def attention_backward(
    pos, x, mod_one, mod, qkv, probs, context, hidden_grad, mod_grad, sum1, sum2, sump,
    wq0, wq1, wq2, wq3,
    left0, left1, left2, left3,
    out0, out1, out2, out3, send_t, send_m, keep_t, keep_m, pack0, pack1, pack2, pack3, joined,
    wq_s, acc, sumq, sumv, grad_s, block_s, mod_s, bias_s,
):
    step = pl.program_id(0)

    @pl.when(step == 0)
    def _():
        place_split((wq0, wq1, wq2, wq3), wq_s, pos)
        for item in (acc, sumq, sumv):
            item[...] = jnp.zeros_like(item)

    third = D // GROUPS
    scale = HD ** (-0.5)
    mod_one_low = mod_one[...]
    per_group = HEADS // GROUPS
    heads = []
    width = x.shape[1]
    columns = latent_columns(mod, width)
    for head in range(HEADS):
        part, at = head // per_group, head % per_group * HD
        for latent, tokens in enumerate(columns):
            heads.append(
                (
                    (part, at, tokens),
                    qkv[part, at : at + HD, tokens],
                    qkv[part, third + at : third + at + HD, tokens],
                    qkv[part, 2 * third + at : 2 * third + at + HD, tokens],
                    context[head * HD : (head + 1) * HD, tokens],
                    probs[latent, head],
                )
            )
    prob_grads = [dot_nn(values.T, grad) for _, _, _, values, grad, _ in heads]
    score_grads = []
    for prob_grad, (_, _, _, _, _, weight) in zip(prob_grads, heads):
        wide = weight.astype(F32)
        product = wide * prob_grad
        row_dot = jnp.sum(product, axis=0, keepdims=True)
        score_grads.append((product - wide * row_dot).astype(BF16))
    for ((part, at, tokens), query, keys, _, grad, weight), score_grad in zip(heads, score_grads):
        parts = (
            dot_nn(keys, score_grad) * scale,
            dot_nt(query, score_grad) * scale,
            dot_nt(grad, weight),
        )
        for which, value in enumerate(parts):
            start = which * third + at
            grad_s[part, start : start + HD, tokens] = value.astype(BF16)
    back = dot_nn(wq_s[0], grad_s[0]) + dot_nn(wq_s[1], grad_s[1])
    for part in range(GROUPS):
        base = part * third
        qkv_grad = grad_s[part]
        sumq[base : base + third] += lane_fold(qkv_grad[:third].astype(F32))
        sumv[base : base + third] += lane_fold(qkv_grad[2 * third :].astype(F32))
        acc[part] += dot_nt(mod_one_low, qkv_grad)
    normed, inverse = norm_stats(x[...].astype(F32))
    scaled = back * normed
    packs = (pack0, pack1, pack2, pack3)
    mine = pl.multiple_of(pos[0] * third, third)
    other = pl.multiple_of((1 - pos[0]) * third, third)
    for latent, tokens in enumerate(columns):
        mod_s[latent] = jnp.zeros_like(mod_s[latent])
        mod_s[latent, :, 0:1] = lane_sum(back[:, tokens])
        mod_s[latent, :, 1:2] = lane_sum(scaled[:, tokens])
        mod_s[latent, :, 2:6] = mod_grad[latent]
        rows = pl.ds(pl.multiple_of((step * mod.shape[0] + latent) * 8, 8), 8)
        vectors = mod_s[latent, pl.ds(mine, third), :].T
        pack0[rows, :] = vectors
        pack1[rows, :] = vectors
        vectors = mod_s[latent, pl.ds(other, third), :].T
        pack2[rows, :] = vectors
        pack3[rows, :] = vectors
    block_s[...] = hidden_grad[...] + norm_back(
        back * (1.0 + spread(mod, 1, width)), normed, inverse
    )
    split_features(block_s, (out0, out1, out2, out3), pos)
    join_tokens(pos, left0, left1, left2, left3, joined)

    @pl.when(step == pl.num_programs(0) - 1)
    def _():
        for part, send, keep in ((pos[1], send_m, keep_m), (1 - pos[1], send_t, keep_t)):
            send[...] = acc[part, pl.ds(other, third), :].astype(send.dtype)
            keep[...] = acc[part, pl.ds(mine, third), :].astype(keep.dtype)

        own = pos[0] * 2 + pos[1]
        quarter = D // 4
        half = FF // GROUPS
        sumq[:, 0:1] = lane_sum(sumq[...])
        sumv[:, 0:1] = lane_sum(sumv[...])
        for index, pack in enumerate(packs):
            col = pos[1] ^ (index & 1)
            bias_s[...] = jnp.zeros_like(bias_s)
            for part in range(4):
                at = pl.multiple_of(col * half + part * third, third)
                bias_s[:, 4 + part : 5 + part] = sum1[pl.ds(at, third), :]
            at = pl.multiple_of(col * third, third)
            bias_s[:, 0:1] = sumq[pl.ds(at, third), 0:1]
            bias_s[:, 1:2] = sumv[pl.ds(at, third), 0:1]
            at = pl.multiple_of((own ^ index) * quarter, quarter)
            bias_s[:quarter, 2:3] = sump[pl.ds(at, quarter), :]
            bias_s[:quarter, 3:4] = sum2[pl.ds(at, quarter), :]
            pack[pack.shape[0] - BIAS_ROWS :, :] = bias_s[...].T


def call(kernel, pos, steps, seq, inputs, outputs, scratch, micros, name):
    together = TOGETHER.get(name, 1)
    steps, seq = steps // together, seq * together

    def spec(kind, shape):
        kind = kind[0]
        rank = len(shape)
        if kind == "t":
            lead = (0,) * (rank - 1)
            return pl.BlockSpec(shape[:-1] + (seq,), lambda i, p: lead + (i,))
        if kind == "o":
            return pl.BlockSpec(
                shape[:-1] + (seq,), lambda i, p: (0, (p[0] * 2 + p[1]) * steps + i)
            )
        if kind == "j":
            return pl.BlockSpec(
                shape[:-1] + (shape[-1] // 4 * together,),
                lambda i, p: (0, (p[0] * 2 + p[1]) // together ^ i),
            )
        if kind == "l":
            tail = (0,) * (rank - 1)
            return pl.BlockSpec((together,) + shape[1:], lambda i, p: (i,) + tail)
        zeros = (0,) * rank
        if steps > 1:
            return pl.BlockSpec(shape, lambda i, p: zeros, pipeline_mode=pl.Buffered(1))
        return pl.BlockSpec(shape, lambda i, p: zeros)

    size = sum(a.size * a.dtype.itemsize for _, a in inputs)
    size += sum(a.size * jnp.dtype(a.dtype).itemsize for _, a in outputs)
    return pl.pallas_call(
        kernel,
        grid_spec=pltpu.PrefetchScalarGridSpec(
            num_scalar_prefetch=1,
            grid=(steps,),
            in_specs=[spec(kind, a.shape) for kind, a in inputs],
            out_specs=[spec(kind, a.shape) for kind, a in outputs],
            scratch_shapes=scratch,
        ),
        out_shape=[
            pltpu.VMEM(a.shape, a.dtype) if kind.endswith("v") else a for kind, a in outputs
        ],
        compiler_params=pltpu.CompilerParams(
            dimension_semantics=("arbitrary",), vmem_limit_bytes=LIMITS.get(name, 16) * 1024 * 1024
        ),
        cost_estimate=pl.CostEstimate(
            flops=int(micros * 1e9), bytes_accessed=size, transcendentals=0
        ),
        name=name,
    )(pos, *[a for _, a in inputs])


def swap(value, axis):
    return lax.ppermute(value, axis, [(0, 1), (1, 0)])


def group_step(value, step):
    return lax.ppermute(value, GROUP, [(at, at ^ step) for at in range(4)])


def gather_pieces(block, beside):
    return (block, beside, swap(block, "row"), swap(beside, "row"))


def in_order(own_first, other, index, axis):
    first = jnp.where(index == 0, own_first, other)
    second = jnp.where(index == 0, other, own_first)
    return jnp.stack([first, second], axis=axis)


def dp_bits():
    count = lax.axis_size("dp")
    return [1 << at for at in range(count.bit_length() - 1)]


def dp_step(value, bit):
    count = lax.axis_size("dp")
    return lax.ppermute(value, "dp", [(at, at ^ bit) for at in range(count)])


def scatter_terms(value):
    count = lax.axis_size("dp")
    rows, columns = value.shape
    return lax.all_to_all(value.reshape(count, rows // count, columns), "dp", 0, 0)


def add_low(*values):
    return sum(value.astype(F32) for value in values).astype(BF16)


def after(value, token):
    return lax.optimization_barrier((value, token))[0]


def double(value, bit):
    here = (lax.axis_index("dp") // bit) % 2
    return in_order(value, dp_step(value, bit), here, value.ndim - 2)


def local(
    block_input, condition, w_ada, b_ada, w_qkv, b_qkv, w_proj, b_proj, w_fc1, b_fc1, w_fc2,
    b_fc2, out_grad,
):
    row = lax.axis_index("row")
    col = lax.axis_index("col")
    pos = jnp.stack([row, col]).astype(jnp.int32)
    latents = condition.shape[0]
    tokens = block_input.shape[1]
    seq = tokens // latents
    steps = latents // 4
    width = tokens // 4
    third = D // GROUPS
    half = FF // GROUPS
    quarter = D // 4
    pack_rows = steps * 8 + BIAS_ROWS

    def shape(dims, kind):
        return jax.ShapeDtypeStruct(dims, kind)

    t_low = shape((D, width), BF16)
    t_wide = shape((D, width), F32)
    t_ff = shape((FF, width), BF16)
    t_piece = shape((quarter, width), BF16)
    pack = ("w", shape((pack_rows, third), F32))

    wq_beside, wp_beside = swap(w_qkv, "col"), swap(w_proj, "col")
    cut1, cut2, cut3, *packs, cond_low, w_ada_by_vector = call(
        modulation_parts, pos, 1, seq,
        [("w", block_input), ("w", condition), ("w", w_ada), ("w", b_ada), ("w", b_qkv),
         ("w", b_proj.reshape(1, -1)), ("w", b_fc2.reshape(1, -1))],
        [("w", t_piece)] * 3 + [pack] * 4 + [("w", shape(condition.shape, BF16)), ("w", shape((6, third, third), BF16))],
        [], 6, "modulation_parts",
    )

    def cut(value, name):
        return call(
            cut_tokens, pos, 1, seq, [("w", value)], [("w", t_piece)] * 3, [], 3, name
        )

    packs, wq_beside, wp_beside, x_cuts = lax.optimization_barrier(
        (packs, wq_beside, wp_beside, (cut1, cut2, cut3))
    )
    x_moved = [group_step(piece, step) for step, piece in zip((1, 2, 3), x_cuts)]
    packs = [packs[0]] + [group_step(packs[step], step) for step in (1, 2, 3)]
    wq = gather_pieces(w_qkv, wq_beside)
    wp = gather_pieces(w_proj, wp_beside)
    out_late, b_fc1 = after((out_grad, b_fc1), x_cuts[0])
    g_cuts = cut(out_late, "cut_grad")
    b_fc1 = b_fc1.reshape(1, -1)
    x_moved, wq, wp, packs, g_cuts, w_fc1, w_fc2, b_fc1 = lax.optimization_barrier(
        (x_moved, wq, wp, packs, g_cuts, w_fc1, w_fc2, b_fc1)
    )
    w1_beside, w2_beside = swap(w_fc1, "col"), swap(w_fc2, "col")
    w1_row, w2_row = swap(w_fc1, "row"), swap(w_fc2, "row")
    b_fc1 = (b_fc1, swap(b_fc1, "col"))
    x, mod_one, qkv, probs, attended, branch, mod = call(
        attention_forward, pos, steps, seq,
        [("o", block_input)] + [("t", a) for a in x_moved]
        + [("w", a) for a in (*wq, *wp, *packs)],
        [("tv", t_low), ("tv", t_low), ("tv", shape((2, 3 * third, width), BF16)),
         ("lv", shape((steps, HEADS, seq, seq), BF16)), ("tv", t_low), ("tv", t_wide),
         ("lv", shape((steps, D, 8), F32))],
        [pltpu.VMEM((D, seq * TOGETHER.get("attention_forward", 1)), F32),
         pltpu.VMEM((2, D, 3 * third), BF16), pltpu.VMEM((2, 3 * third, D), BF16), pltpu.VMEM((2, D, third), BF16),
         pltpu.VMEM((2, third, D), BF16), pltpu.VMEM((D, 1), F32), pltpu.VMEM((D, 1), F32),
         pltpu.VMEM((D, 1), F32)],
        16, "attention_forward",
    )

    g_cuts, branch, w1_beside, w2_beside, w1_row, w2_row, b_fc1 = lax.optimization_barrier(
        (g_cuts, branch, w1_beside, w2_beside, w1_row, w2_row, b_fc1)
    )
    w1 = (w_fc1, w1_beside, w1_row, swap(w1_beside, "row"))
    w2 = (w_fc2, w2_beside, w2_row, swap(w2_beside, "row"))
    g_moved = [group_step(piece, step) for step, piece in zip((1, 2, 3), g_cuts)]
    *outs, mod_two, act, slope, mlp = call(
        mlp_forward, pos, steps, seq,
        [("t", x), ("t", branch), ("l", mod)] + [("w", a) for a in w1 + w2]
        + [("w", a) for a in (*packs, *b_fc1)],
        [("t", t_piece)] * 4 + [("tv", t_low), ("tv", t_ff), ("tv", t_ff), ("tv", t_low)],
        [pltpu.VMEM((2, D, half), BF16), pltpu.VMEM((2, half, D), BF16),
         pltpu.VMEM((2, D, half), BF16),
         pltpu.VMEM((D, seq * TOGETHER.get("mlp_forward", 1)), F32), pltpu.VMEM((FF, 1), F32),
         pltpu.VMEM((D, 1), F32)],
        12, "mlp_forward",
    )
    outs, g_moved, mlp = lax.optimization_barrier((outs, g_moved, mlp))
    outs = [outs[0]] + [group_step(outs[step], step) for step in (1, 2, 3)]
    fc_block = (third, 2 * half + third)
    qkv_block = (third, 3 * third)
    blocks = lambda dims: [("w", shape(dims, BF16))] * 4
    hidden_grad, context, mod_grad, send_t, send_m, keep_t, keep_m, sum1, sum2, sump = call(
        mlp_backward, pos, steps, seq,
        [("o", out_grad)] + [("t", a) for a in g_moved]
        + [("t", x), ("t", branch), ("l", mod), ("t", mod_two), ("t", act), ("t", slope),
           ("t", mlp), ("t", attended)]
        + [("w", a) for a in w1 + w2 + wp],
        [("tv", t_low), ("tv", t_low), ("lv", shape((steps, D, 4), F32))] + blocks(fc_block)
        + [("w", shape((FF, 1), F32)), ("w", shape((D, 1), F32)), ("w", shape((D, 1), F32))],
        [pltpu.VMEM((D, seq * TOGETHER.get("mlp_backward", 1)), F32),
         pltpu.VMEM((2, D, half), BF16), pltpu.VMEM((2, D, half), BF16),
         pltpu.VMEM((2, half, D), BF16), pltpu.VMEM((2, D, third), BF16),
         pltpu.VMEM((2, D, half), F32), pltpu.VMEM((2, D, half), F32),
         pltpu.VMEM((2, D, third), F32), pltpu.VMEM((FF, 128), F32),
         pltpu.VMEM((D, 128), F32), pltpu.VMEM((D, 128), F32)],
        20, "mlp_backward",
    )
    outs, send_t = lax.optimization_barrier((outs, send_t))
    theirs = add_low(keep_t, swap(send_t, "row"))
    theirs, context, send_m = lax.optimization_barrier((theirs, context, send_m))
    fc_terms = (keep_m, swap(send_m, "row"), swap(theirs, "col"))

    *ins, send_t, send_m, keep_t, keep_m, back0, back1, back2, back3, block_output = call(
        attention_backward, pos, steps, seq,
        [("t", x), ("t", mod_one), ("l", mod), ("t", qkv), ("l", probs), ("t", context),
         ("t", hidden_grad), ("l", mod_grad), ("w", sum1), ("w", sum2), ("w", sump)]
        + [("w", a) for a in (*wq, *outs)],
        [("t", t_piece)] * 4 + blocks(qkv_block) + [pack] * 4
        + [("j", shape((quarter, tokens), F32))],
        [pltpu.VMEM((2, D, 3 * third), BF16), pltpu.VMEM((2, D, 3 * third), F32),
         pltpu.VMEM((D, 128), F32), pltpu.VMEM((D, 128), F32),
         pltpu.VMEM((2, 3 * third, seq * TOGETHER.get("attention_backward", 1)), BF16),
         pltpu.VMEM((D, seq * TOGETHER.get("attention_backward", 1)), F32),
         pltpu.VMEM((TOGETHER.get("attention_backward", 1), D, 8), F32),
         pltpu.VMEM((third, 8), F32)],
        16, "attention_backward",
    )
    bits = list(reversed(dp_bits()))
    count = lax.axis_size("dp")
    fc_terms, send_t = lax.optimization_barrier((fc_terms, send_t))
    fc_parts = scatter_terms(add_low(*fc_terms))
    theirs = add_low(keep_t, swap(send_t, "row"))
    qkv = add_low(keep_m, swap(send_m, "row"), swap(theirs, "col"))
    backs = [back0] + [group_step(a, step) for step, a in ((1, back1), (2, back2), (3, back3))]
    ins = [ins[0]] + [group_step(ins[step], step) for step in (1, 2, 3)]
    rows = 7 * latents + 2 * BIAS_ROWS
    everyone, cond_part = call(
        group_vectors, pos, 1, seq,
        [("w", a) for a in backs] + [("w", cond_low), ("w", w_ada_by_vector)],
        [("w", shape((rows, third), BF16)), ("w", shape(condition.shape, F32))], [], 2,
        "group_vectors",
    )
    everyone, ins = lax.optimization_barrier((everyone[None], ins))
    for bit in bits[:-2]:
        everyone = jnp.concatenate([everyone, dp_step(everyone, bit)])
    cond_part = cond_part + swap(cond_part, "row")
    fc_parts, qkv, ins, everyone, cond_part = lax.optimization_barrier(
        (fc_parts, qkv, ins, everyone, cond_part)
    )
    qkv_parts = scatter_terms(qkv)
    fc = jnp.sum(fc_parts.astype(F32), axis=0).astype(BF16)
    for bit in bits[:-2]:
        fc = double(fc, bit)
    for bit in bits[-2:-1]:
        everyone = jnp.concatenate([everyone, dp_step(everyone, bit)])
    input_grad = call(
        join_tokens, pos, 4, seq, [("w", a) for a in ins],
        [("j", shape((quarter, tokens), F32))], [], 2, "join_tokens",
    )[0]
    cond_grad = jax.vjp(jax.nn.silu, condition)[1](cond_part)[0]
    qkv_parts, fc, everyone, input_grad, cond_grad = lax.optimization_barrier(
        (qkv_parts, fc, everyone, input_grad, cond_grad)
    )
    qkv = jnp.sum(qkv_parts.astype(F32), axis=0).astype(BF16)
    qkv = lax.all_to_all(jnp.broadcast_to(qkv[None], (count,) + qkv.shape), "dp", 0, 0)
    for bit in bits[-2:]:
        fc = double(fc, bit)
    for bit in bits[-1:]:
        everyone = jnp.concatenate([everyone, dp_step(everyone, bit)])
    grads_fc = fc.reshape(fc_block).astype(F32)
    grad_w_ada, grad_b_ada, grad_b_fc1, grad_b_qkv, grad_b_proj, grad_b_fc2 = call(
        modulation_grads, pos, 1, seq, [("w", everyone)],
        [("w", shape((third, 6 * third), F32)), ("w", shape((6, quarter), F32)),
         ("w", shape((4, third), F32)), ("w", shape((2, third), F32)),
         ("w", shape((1, quarter), F32)), ("w", shape((1, quarter), F32))], [], 2,
        "modulation_grads",
    )
    grads_qkv = qkv.reshape(qkv_block).astype(F32)
    return (
        block_output,
        input_grad,
        cond_grad,
        grad_w_ada,
        grad_b_ada,
        grads_qkv,
        grad_b_qkv,
        grads_fc[:, 2 * half :],
        grad_b_proj.reshape(-1),
        grads_fc[:, :half],
        grad_b_fc1.reshape(-1),
        grads_fc[:, half : 2 * half],
        grad_b_fc2.reshape(-1),
    )


def solution(mesh):
    return jax.shard_map(
        local,
        mesh=mesh,
        in_specs=(
            P(("row", "col"), "dp"),
            P("dp", "col"),
            P("col", "row"),
            P(None, ("row", "col")),
            P("row", "col"),
            P(None, "col"),
            P("col", "row"),
            P(("row", "col")),
            P("row", "col"),
            P("col"),
            P("row", "col"),
            P(("row", "col")),
            P(("row", "col"), "dp"),
        ),
        out_specs=(
            P(("row", "col"), "dp"),
            P(("row", "col"), "dp"),
            P("dp", "col"),
            P("col", "row"),
            P(None, ("row", "col")),
            P("row", "col"),
            P(None, "col"),
            P("col", "row"),
            P(("row", "col")),
            P("row", "col"),
            P("col"),
            P("row", "col"),
            P(("row", "col")),
        ),
        check_vma=False,
    )
```

```python
import jax
import jax.numpy as jnp
from jax import lax
from jax.experimental import pallas as pl
from jax.experimental.pallas import tpu as pltpu
from jax.sharding import PartitionSpec as P

D = 384
HEADS = 6
HD = 64
FF = 1536
GROUPS = 2
EPSILON = 1e-06
BF16 = jnp.bfloat16
F32 = jnp.float32
GROUP = ("row", "col")
LIMITS = {"modulation_parts": 60, "attention_forward": 18, "mlp_forward": 22, "mlp_backward": 30, "attention_backward": 24}
TOGETHER = {"attention_forward": 2, "mlp_forward": 2, "mlp_backward": 2, "attention_backward": 2}


def dot_nn(left, right):
    return lax.dot_general(left, right, (((1,), (0,)), ((), ())), preferred_element_type=F32)


def dot_nt(left, right):
    return lax.dot_general(left, right, (((1,), (1,)), ((), ())), preferred_element_type=F32)


def dot_tn(left, right):
    return lax.dot_general(left, right, (((0,), (0,)), ((), ())), preferred_element_type=F32)


def lane_sum(value):
    return jnp.sum(value, axis=1, keepdims=True)


def lane_fold(value):
    parts = [value[:, at : at + 128] for at in range(0, value.shape[1], 128)]
    return sum(parts[1:], parts[0])


def latent_columns(mod, width):
    seq = width // mod.shape[0]
    return [slice(at * seq, (at + 1) * seq) for at in range(mod.shape[0])]


def spread(mod, vector, width):
    shape = (mod.shape[1], width // mod.shape[0])
    parts = [
        jnp.broadcast_to(mod[at, :, vector : vector + 1], shape) for at in range(mod.shape[0])
    ]
    return parts[0] if len(parts) == 1 else jnp.concatenate(parts, axis=1)


def norm_stats(value):
    center = jnp.sum(value, axis=0, keepdims=True) * (1.0 / D)
    square = jnp.sum(value * value, axis=0, keepdims=True) * (1.0 / D)
    inverse = lax.rsqrt(square - center * center + EPSILON)
    return (value - center) * inverse, inverse


def norm_back(grad, normed, inverse):
    first = jnp.sum(grad, axis=0, keepdims=True) * (1.0 / D)
    second = jnp.sum(grad * normed, axis=0, keepdims=True) * (1.0 / D)
    return inverse * (grad - first - normed * second)


PIECES = ((0, 0), (0, 1), (1, 0), (1, 1))


def place_split(pieces, target, pos):
    row, col = pos[0], pos[1]
    for piece, (step_row, step_col) in zip(pieces, PIECES):
        height = piece.shape[0]
        at = pl.multiple_of((row ^ step_row) * height, height)
        target[col ^ step_col, pl.ds(at, height), :] = piece[...]


def place_proj(pieces, target, pos):
    row, col = pos[0], pos[1]
    for piece, (step_row, step_col) in zip(pieces, PIECES):
        height = piece.shape[0]
        at = pl.multiple_of((col ^ step_col) * height, height)
        target[row ^ step_row, pl.ds(at, height), :] = piece[...]


BIAS_ROWS = 8


def bias_columns(packs, pos, query_s, value_s, proj_s, last_s):
    own, col = pos[0] * 2 + pos[1], pos[1]
    third = D // GROUPS
    quarter = D // 4
    for step, pack in enumerate(packs):
        columns = pack[pack.shape[0] - BIAS_ROWS :, :].T
        if step < 2 and query_s is not None:
            at = pl.multiple_of((col ^ step) * third, third)
            query_s[pl.ds(at, third), :] = columns[:, 0:1]
            value_s[pl.ds(at, third), :] = columns[:, 1:2]
        at = pl.multiple_of((own ^ step) * quarter, quarter)
        if proj_s is not None:
            proj_s[pl.ds(at, quarter), :] = columns[:quarter, 2:3]
        if last_s is not None:
            last_s[pl.ds(at, quarter), :] = columns[:quarter, 3:4]


def cut_tokens(pos, x, out1, out2, out3):
    own = pos[0] * 2 + pos[1]
    width = out1.shape[1]
    for step, out in ((1, out1), (2, out2), (3, out3)):
        at = pl.multiple_of((own ^ step) * width, width)
        out[...] = x[:, pl.ds(at, width)]


def piece_order(latents, steps, own):
    here = lax.broadcasted_iota(jnp.int32, (latents, latents), 0)
    there = lax.broadcasted_iota(jnp.int32, (latents, latents), 1)
    return (there == (own ^ (here // steps)) * steps + here % steps).astype(BF16)


def modulation_parts(
    pos, x, condition, w_ada, b_ada, b_qkv, b_proj, b_fc2,
    out1, out2, out3, pack0, pack1, pack2, pack3, cond_out, w_ada_out,
):
    cut_tokens(pos, x, out1, out2, out3)
    own, col = pos[0] * 2 + pos[1], pos[1]
    latents = condition.shape[0]
    steps = latents // 4
    third = D // GROUPS
    quarter = D // 4
    value = condition[...]
    cond_low = (value * jax.nn.sigmoid(value)).astype(BF16)
    cond_out[...] = cond_low
    ordered = dot_nn(piece_order(latents, steps, own), cond_low).astype(BF16)
    zeros = jnp.zeros((6, quarter), F32)
    bias = b_ada[...].astype(F32)
    bias = jnp.where(
        col == 0, jnp.concatenate([bias, zeros], 1), jnp.concatenate([zeros, bias], 1)
    )
    rows = lax.broadcasted_iota(jnp.int32, (third * 6, third), 0)
    columns = lax.broadcasted_iota(jnp.int32, (third * 6, third), 1)
    packs = (pack0, pack1, pack2, pack3)
    for vector in range(6):
        select = (rows == columns * 6 + vector).astype(BF16)
        weight = dot_nn(w_ada[...], select).astype(BF16)
        w_ada_out[vector] = weight
        part = dot_nn(ordered, weight) + bias[vector : vector + 1]
        for step in range(4):
            for at in range(steps):
                packs[step][at * 8 + vector : at * 8 + vector + 1, :] = part[
                    step * steps + at : step * steps + at + 1
                ]
    for pack in packs:
        at = steps * 8
        pack[at : at + 2, :] = b_qkv[...].astype(F32)
        pack[at + 2 : at + 8, :] = jnp.zeros((6, third), F32)
        pack[at + 2 : at + 3, :quarter] = b_proj[...].astype(F32)
        pack[at + 3 : at + 4, :quarter] = b_fc2[...].astype(F32)
        for latent in range(steps):
            pack[latent * 8 + 6 : latent * 8 + 8, :] = jnp.zeros((2, third), F32)


def join_tokens(pos, x0, x1, x2, x3, out):
    own = pos[0] * 2 + pos[1]
    width = x0.shape[1]
    here = out.shape[1] // width
    for step, piece in enumerate((x0, x1, x2, x3)):

        @pl.when(pl.program_id(0) == step // here)
        def _():
            at = pl.multiple_of(((own ^ step) & (here - 1)) * width, width)
            out[:, pl.ds(at, width)] = piece[...].astype(out.dtype)


def group_vectors(pos, pack0, pack1, pack2, pack3, cond, w_ada, everyone, cond_part):
    own = pos[0] * 2 + pos[1]
    packs = (pack0, pack1, pack2, pack3)
    latents = cond.shape[0]
    steps = latents // 4
    low = jnp.concatenate([pack[: steps * 8, :].astype(BF16) for pack in packs], 0)
    wanted = lax.broadcasted_iota(jnp.int32, (6 * latents, 4 * steps * 8), 0)
    source = lax.broadcasted_iota(jnp.int32, (6 * latents, 4 * steps * 8), 1)
    latent = wanted % latents
    found = ((own ^ (latent // steps)) * steps + latent % steps) * 8 + wanted // latents
    rows = dot_nn((source == found).astype(BF16), low).astype(BF16)
    everyone[: 6 * latents] = rows
    total = None
    for vector in range(6):
        partial = dot_nt(rows[vector * latents : (vector + 1) * latents], w_ada[vector])
        total = partial if total is None else total + partial
    cond_part[...] = total
    sums = sum(pack[steps * 8 :, :] for pack in packs)
    sums = jnp.concatenate([sums, jnp.zeros_like(sums)], 0)
    everyone[6 * latents : 6 * latents + 2 * BIAS_ROWS] = sums.astype(BF16)
    everyone[6 * latents + 2 * BIAS_ROWS :] = cond[...]


def modulation_grads(pos, *refs):
    everyone, (w_out, b_out, fc1_out, qkv_out, proj_out, fc2_out) = refs[:-6], refs[-6:]
    third = D // GROUPS
    quarter = D // 4
    latents = (refs[0].shape[1] - 2 * BIAS_ROWS) // 7

    def rows_of(start, size):
        found = [ref[:, start : start + size, :].reshape(-1, third) for ref in everyone]
        return jnp.concatenate(found, 0)

    rows = lax.broadcasted_iota(jnp.int32, (third, third * 6), 0)
    columns = lax.broadcasted_iota(jnp.int32, (third, third * 6), 1)
    total = None
    for vector in range(6):
        grads = rows_of(vector * latents, latents)
        select = (columns == rows * 6 + vector).astype(BF16)
        partial = dot_nn(grads, select)
        total = partial if total is None else total + partial
        summed = jnp.sum(grads.astype(F32), axis=0, keepdims=True)
        b_out[vector : vector + 1, :] = jnp.where(
            pos[1] == 0, summed[:, :quarter], summed[:, quarter:]
        )
    cond = rows_of(6 * latents + 2 * BIAS_ROWS, latents)
    w_out[...] = dot_tn(cond, total.astype(BF16))
    sums = rows_of(6 * latents, 2 * BIAS_ROWS).astype(F32)
    sums = jnp.sum(sums.reshape(-1, 2 * BIAS_ROWS, third), axis=0)
    qkv_out[...] = sums[0:2]
    proj_out[...] = sums[2:3, :quarter]
    fc2_out[...] = sums[3:4, :quarter]
    fc1_out[...] = sums[4:8]


def place_features(pieces, target, pos):
    own = pos[0] * 2 + pos[1]
    for step, piece in enumerate(pieces):
        height = piece.shape[0]
        at = pl.multiple_of((own ^ step) * height, height)
        target[pl.ds(at, height), :] = piece[...].astype(target.dtype)


def split_features(source, pieces, pos):
    own = pos[0] * 2 + pos[1]
    for step, piece in enumerate(pieces):
        height = piece.shape[0]
        at = pl.multiple_of((own ^ step) * height, height)
        piece[...] = source[pl.ds(at, height), :].astype(piece.dtype)


def attention_forward(
    pos, x0, x1, x2, x3, wq0, wq1, wq2, wq3, wp0, wp1, wp2, wp3, pack0, pack1, pack2, pack3,
    x_out, mod_one_out, qkv_out, probs_out, attended_out, branch_out, mod,
    x_s, wq_s, wq_t, wp_s, wp_t, bias_q, bias_v, bias_p,
):
    @pl.when(pl.program_id(0) == 0)
    def _():
        place_split((wq0, wq1, wq2, wq3), wq_s, pos)
        place_proj((wp0, wp1, wp2, wp3), wp_s, pos)
        bias_columns((pack0, pack1, pack2, pack3), pos, bias_q, bias_v, bias_p, None)
        for part in range(GROUPS):
            wq_t[part] = wq_s[part].T
            wp_t[part] = wp_s[part].T

    third = D // GROUPS
    for first, second, who in ((pack0, pack1, pos[0]), (pack2, pack3, 1 - pos[0])):
        at = pl.multiple_of(who * third, third)
        for latent in range(mod.shape[0]):
            rows = pl.multiple_of((pl.program_id(0) * mod.shape[0] + latent) * 8, 8)
            rows = pl.ds(rows, 8)
            mod[latent, pl.ds(at, third), :] = (first[rows, :] + second[rows, :]).T
    place_features((x0, x1, x2, x3), x_s, pos)
    x = x_s[...]
    x_out[...] = x.astype(BF16)
    normed, _ = norm_stats(x)
    width = x.shape[1]
    columns = latent_columns(mod, width)
    mod_one = (normed * (1.0 + spread(mod, 1, width)) + spread(mod, 0, width)).astype(BF16)
    mod_one_out[...] = mod_one
    per_group = HEADS // GROUPS
    heads = []
    for part in range(GROUPS):
        qkv = dot_nn(wq_t[part], mod_one)
        base = part * third
        query = (qkv[:third] + bias_q[base : base + third]).astype(BF16)
        keys = qkv[third : 2 * third].astype(BF16)
        values = (qkv[2 * third :] + bias_v[base : base + third]).astype(BF16)
        qkv_out[part, :third] = query
        qkv_out[part, third : 2 * third] = keys
        qkv_out[part, 2 * third :] = values
        scaled = query * jnp.asarray(HD ** (-0.5), BF16)
        for head in range(per_group):
            rows = slice(head * HD, (head + 1) * HD)
            for latent, tokens in enumerate(columns):
                place = (latent, part * per_group + head, tokens)
                heads.append((place, keys[rows, tokens], scaled[rows, tokens], values[rows, tokens]))
    scores = [dot_nn(keys.T, query) for _, keys, query, _ in heads]
    probs = []
    for score in scores:
        raised = jnp.exp(score - jnp.max(score, axis=0, keepdims=True))
        total = jnp.sum(raised, axis=0, keepdims=True)
        probs.append((raised * (1.0 / total)).astype(BF16))
    for ((latent, head, tokens), _, _, values), prob in zip(heads, probs):
        probs_out[latent, head] = prob
        attended_out[head * HD : (head + 1) * HD, tokens] = dot_nn(values, prob).astype(BF16)
    attended = attended_out[...]
    for part in range(2):
        rows = slice(part * third, (part + 1) * third)
        branch_out[rows] = (dot_nn(wp_t[part], attended) + bias_p[rows]).astype(BF16)


def mlp_forward(
    pos, x, branch, mod, w10, w11, w12, w13, w20, w21, w22, w23, pack0, pack1, pack2, pack3,
    b10, b11,
    out0, out1, out2, out3, mod_two_out, act_out, slope_out, mlp_out,
    w1_s, w1_t, w2_s, block_s, bias_1, bias_2,
):
    @pl.when(pl.program_id(0) == 0)
    def _():
        bias_columns((pack0, pack1, pack2, pack3), pos, None, None, None, bias_2)
        for step, piece in enumerate((b10, b11)):
            height = piece.shape[1]
            column = jnp.broadcast_to(piece[...].astype(F32), (8, height)).T
            at = pl.multiple_of((pos[1] ^ step) * height, height)
            bias_1[pl.ds(at, height), :] = column[:, 0:1]
        place_split((w10, w11, w12, w13), w1_s, pos)
        place_split((w20, w21, w22, w23), w2_s, pos)
        for part in range(GROUPS):
            w1_t[part] = w1_s[part].T

    width = x.shape[1]
    hidden = x[...].astype(F32) + spread(mod, 2, width) * branch[...]
    normed, _ = norm_stats(hidden)
    mod_two = (normed * (1.0 + spread(mod, 4, width)) + spread(mod, 3, width)).astype(BF16)
    mod_two_out[...] = mod_two
    half = FF // GROUPS
    slope = (2.0 / jnp.pi) ** 0.5
    parts = [slice(part * half, (part + 1) * half) for part in range(GROUPS)]
    pres = [dot_nn(w1_t[part], mod_two) + bias_1[rows] for part, rows in enumerate(parts)]
    acts = []
    for pre, rows in zip(pres, parts):
        square = pre * pre
        tanh = jnp.tanh(pre * (slope + (slope * 0.044715) * square))
        upper = 0.5 + 0.5 * tanh
        acts.append((pre * upper).astype(BF16))
        act_out[rows] = acts[-1]
        slope_out[rows] = (
            upper + pre * (1.0 - tanh * tanh) * (0.5 * slope + (1.5 * slope * 0.044715) * square)
        ).astype(BF16)
    total = dot_nn(w2_s[0], acts[0]) + dot_nn(w2_s[1], acts[1])
    mlp = total + bias_2[...]
    mlp_out[...] = mlp.astype(BF16)
    block_s[...] = hidden + spread(mod, 5, width) * mlp
    split_features(block_s, (out0, out1, out2, out3), pos)


def mlp_backward(
    pos, g0, g1, g2, g3, x, branch, mod, mod_two, act, slope, mlp, attended,
    w10, w11, w12, w13, w20, w21, w22, w23, wp0, wp1, wp2, wp3,
    hidden_grad_out, context_out, mod_grad_out, send_t, send_m, keep_t, keep_m, sum1_out, sum2_out, sump_out,
    g_s, w1_s, w2_s, w2_t, wp_s, acc1, acc2, accp, sum1, sum2, sump,
):
    step = pl.program_id(0)

    @pl.when(step == 0)
    def _():
        place_split((w10, w11, w12, w13), w1_s, pos)
        place_split((w20, w21, w22, w23), w2_s, pos)
        place_proj((wp0, wp1, wp2, wp3), wp_s, pos)
        for part in range(GROUPS):
            w2_t[part] = w2_s[part].T
        for acc in (acc1, acc2, accp, sum1, sum2, sump):
            acc[...] = jnp.zeros_like(acc)

    place_features((g0, g1, g2, g3), g_s, pos)
    grad = g_s[...]
    width = x.shape[1]
    columns = latent_columns(mod, width)
    gate_one = spread(mod, 2, width)
    gate_two = spread(mod, 5, width)

    def latent_sums(vector, value):
        for latent, tokens in enumerate(columns):
            mod_grad_out[latent, :, vector : vector + 1] = lane_sum(value[:, tokens])

    hidden = x[...].astype(F32) + gate_one * branch[...]
    normed, inverse = norm_stats(hidden)
    latent_sums(3, grad * mlp[...])
    mlp_grad = (gate_two * grad).astype(BF16)
    sum2[...] += lane_fold(mlp_grad.astype(F32))
    half = FF // GROUPS
    third = D // GROUPS
    mod_two_low = mod_two[...]
    parts = [slice(part * half, (part + 1) * half) for part in range(GROUPS)]
    act_grads = [dot_nn(w2_t[part], mlp_grad) for part in range(GROUPS)]
    pre_grads = []
    for act_grad, rows in zip(act_grads, parts):
        pre_grads.append((act_grad * slope[rows].astype(F32)).astype(BF16))
        sum1[rows] += lane_fold(pre_grads[-1].astype(F32))
    back = dot_nn(w1_s[0], pre_grads[0]) + dot_nn(w1_s[1], pre_grads[1])
    for part, rows in enumerate(parts):
        acc2[part] += dot_nt(mlp_grad, act[rows])
        acc1[part] += dot_nt(mod_two_low, pre_grads[part])
    latent_sums(1, back)
    latent_sums(2, back * normed)
    hidden_grad = grad + norm_back(back * (1.0 + spread(mod, 4, width)), normed, inverse)
    hidden_grad_out[...] = hidden_grad.astype(BF16)
    latent_sums(0, hidden_grad * branch[...])
    branch_grad = (gate_one * hidden_grad).astype(BF16)
    sump[...] += lane_fold(branch_grad.astype(F32))
    context = None
    for part in range(2):
        rows = slice(part * third, (part + 1) * third)
        accp[part] += dot_nt(attended[...], branch_grad[rows])
        partial = dot_nn(wp_s[part], branch_grad[rows])
        context = partial if context is None else context + partial
    context_out[...] = context.astype(BF16)

    @pl.when(step == pl.num_programs(0) - 1)
    def _():
        mine = pl.multiple_of(pos[0] * third, third)
        other = pl.multiple_of((1 - pos[0]) * third, third)
        for part, pair in ((pos[1], (send_m, keep_m)), (1 - pos[1], (send_t, keep_t))):
            rows = pl.ds(pl.multiple_of(part * third, third), third)
            for out, at, who in ((pair[0], other, 1 - pos[0]), (pair[1], mine, pos[0])):
                out[:, :half] = acc1[part, pl.ds(at, third), :].astype(out.dtype)
                out[:, half : 2 * half] = acc2[part, pl.ds(at, third), :].astype(out.dtype)
                out[:, 2 * half :] = accp[who, rows, :].astype(out.dtype)
        sum1_out[...] = lane_sum(sum1[...])
        sum2_out[...] = lane_sum(sum2[...])
        sump_out[...] = lane_sum(sump[...])


def attention_backward(
    pos, x, mod_one, mod, qkv, probs, context, hidden_grad, mod_grad, sum1, sum2, sump,
    wq0, wq1, wq2, wq3,
    left0, left1, left2, left3,
    out0, out1, out2, out3, send_t, send_m, keep_t, keep_m, pack0, pack1, pack2, pack3, joined,
    wq_s, acc, sumq, sumv, grad_s, block_s, mod_s, bias_s,
):
    step = pl.program_id(0)

    @pl.when(step == 0)
    def _():
        place_split((wq0, wq1, wq2, wq3), wq_s, pos)
        for item in (acc, sumq, sumv):
            item[...] = jnp.zeros_like(item)

    third = D // GROUPS
    scale = HD ** (-0.5)
    mod_one_low = mod_one[...]
    per_group = HEADS // GROUPS
    heads = []
    width = x.shape[1]
    columns = latent_columns(mod, width)
    for head in range(HEADS):
        part, at = head // per_group, head % per_group * HD
        for latent, tokens in enumerate(columns):
            heads.append(
                (
                    (part, at, tokens),
                    qkv[part, at : at + HD, tokens],
                    qkv[part, third + at : third + at + HD, tokens],
                    qkv[part, 2 * third + at : 2 * third + at + HD, tokens],
                    context[head * HD : (head + 1) * HD, tokens],
                    probs[latent, head],
                )
            )
    prob_grads = [dot_nn(values.T, grad) for _, _, _, values, grad, _ in heads]
    score_grads = []
    for prob_grad, (_, _, _, _, _, weight) in zip(prob_grads, heads):
        wide = weight.astype(F32)
        product = wide * prob_grad
        row_dot = jnp.sum(product, axis=0, keepdims=True)
        score_grads.append((product - wide * row_dot).astype(BF16))
    for ((part, at, tokens), query, keys, _, grad, weight), score_grad in zip(heads, score_grads):
        parts = (
            dot_nn(keys, score_grad) * scale,
            dot_nt(query, score_grad) * scale,
            dot_nt(grad, weight),
        )
        for which, value in enumerate(parts):
            start = which * third + at
            grad_s[part, start : start + HD, tokens] = value.astype(BF16)
    back = dot_nn(wq_s[0], grad_s[0]) + dot_nn(wq_s[1], grad_s[1])
    for part in range(GROUPS):
        base = part * third
        qkv_grad = grad_s[part]
        sumq[base : base + third] += lane_fold(qkv_grad[:third].astype(F32))
        sumv[base : base + third] += lane_fold(qkv_grad[2 * third :].astype(F32))
        acc[part] += dot_nt(mod_one_low, qkv_grad)
    normed, inverse = norm_stats(x[...].astype(F32))
    scaled = back * normed
    packs = (pack0, pack1, pack2, pack3)
    mine = pl.multiple_of(pos[0] * third, third)
    other = pl.multiple_of((1 - pos[0]) * third, third)
    for latent, tokens in enumerate(columns):
        mod_s[latent] = jnp.zeros_like(mod_s[latent])
        mod_s[latent, :, 0:1] = lane_sum(back[:, tokens])
        mod_s[latent, :, 1:2] = lane_sum(scaled[:, tokens])
        mod_s[latent, :, 2:6] = mod_grad[latent]
        rows = pl.ds(pl.multiple_of((step * mod.shape[0] + latent) * 8, 8), 8)
        vectors = mod_s[latent, pl.ds(mine, third), :].T
        pack0[rows, :] = vectors
        pack1[rows, :] = vectors
        vectors = mod_s[latent, pl.ds(other, third), :].T
        pack2[rows, :] = vectors
        pack3[rows, :] = vectors
    block_s[...] = hidden_grad[...] + norm_back(
        back * (1.0 + spread(mod, 1, width)), normed, inverse
    )
    split_features(block_s, (out0, out1, out2, out3), pos)
    join_tokens(pos, left0, left1, left2, left3, joined)

    @pl.when(step == pl.num_programs(0) - 1)
    def _():
        for part, send, keep in ((pos[1], send_m, keep_m), (1 - pos[1], send_t, keep_t)):
            send[...] = acc[part, pl.ds(other, third), :].astype(send.dtype)
            keep[...] = acc[part, pl.ds(mine, third), :].astype(keep.dtype)

        own = pos[0] * 2 + pos[1]
        quarter = D // 4
        half = FF // GROUPS
        sumq[:, 0:1] = lane_sum(sumq[...])
        sumv[:, 0:1] = lane_sum(sumv[...])
        for index, pack in enumerate(packs):
            col = pos[1] ^ (index & 1)
            bias_s[...] = jnp.zeros_like(bias_s)
            for part in range(4):
                at = pl.multiple_of(col * half + part * third, third)
                bias_s[:, 4 + part : 5 + part] = sum1[pl.ds(at, third), :]
            at = pl.multiple_of(col * third, third)
            bias_s[:, 0:1] = sumq[pl.ds(at, third), 0:1]
            bias_s[:, 1:2] = sumv[pl.ds(at, third), 0:1]
            at = pl.multiple_of((own ^ index) * quarter, quarter)
            bias_s[:quarter, 2:3] = sump[pl.ds(at, quarter), :]
            bias_s[:quarter, 3:4] = sum2[pl.ds(at, quarter), :]
            pack[pack.shape[0] - BIAS_ROWS :, :] = bias_s[...].T


def call(kernel, pos, steps, seq, inputs, outputs, scratch, micros, name):
    together = TOGETHER.get(name, 1)
    steps, seq = steps // together, seq * together

    def spec(kind, shape):
        kind = kind[0]
        rank = len(shape)
        if kind == "t":
            lead = (0,) * (rank - 1)
            return pl.BlockSpec(shape[:-1] + (seq,), lambda i, p: lead + (i,))
        if kind == "o":
            return pl.BlockSpec(
                shape[:-1] + (seq,), lambda i, p: (0, (p[0] * 2 + p[1]) * steps + i)
            )
        if kind == "j":
            return pl.BlockSpec(
                shape[:-1] + (shape[-1] // 4 * together,),
                lambda i, p: (0, (p[0] * 2 + p[1]) // together ^ i),
            )
        if kind == "l":
            tail = (0,) * (rank - 1)
            return pl.BlockSpec((together,) + shape[1:], lambda i, p: (i,) + tail)
        zeros = (0,) * rank
        if steps > 1:
            return pl.BlockSpec(shape, lambda i, p: zeros, pipeline_mode=pl.Buffered(1))
        return pl.BlockSpec(shape, lambda i, p: zeros)

    size = sum(a.size * a.dtype.itemsize for _, a in inputs)
    size += sum(a.size * jnp.dtype(a.dtype).itemsize for _, a in outputs)
    return pl.pallas_call(
        kernel,
        grid_spec=pltpu.PrefetchScalarGridSpec(
            num_scalar_prefetch=1,
            grid=(steps,),
            in_specs=[spec(kind, a.shape) for kind, a in inputs],
            out_specs=[spec(kind, a.shape) for kind, a in outputs],
            scratch_shapes=scratch,
        ),
        out_shape=[
            pltpu.VMEM(a.shape, a.dtype) if kind.endswith("v") else a for kind, a in outputs
        ],
        compiler_params=pltpu.CompilerParams(
            dimension_semantics=("arbitrary",), vmem_limit_bytes=LIMITS.get(name, 16) * 1024 * 1024
        ),
        cost_estimate=pl.CostEstimate(
            flops=int(micros * 1e9), bytes_accessed=size, transcendentals=0
        ),
        name=name,
    )(pos, *[a for _, a in inputs])


def swap(value, axis):
    return lax.ppermute(value, axis, [(0, 1), (1, 0)])


def group_step(value, step):
    return lax.ppermute(value, GROUP, [(at, at ^ step) for at in range(4)])


def gather_pieces(block, beside):
    return (block, beside, swap(block, "row"), swap(beside, "row"))


def in_order(own_first, other, index, axis):
    first = jnp.where(index == 0, own_first, other)
    second = jnp.where(index == 0, other, own_first)
    return jnp.stack([first, second], axis=axis)


def dp_bits():
    count = lax.axis_size("dp")
    return [1 << at for at in range(count.bit_length() - 1)]


def dp_step(value, bit):
    count = lax.axis_size("dp")
    return lax.ppermute(value, "dp", [(at, at ^ bit) for at in range(count)])


def scatter_terms(value):
    count = lax.axis_size("dp")
    rows, columns = value.shape
    return lax.all_to_all(value.reshape(count, rows // count, columns), "dp", 0, 0)


def add_low(*values):
    return sum(value.astype(F32) for value in values).astype(BF16)


def after(value, token):
    return lax.optimization_barrier((value, token))[0]


def double(value, bit):
    here = (lax.axis_index("dp") // bit) % 2
    return in_order(value, dp_step(value, bit), here, value.ndim - 2)


def local(
    block_input, condition, w_ada, b_ada, w_qkv, b_qkv, w_proj, b_proj, w_fc1, b_fc1, w_fc2,
    b_fc2, out_grad,
):
    row = lax.axis_index("row")
    col = lax.axis_index("col")
    pos = jnp.stack([row, col]).astype(jnp.int32)
    latents = condition.shape[0]
    tokens = block_input.shape[1]
    seq = tokens // latents
    steps = latents // 4
    width = tokens // 4
    third = D // GROUPS
    half = FF // GROUPS
    quarter = D // 4
    pack_rows = steps * 8 + BIAS_ROWS

    def shape(dims, kind):
        return jax.ShapeDtypeStruct(dims, kind)

    t_low = shape((D, width), BF16)
    t_wide = shape((D, width), F32)
    t_ff = shape((FF, width), BF16)
    t_piece = shape((quarter, width), BF16)
    pack = ("w", shape((pack_rows, third), F32))

    wq_beside, wp_beside = swap(w_qkv, "col"), swap(w_proj, "col")
    cut1, cut2, cut3, *packs, cond_low, w_ada_by_vector = call(
        modulation_parts, pos, 1, seq,
        [("w", block_input), ("w", condition), ("w", w_ada), ("w", b_ada), ("w", b_qkv),
         ("w", b_proj.reshape(1, -1)), ("w", b_fc2.reshape(1, -1))],
        [("w", t_piece)] * 3 + [pack] * 4 + [("w", shape(condition.shape, BF16)), ("w", shape((6, third, third), BF16))],
        [], 6, "modulation_parts",
    )

    def cut(value, name):
        return call(
            cut_tokens, pos, 1, seq, [("w", value)], [("w", t_piece)] * 3, [], 3, name
        )

    packs, wq_beside, wp_beside, x_cuts = lax.optimization_barrier(
        (packs, wq_beside, wp_beside, (cut1, cut2, cut3))
    )
    x_moved = [group_step(piece, step) for step, piece in zip((1, 2, 3), x_cuts)]
    packs = [packs[0]] + [group_step(packs[step], step) for step in (1, 2, 3)]
    wq = gather_pieces(w_qkv, wq_beside)
    wp = gather_pieces(w_proj, wp_beside)
    out_late, b_fc1 = after((out_grad, b_fc1), x_cuts[0])
    g_cuts = cut(out_late, "cut_grad")
    b_fc1 = b_fc1.reshape(1, -1)
    x_moved, wq, wp, packs, g_cuts, w_fc1, w_fc2, b_fc1 = lax.optimization_barrier(
        (x_moved, wq, wp, packs, g_cuts, w_fc1, w_fc2, b_fc1)
    )
    w1_beside, w2_beside = swap(w_fc1, "col"), swap(w_fc2, "col")
    w1_row, w2_row = swap(w_fc1, "row"), swap(w_fc2, "row")
    b_fc1 = (b_fc1, swap(b_fc1, "col"))
    x, mod_one, qkv, probs, attended, branch, mod = call(
        attention_forward, pos, steps, seq,
        [("o", block_input)] + [("t", a) for a in x_moved]
        + [("w", a) for a in (*wq, *wp, *packs)],
        [("tv", t_low), ("tv", t_low), ("tv", shape((2, 3 * third, width), BF16)),
         ("lv", shape((steps, HEADS, seq, seq), BF16)), ("tv", t_low), ("tv", t_low),
         ("lv", shape((steps, D, 8), F32))],
        [pltpu.VMEM((D, seq * TOGETHER.get("attention_forward", 1)), F32),
         pltpu.VMEM((2, D, 3 * third), BF16), pltpu.VMEM((2, 3 * third, D), BF16), pltpu.VMEM((2, D, third), BF16),
         pltpu.VMEM((2, third, D), BF16), pltpu.VMEM((D, 1), F32), pltpu.VMEM((D, 1), F32),
         pltpu.VMEM((D, 1), F32)],
        16, "attention_forward",
    )

    g_cuts, branch, w1_beside, w2_beside, w1_row, w2_row, b_fc1 = lax.optimization_barrier(
        (g_cuts, branch, w1_beside, w2_beside, w1_row, w2_row, b_fc1)
    )
    w1 = (w_fc1, w1_beside, w1_row, swap(w1_beside, "row"))
    w2 = (w_fc2, w2_beside, w2_row, swap(w2_beside, "row"))
    g_moved = [group_step(piece, step) for step, piece in zip((1, 2, 3), g_cuts)]
    *outs, mod_two, act, slope, mlp = call(
        mlp_forward, pos, steps, seq,
        [("t", x), ("t", branch), ("l", mod)] + [("w", a) for a in w1 + w2]
        + [("w", a) for a in (*packs, *b_fc1)],
        [("t", t_piece)] * 4 + [("tv", t_low), ("tv", t_ff), ("tv", t_ff), ("tv", t_low)],
        [pltpu.VMEM((2, D, half), BF16), pltpu.VMEM((2, half, D), BF16),
         pltpu.VMEM((2, D, half), BF16),
         pltpu.VMEM((D, seq * TOGETHER.get("mlp_forward", 1)), F32), pltpu.VMEM((FF, 1), F32),
         pltpu.VMEM((D, 1), F32)],
        12, "mlp_forward",
    )
    outs, g_moved, mlp = lax.optimization_barrier((outs, g_moved, mlp))
    outs = [outs[0]] + [group_step(outs[step], step) for step in (1, 2, 3)]
    fc_block = (third, 2 * half + third)
    qkv_block = (third, 3 * third)
    blocks = lambda dims: [("w", shape(dims, BF16))] * 4
    hidden_grad, context, mod_grad, send_t, send_m, keep_t, keep_m, sum1, sum2, sump = call(
        mlp_backward, pos, steps, seq,
        [("o", out_grad)] + [("t", a) for a in g_moved]
        + [("t", x), ("t", branch), ("l", mod), ("t", mod_two), ("t", act), ("t", slope),
           ("t", mlp), ("t", attended)]
        + [("w", a) for a in w1 + w2 + wp],
        [("tv", t_low), ("tv", t_low), ("lv", shape((steps, D, 4), F32))] + blocks(fc_block)
        + [("w", shape((FF, 1), F32)), ("w", shape((D, 1), F32)), ("w", shape((D, 1), F32))],
        [pltpu.VMEM((D, seq * TOGETHER.get("mlp_backward", 1)), F32),
         pltpu.VMEM((2, D, half), BF16), pltpu.VMEM((2, D, half), BF16),
         pltpu.VMEM((2, half, D), BF16), pltpu.VMEM((2, D, third), BF16),
         pltpu.VMEM((2, D, half), F32), pltpu.VMEM((2, D, half), F32),
         pltpu.VMEM((2, D, third), F32), pltpu.VMEM((FF, 128), F32),
         pltpu.VMEM((D, 128), F32), pltpu.VMEM((D, 128), F32)],
        20, "mlp_backward",
    )
    outs, send_t = lax.optimization_barrier((outs, send_t))
    theirs = add_low(keep_t, swap(send_t, "row"))
    theirs, context, send_m = lax.optimization_barrier((theirs, context, send_m))
    fc_terms = (keep_m, swap(send_m, "row"), swap(theirs, "col"))

    *ins, send_t, send_m, keep_t, keep_m, back0, back1, back2, back3, block_output = call(
        attention_backward, pos, steps, seq,
        [("t", x), ("t", mod_one), ("l", mod), ("t", qkv), ("l", probs), ("t", context),
         ("t", hidden_grad), ("l", mod_grad), ("w", sum1), ("w", sum2), ("w", sump)]
        + [("w", a) for a in (*wq, *outs)],
        [("t", t_piece)] * 4 + blocks(qkv_block) + [pack] * 4
        + [("j", shape((quarter, tokens), F32))],
        [pltpu.VMEM((2, D, 3 * third), BF16), pltpu.VMEM((2, D, 3 * third), F32),
         pltpu.VMEM((D, 128), F32), pltpu.VMEM((D, 128), F32),
         pltpu.VMEM((2, 3 * third, seq * TOGETHER.get("attention_backward", 1)), BF16),
         pltpu.VMEM((D, seq * TOGETHER.get("attention_backward", 1)), F32),
         pltpu.VMEM((TOGETHER.get("attention_backward", 1), D, 8), F32),
         pltpu.VMEM((third, 8), F32)],
        16, "attention_backward",
    )
    bits = list(reversed(dp_bits()))
    count = lax.axis_size("dp")
    fc_terms, send_t = lax.optimization_barrier((fc_terms, send_t))
    fc_parts = scatter_terms(add_low(*fc_terms))
    theirs = add_low(keep_t, swap(send_t, "row"))
    qkv = add_low(keep_m, swap(send_m, "row"), swap(theirs, "col"))
    backs = [back0] + [group_step(a, step) for step, a in ((1, back1), (2, back2), (3, back3))]
    ins = [ins[0]] + [group_step(ins[step], step) for step in (1, 2, 3)]
    rows = 7 * latents + 2 * BIAS_ROWS
    everyone, cond_part = call(
        group_vectors, pos, 1, seq,
        [("w", a) for a in backs] + [("w", cond_low), ("w", w_ada_by_vector)],
        [("w", shape((rows, third), BF16)), ("w", shape(condition.shape, F32))], [], 2,
        "group_vectors",
    )
    everyone, ins = lax.optimization_barrier((everyone[None], ins))
    for bit in bits[:-2]:
        everyone = jnp.concatenate([everyone, dp_step(everyone, bit)])
    cond_part = cond_part + swap(cond_part, "row")
    fc_parts, qkv, ins, everyone, cond_part = lax.optimization_barrier(
        (fc_parts, qkv, ins, everyone, cond_part)
    )
    qkv_parts = scatter_terms(qkv)
    fc = jnp.sum(fc_parts.astype(F32), axis=0).astype(BF16)
    for bit in bits[:-2]:
        fc = double(fc, bit)
    for bit in bits[-2:-1]:
        everyone = jnp.concatenate([everyone, dp_step(everyone, bit)])
    input_grad = call(
        join_tokens, pos, 4, seq, [("w", a) for a in ins],
        [("j", shape((quarter, tokens), F32))], [], 2, "join_tokens",
    )[0]
    cond_grad = jax.vjp(jax.nn.silu, condition)[1](cond_part)[0]
    qkv_parts, fc, everyone, input_grad, cond_grad = lax.optimization_barrier(
        (qkv_parts, fc, everyone, input_grad, cond_grad)
    )
    qkv = jnp.sum(qkv_parts.astype(F32), axis=0).astype(BF16)
    qkv = lax.all_to_all(jnp.broadcast_to(qkv[None], (count,) + qkv.shape), "dp", 0, 0)
    for bit in bits[-2:]:
        fc = double(fc, bit)
    for bit in bits[-1:]:
        everyone = jnp.concatenate([everyone, dp_step(everyone, bit)])
    grads_fc = fc.reshape(fc_block).astype(F32)
    grad_w_ada, grad_b_ada, grad_b_fc1, grad_b_qkv, grad_b_proj, grad_b_fc2 = call(
        modulation_grads, pos, 1, seq, [("w", everyone)],
        [("w", shape((third, 6 * third), F32)), ("w", shape((6, quarter), F32)),
         ("w", shape((4, third), F32)), ("w", shape((2, third), F32)),
         ("w", shape((1, quarter), F32)), ("w", shape((1, quarter), F32))], [], 2,
        "modulation_grads",
    )
    grads_qkv = qkv.reshape(qkv_block).astype(F32)
    return (
        block_output,
        input_grad,
        cond_grad,
        grad_w_ada,
        grad_b_ada,
        grads_qkv,
        grad_b_qkv,
        grads_fc[:, 2 * half :],
        grad_b_proj.reshape(-1),
        grads_fc[:, :half],
        grad_b_fc1.reshape(-1),
        grads_fc[:, half : 2 * half],
        grad_b_fc2.reshape(-1),
    )


def solution(mesh):
    return jax.shard_map(
        local,
        mesh=mesh,
        in_specs=(
            P(("row", "col"), "dp"),
            P("dp", "col"),
            P("col", "row"),
            P(None, ("row", "col")),
            P("row", "col"),
            P(None, "col"),
            P("col", "row"),
            P(("row", "col")),
            P("row", "col"),
            P("col"),
            P("row", "col"),
            P(("row", "col")),
            P(("row", "col"), "dp"),
        ),
        out_specs=(
            P(("row", "col"), "dp"),
            P(("row", "col"), "dp"),
            P("dp", "col"),
            P("col", "row"),
            P(None, ("row", "col")),
            P("row", "col"),
            P(None, "col"),
            P("col", "row"),
            P(("row", "col")),
            P("row", "col"),
            P("col"),
            P("row", "col"),
            P(("row", "col")),
        ),
        check_vma=False,
    )
```
